32 devices in a mesh: dp: 16 (over z, y, core), tensor: 2 (over x).
Axes of the slice: x: 2, y: 2, z: 4, core: 2. Of those that a mesh axis runs over, the one named last changes fastest.
Arguments:
- inputs: bfloat16 [32, 512, 768], P('dp'), may hold values from -6 to 6
- lengths: int32 [32], P('dp'), may hold values from 1 to 512, as said below
- w_qkv: bfloat16 [768, 3, 768], P(None, None, 'tensor'), may hold values from -0.21875 to 0.21875
- b_qv: float32 [2, 768], P(None, 'tensor'), may hold values from -3 to 3
- w_out: bfloat16 [768, 768], P('tensor'), may hold values from -0.875 to 0.875
- b_out: float32 [768], replicated, may hold values from -2 to 2
- ln_gains: float32 [2, 768], replicated, may hold values from 0.1 to 1.9
- ln_biases: float32 [2, 768], replicated, may hold values from -3 to 3
- w_in: bfloat16 [768, 3072], P(None, 'tensor'), may hold values from -0.21875 to 0.21875
- b_in: float32 [3072], P('tensor'), may hold values from -3 to 3
- w_down: bfloat16 [3072, 768], P('tensor'), may hold values from -0.109375 to 0.109375
- b_down: float32 [768], replicated, may hold values from -2 to 2
- cotangent: bfloat16 [32, 512, 768], P('dp'), may hold values from -6 to 6
Outputs:
- output: bfloat16 [32, 512, 768], P('dp')
- grad_inputs: float32 [32, 512, 768], P('dp')
- grad_w_qkv: float32 [768, 3, 768], P('dp', None, 'tensor')
- grad_b_qv: float32 [2, 768], P(None, 'tensor')
- grad_w_out: float32 [768, 768], P('tensor', 'dp')
- grad_b_out: float32 [768], replicated
- grad_ln_gains: float32 [2, 768], replicated
- grad_ln_biases: float32 [2, 768], replicated
- grad_w_in: float32 [768, 3072], P('dp', 'tensor')
- grad_b_in: float32 [3072], P('tensor')
- grad_w_down: float32 [3072, 768], P('tensor', 'dp')
- grad_b_down: float32 [768], replicated
The draws below stay inside these ranges and needn't reach their ends.
Inputs may be any that keep to these rules, and one draw needn't show every extreme that they name: `lengths`: keys below this count are visible; in every draw some sequence has all 512.
All inputs are finite; a program needn't handle non-finite values.
Results may differ from the reference program's by a relative error of at most 0.012.
Values sent between devices are 32-bit elements; how exact they have to be, the bound alone decides.
No kernel may reach another device: no remote copies, remote signals or barrier semaphores. Data moves between devices by JAX's collectives and lax.ppermute only.
A program may use at most 128 MiB of HBM per device.

```python
import math
import jax
import jax.numpy as jnp
from jax import lax

D = 768
HEADS = 12
HEAD_DIM = 64
FF = 3072
SEQ_LEN = 512
SEQS = 32


def draw_lengths(key, part):
    key = jax.random.fold_in(key, 7)
    key_scale, key_value, key_full = jax.random.split(key, 3)
    exponent = jax.random.randint(key_scale, (SEQS,), 0, 4)
    reach_cap = jnp.left_shift(jnp.full((SEQS,), max(SEQ_LEN // 4, 1), jnp.int32), exponent)
    raw_value = jax.random.randint(key_value, (SEQS,), 0, 1 << 30)
    drawn = jnp.minimum(1 + raw_value % reach_cap, SEQ_LEN)
    full_index = jax.random.randint(key_full, (), 0, SEQS)
    return jnp.where(jnp.arange(SEQS) == full_index, SEQ_LEN, drawn).astype(jnp.int32)


def level_of(key, extent, pieces, smallest, largest):
    gain, own = 1.0, jax.random.fold_in(key, 6)
    for axis_at, parts in pieces:
        heights = jnp.exp(jax.random.uniform(jax.random.fold_in(own, axis_at), (parts,), jnp.float32, smallest / len(pieces), largest / len(pieces)))
        gain = gain * jnp.repeat(heights, extent[axis_at] // parts).reshape([-1 if axis == axis_at else 1 for axis in range(len(extent))])
    return gain


def noise(own_key, shape, scale, most, cuts=(), dtype=jnp.bfloat16):
    values = jax.random.normal(own_key, shape, jnp.float32) * scale
    if len(cuts) > 0:
        values = level_of(own_key, shape, cuts, -0.22, 0.18) * values
    return jnp.clip(values, min=-most, max=most).astype(dtype)


def setup_inputs(seed: int = 0) -> dict:
    key_list = jax.random.split(jax.random.key(seed), 14)
    return {
        "inputs": noise(key_list[0], (SEQS, SEQ_LEN, D), 1.0, 6.0, ((0, 16),)),
        "lengths": draw_lengths(jax.random.fold_in(key_list[13], 71), 0),
        "w_qkv": noise(key_list[2], (D, 3, D), D ** -0.5, 0.21875, ((2, 2),)),
        "b_qv": noise(key_list[3], (2, D), 0.5, 3.0, ((1, 2),), jnp.float32),
        "w_out": noise(key_list[4], (D, D), (D // 16) ** -0.5, 0.875, ((0, 2),)),
        "b_out": noise(key_list[5], (D,), 0.3, 2.0, (), jnp.float32),
        "ln_gains": jnp.clip(1.0 + 0.18 * jax.random.normal(key_list[6], (2, D), jnp.float32), 0.1, 1.9),
        "ln_biases": noise(key_list[7], (2, D), 0.5, 3.0, (), jnp.float32),
        "w_in": noise(key_list[8], (D, FF), D ** -0.5, 0.21875, ((1, 2),)),
        "b_in": noise(key_list[9], (FF,), 0.5, 3.0, ((0, 2),), jnp.float32),
        "w_down": noise(key_list[10], (FF, D), FF ** -0.5, 0.109375, ((0, 2),)),
        "b_down": noise(key_list[11], (D,), 0.3, 2.0, (), jnp.float32),
        "cotangent": noise(key_list[12], (SEQS, SEQ_LEN, D), 1.0, 6.0, ((0, 16),)),
    }


@jax.custom_vjp
def low(v):
    return lax.optimization_barrier(v.astype(jnp.bfloat16)).astype(jnp.float32)

@jax.custom_vjp
def low_back(v):
    return v

def low_keep(v):
    return (low(v), None)

def low_pass(kept, grad):
    return (grad,)

def back_keep(v):
    return (v, None)

def back_low(kept, grad):
    return (low(grad),)
low.defvjp(low_keep, low_pass)
low_back.defvjp(back_keep, back_low)
norm_eps = 1e-12
exact_mode = lax.Precision.HIGHEST

def normalize(hidden, gain_vec, offset):
    centred = hidden - lax.optimization_barrier(jnp.mean(hidden, axis=-1, keepdims=True))
    second_moment = lax.optimization_barrier(jnp.mean(centred * centred, axis=-1, keepdims=True))
    return centred * lax.rsqrt(second_moment + norm_eps) * gain_vec + offset

def block_layer(weights, block_rows, block_lengths):
    w_qkv, b_qv, w_out, b_out, ln_gains, ln_biases, w_in, b_in, w_down, b_down = weights
    seq_count = block_rows.shape[0]
    flat_rows = block_rows.reshape(seq_count * SEQ_LEN, D)
    projected = jnp.dot(flat_rows, w_qkv.reshape(D, 3 * D), precision=exact_mode).reshape(-1, 3, D)
    head_shape = (seq_count, SEQ_LEN, HEADS, HEAD_DIM)
    queries = low_back(low(projected[:, 0] + b_qv[0])).reshape(head_shape)
    key_rows = low_back(low(projected[:, 1])).reshape(head_shape)
    value_rows = low_back(low(projected[:, 2] + b_qv[1])).reshape(head_shape)
    scores = low_back(jnp.einsum('sqhd,skhd->shqk', queries, key_rows, precision=exact_mode) * HEAD_DIM ** (-0.5))
    visible = jnp.arange(SEQ_LEN)[None, :] < block_lengths[:, None]
    scores = jnp.where(visible[:, None, None, :], scores, -1000000000.0)
    soft_weights = low(jax.nn.softmax(scores, axis=-1))
    context = jnp.einsum('shqk,skhd->sqhd', soft_weights, value_rows, precision=exact_mode).reshape(-1, D)
    context = low_back(low(context))
    attended = low_back(jnp.dot(context, w_out, precision=exact_mode))
    normed_one = normalize(flat_rows + attended + b_out, ln_gains[0], ln_biases[0])
    hidden_pre = low_back(jnp.dot(low(normed_one), w_in, precision=exact_mode) + b_in)
    hidden_act = low(jax.nn.gelu(hidden_pre, approximate=False))
    ffn_branch = low_back(jnp.dot(hidden_act, w_down, precision=exact_mode))
    normed_two = normalize(normed_one + ffn_branch + b_down, ln_gains[1], ln_biases[1])
    return normed_two.reshape(seq_count, SEQ_LEN, D)

def reference(inputs, lengths, w_qkv, b_qv, w_out, b_out, ln_gains, ln_biases, w_in, b_in, w_down, b_down, cotangent):
    block_size = math.gcd(SEQS, 8)
    blocks = SEQS // block_size
    weights = tuple((member.astype(jnp.float32) for member in (w_qkv, b_qv, w_out, b_out, ln_gains, ln_biases, w_in, b_in, w_down, b_down)))
    start_rows = inputs.astype(jnp.float32).reshape(blocks, block_size, SEQ_LEN, D)
    block_spans = lengths.reshape(blocks, block_size)
    checked = jax.checkpoint(block_layer)

    def forward(weight_set, all_rows):
        return lax.map(lambda joined: checked(weight_set, joined[0], joined[1]), (all_rows, block_spans))
    result, backward = jax.vjp(forward, weights, start_rows)
    weight_grads, input_grad = backward(cotangent.astype(jnp.float32).reshape(result.shape))
    return (result.reshape(SEQS, SEQ_LEN, D).astype(jnp.bfloat16), input_grad.reshape(SEQS, SEQ_LEN, D), weight_grads[0], weight_grads[1], weight_grads[2], weight_grads[3], weight_grads[4], weight_grads[5], weight_grads[6], weight_grads[7], weight_grads[8], weight_grads[9])
```

```python
import functools

import jax
import jax.numpy as jnp
from jax import lax
from jax.experimental import pallas as pl
from jax.experimental.pallas import tpu as pltpu
from jax.sharding import PartitionSpec as P

HEAD_DIM = 64
norm_eps = 1e-12
bfloat = jnp.bfloat16
single = jnp.float32


def dot(left, right):
    return jnp.dot(left, right, preferred_element_type=single)


def dot_rows(left, right):
    return lax.dot_general(
        left, right, (((0,), (0,)), ((), ())), preferred_element_type=single
    )


def dot_cols(left, right):
    return lax.dot_general(
        left, right, (((1,), (1,)), ((), ())), preferred_element_type=single
    )


def swap_dp(value, mask, size):
    return lax.ppermute(value, "dp", [(i, i ^ mask) for i in range(size)])


def swap_x(value):
    return lax.ppermute(value, "tensor", [(0, 1), (1, 0)])


def reverse_bits(position, bits):
    out = 0
    for k in range(bits):
        out |= ((position >> k) & 1) << (bits - 1 - k)
    return out


def place_kernel(order_ref, block_ref, out_ref):
    out_ref[...] = block_ref[...].astype(out_ref.dtype)


def place(blocks, order):
    count, rows, width = blocks.shape
    return pl.pallas_call(
        place_kernel,
        grid_spec=pltpu.PrefetchScalarGridSpec(
            num_scalar_prefetch=1,
            grid=(count,),
            in_specs=[pl.BlockSpec((1, rows, width), lambda p, order: (p, 0, 0))],
            out_specs=pl.BlockSpec((1, rows, width), lambda p, order: (order[p], 0, 0)),
        ),
        out_shape=jax.ShapeDtypeStruct((count, rows, width), bfloat),
    )(order, blocks).reshape(count * rows, width)


def fetch_spread(own, me, size):
    bits = min(size, 16).bit_length() - 1
    count = 1 << bits
    rank = me % count
    rows = own.shape[0] // count
    held = lax.dynamic_slice_in_dim(own, rank * rows, rows).astype(single)
    held = swap_x(held)
    for k in reversed(range(1, bits)):
        held = jnp.concatenate([held, swap_dp(held, 1 << k, size)], axis=0)
    held = jnp.concatenate([held, swap_dp(held, 1, size)], axis=0)
    order = jnp.array([reverse_bits(p, bits) for p in range(count)], jnp.int32) ^ rank
    return place(held.reshape(count, rows, own.shape[1]), order)


def fetch_direct(own, me, size):
    rows = own.shape[0] // 2
    core = me % 2
    held = swap_x(lax.dynamic_slice_in_dim(own, core * rows, rows).astype(single))
    held = jnp.stack([held, swap_dp(held, 1, size)])
    return place(held, jnp.arange(2, dtype=jnp.int32) ^ core)


def halve(value, mask, size):
    middle = value.shape[0] // 2
    return value[:middle] + swap_dp(value[middle:], mask, size)


def scatter_sum(left_rel, own_side, other_side, size, x_first):
    middle = left_rel.shape[1] // 2
    keep, send = left_rel[:, :middle], left_rel[:, middle:]
    other_in = swap_dp(dot_rows(send, other_side), 1, size)
    own_in = swap_dp(dot_rows(send, own_side), 1, size)
    other = dot_rows(keep, other_side) + other_in
    own = dot_rows(keep, own_side) + own_in
    masks = [1 << k for k in range(1, size.bit_length() - 1)]
    if x_first:
        total = own + swap_x(other)
        for mask in masks:
            total = halve(total, mask, size)
        return total
    for mask in masks:
        other = halve(other, mask, size)
        own = halve(own, mask, size)
    return own + swap_x(other)


def sum_all(value, size):
    for k in range(size.bit_length() - 1):
        value = value + swap_dp(value, 1 << k, size)
    return value


def norm_parts(hidden):
    centred = hidden - jnp.mean(hidden, axis=-1, keepdims=True)
    scale = lax.rsqrt(jnp.mean(centred * centred, axis=-1, keepdims=True) + norm_eps)
    return centred * scale, scale


def norm_back(upstream, unit, scale, gain):
    scaled = upstream * gain
    return scale * (
        scaled
        - jnp.mean(scaled, axis=-1, keepdims=True)
        - unit * jnp.mean(scaled * unit, axis=-1, keepdims=True)
    )


def split_heads(rows):
    return rows.reshape(rows.shape[0], -1, HEAD_DIM)


def masked_scores(queries, keys, visible):
    scores = jnp.einsum("qhd,khd->hqk", queries, keys, preferred_element_type=single)
    return jnp.where(visible[None, None, :], scores * HEAD_DIM**-0.5, -1e9)


def attend(queries, keys, values, visible):
    queries, keys, values = map(split_heads, (queries, keys, values))
    scores = masked_scores(queries, keys, visible)
    highest = jnp.max(scores, axis=-1, keepdims=True)
    raised = jnp.exp(scores - highest)
    totals = jnp.sum(raised, axis=-1, keepdims=True)
    context = jnp.einsum(
        "hqk,khd->qhd", (raised / totals).astype(bfloat), values, preferred_element_type=single
    )
    return context.astype(bfloat).reshape(context.shape[0], -1), highest + jnp.log(totals)


def attend_back(queries, keys, values, visible, log_total, grad_context):
    queries, keys, values, grad_context = map(
        split_heads, (queries, keys, values, grad_context)
    )
    chances = jnp.exp(masked_scores(queries, keys, visible) - log_total)
    grad_values = jnp.einsum(
        "hqk,qhd->khd", chances.astype(bfloat), grad_context, preferred_element_type=single
    )
    grad_chances = jnp.einsum(
        "qhd,khd->hqk", grad_context, values, preferred_element_type=single
    )
    inner = jnp.sum(chances * grad_chances, axis=-1, keepdims=True)
    grad_scores = (chances * (grad_chances - inner)).astype(bfloat)
    factor = HEAD_DIM**-0.5
    grad_queries = factor * jnp.einsum(
        "hqk,khd->qhd", grad_scores, keys, preferred_element_type=single
    )
    grad_keys = factor * jnp.einsum(
        "hqk,qhd->khd", grad_scores, queries, preferred_element_type=single
    )
    return tuple(
        part.astype(bfloat).reshape(part.shape[0], -1)
        for part in (grad_queries, grad_keys, grad_values)
    )


def body(
    inputs,
    lengths,
    w_qkv,
    b_qv,
    w_out,
    b_out,
    ln_gains,
    ln_biases,
    w_in,
    b_in,
    w_down,
    b_down,
    cotangent,
):
    size = lax.axis_size("dp")
    me = lax.axis_index("dp")
    side = lax.axis_index("tensor")
    width = inputs.shape[2]
    local = w_qkv.shape[2]
    rows = lax.dynamic_index_in_dim(inputs, side, 0, keepdims=False)
    length = lax.dynamic_index_in_dim(lengths, side, 0, keepdims=False)
    upstream = lax.dynamic_index_in_dim(cotangent, side, 0, keepdims=False)
    visible = jnp.arange(rows.shape[0]) < length

    qkv_own = w_qkv.reshape(width, 3 * local)
    middle = w_down.shape[0] // 2
    small_other = swap_x(jnp.concatenate([b_qv.reshape(-1), b_in]))
    b_qv_other, b_in_other = small_other[: 2 * local].reshape(2, local), small_other[2 * local :]
    qkv_other = fetch_spread(qkv_own, me, size)
    out_other = fetch_direct(w_out, me, size)
    in_other = fetch_spread(w_in, me, size)
    down_other = jnp.concatenate(
        [fetch_spread(w_down[:middle], me, size), fetch_direct(w_down[middle:], me, size)]
    )
    sides = (
        (qkv_own, b_qv, w_out, w_in, b_in, w_down),
        (qkv_other, b_qv_other, out_other, in_other, b_in_other, down_other),
    )

    bits = size.bit_length() - 1
    share = width // size
    block_of = jnp.array([reverse_bits(p, bits) for p in range(size)], jnp.int32) ^ me
    source = (block_of[:, None] * share + jnp.arange(share)[None, :]).reshape(-1)
    reorder = (jnp.arange(width)[:, None] == source[None, :]).astype(bfloat)

    def relative(value):
        return dot(value, reorder).astype(bfloat)

    heads = []
    hidden = rows.astype(single) + b_out
    for qkv, bias, out, _, _, _ in sides:
        projected = dot(rows, qkv)
        queries = (projected[:, :local] + bias[0]).astype(bfloat)
        keys = projected[:, local : 2 * local].astype(bfloat)
        values = (projected[:, 2 * local :] + bias[1]).astype(bfloat)
        context, log_total = attend(queries, keys, values, visible)
        hidden = hidden + dot(context, out)
        heads.append((queries, keys, values, log_total, context))
    unit_one, scale_one = norm_parts(hidden)
    normed = unit_one * ln_gains[0] + ln_biases[0]
    normed_low = normed.astype(bfloat)
    hidden_two = normed + b_down
    acts = []
    for _, _, _, into, bias, down in sides:
        pre = dot(normed_low, into) + bias
        chance = 0.5 * (1.0 + lax.erf(pre * 0.7071067811865476))
        act = (pre * chance).astype(bfloat)
        slope = chance + pre * jnp.exp(-0.5 * pre * pre) * 0.3989422804014327
        hidden_two = hidden_two + dot(act, down)
        acts.append((act, slope))
    unit_two, scale_two = norm_parts(hidden_two)
    result = unit_two * ln_gains[1] + ln_biases[1]
    result_other = swap_x(unit_two) * ln_gains[1] + ln_biases[1]

    upstream = upstream.astype(single)
    grad_two = norm_back(upstream, unit_two, scale_two, ln_gains[1])
    branch = grad_two.astype(bfloat)
    branch_rel = relative(branch)
    normed_rel = relative(normed_low)
    rows_rel = relative(rows)
    share_down = scatter_sum(branch_rel, acts[0][0], acts[1][0], size, True)
    grad_pres = []
    grad_normed = grad_two
    for (_, slope), (_, _, _, into, _, down) in zip(acts, sides):
        grad_pre = (dot_cols(branch, down) * slope).astype(bfloat)
        grad_normed = grad_normed + dot_cols(grad_pre, into)
        grad_pres.append(grad_pre)
    share_in = scatter_sum(normed_rel, grad_pres[0], grad_pres[1], size, False)
    grad_one = norm_back(grad_normed, unit_one, scale_one, ln_gains[0])
    attended = grad_one.astype(bfloat)
    attended_rel = relative(attended)
    share_out = scatter_sum(attended_rel, heads[0][4], heads[1][4], size, False)
    grad_rows = grad_one
    grad_projs = []
    for (queries, keys, values, log_total, _), (qkv, _, out, _, _, _) in zip(heads, sides):
        grad_context = dot_cols(attended, out).astype(bfloat)
        parts = attend_back(queries, keys, values, visible, log_total, grad_context)
        grad_proj = jnp.concatenate(parts, axis=1)
        grad_rows = grad_rows + dot_cols(grad_proj, qkv)
        grad_projs.append(grad_proj)
    grad_rows_other = swap_x(grad_rows)
    share_qkv = scatter_sum(rows_rel, grad_projs[0], grad_projs[1], size, True)

    def columns(value):
        return jnp.sum(value.astype(single), axis=0)

    every = jnp.concatenate(
        [
            columns(grad_one),
            columns(grad_normed * unit_one),
            columns(upstream * unit_two),
            columns(grad_normed),
            columns(upstream),
            columns(grad_two),
        ]
    )
    vectors = jnp.concatenate([every, columns(grad_pres[0])])
    vectors_other = swap_x(jnp.concatenate([every, columns(grad_pres[1])]))
    vectors = sum_all(vectors + vectors_other, size)
    low_part, high_part = grad_projs[0], grad_projs[1]
    qv_own = jnp.concatenate([columns(low_part[:, :local]), columns(low_part[:, 2 * local :])])
    qv_other = jnp.concatenate([columns(high_part[:, :local]), columns(high_part[:, 2 * local :])])
    grad_b_qv = sum_all(qv_own + swap_x(qv_other), size).reshape(2, local)
    b_out_g, gain_one, gain_two, shift_one, shift_two, b_down_g = (
        vectors[k * width : (k + 1) * width] for k in range(6)
    )

    def both(mine, other):
        mine, other = mine[None], other[None]
        return jnp.where(
            side == 0,
            jnp.concatenate([mine, other], axis=0),
            jnp.concatenate([other, mine], axis=0),
        )

    return (
        both(result.astype(bfloat), result_other.astype(bfloat)),
        both(grad_rows, grad_rows_other),
        share_qkv.reshape(-1, 3, local),
        grad_b_qv,
        share_out.T,
        b_out_g,
        jnp.stack([gain_one, gain_two]),
        jnp.stack([shift_one, shift_two]),
        share_in,
        vectors[6 * width :],
        share_down.T,
        b_down_g,
    )


def solution(mesh):
    placed = (
        P("dp", None, None),
        P("dp"),
        P(None, None, "tensor"),
        P(None, "tensor"),
        P("tensor", None),
        P(),
        P(),
        P(),
        P(None, "tensor"),
        P("tensor"),
        P("tensor", None),
        P(),
        P("dp", None, None),
    )
    return jax.shard_map(
        body,
        mesh=mesh,
        in_specs=placed,
        out_specs=(
            P("dp", None, None),
            P("dp", None, None),
            P("dp", None, "tensor"),
            P(None, "tensor"),
            P("tensor", "dp"),
            P(),
            P(),
            P(),
            P("dp", "tensor"),
            P("tensor"),
            P("tensor", "dp"),
            P(),
        ),
        check_vma=False,
    )
```

```python
import functools

import jax
import jax.numpy as jnp
from jax import lax
from jax.experimental import pallas as pl
from jax.experimental.pallas import tpu as pltpu
from jax.sharding import PartitionSpec as P

HEAD_DIM = 64
PAIR = 2 * HEAD_DIM
norm_eps = 1e-12
bfloat = jnp.bfloat16
single = jnp.float32
MIB = 1 << 20


def dot(left, right):
    return jnp.dot(left, right, preferred_element_type=single)


def dot_cols(left, right):
    return lax.dot_general(
        left, right, (((1,), (1,)), ((), ())), preferred_element_type=single
    )


def shaped(shape, dtype):
    return jax.ShapeDtypeStruct(shape, dtype)


def call(kernel, outs, *args, scalars=(), scratch=(), grid=(), in_specs=None, out_specs=None, limit=48):
    many = isinstance(outs, (tuple, list))
    if in_specs is None:
        in_specs = [pl.BlockSpec(memory_space=pltpu.VMEM)] * len(args)
        out_specs = [pl.BlockSpec(memory_space=pltpu.VMEM)] * len(outs) if many else pl.BlockSpec(memory_space=pltpu.VMEM)
    return pl.pallas_call(
        kernel,
        out_shape=outs,
        grid=grid,
        in_specs=[pl.BlockSpec(memory_space=pltpu.SMEM)] * len(scalars) + list(in_specs),
        out_specs=out_specs,
        scratch_shapes=list(scratch),
        compiler_params=pltpu.CompilerParams(vmem_limit_bytes=limit * MIB),
        cost_estimate=pl.CostEstimate(flops=1000, bytes_accessed=1000, transcendentals=0),
    )(*scalars, *args)


def swap_dp(value, mask, size):
    return lax.ppermute(value, "dp", [(i, i ^ mask) for i in range(size)])


def swap_x(value):
    return lax.ppermute(value, "tensor", [(0, 1), (1, 0)])


def reverse_bits(position, bits):
    out = 0
    for k in range(bits):
        out |= ((position >> k) & 1) << (bits - 1 - k)
    return out


def place_kernel(groups, rows, order_ref, *refs):
    out_ref = refs[-1]
    at = 0
    for piece, count in zip(refs[:-1], groups):
        for b in range(count):
            start = pl.multiple_of(order_ref[at], 16)
            height = rows[at]
            if out_ref.ndim == 3:
                out_ref[:, pl.ds(start, height), :] = piece[b].astype(out_ref.dtype)
            else:
                out_ref[pl.ds(start, height), :] = piece[b].astype(out_ref.dtype)
            at += 1


def place(parts, shape):
    pieces, rows, starts = [], [], []
    for held, begin in parts:
        pieces += held
        starts += begin
        rows += [held[0].shape[-2]] * len(begin)
    groups = tuple(piece.shape[0] for piece in pieces)
    kernel = functools.partial(place_kernel, groups, tuple(rows))
    return call(kernel, shaped(shape, bfloat), *pieces, scalars=(jnp.stack(starts),))


def fetch_spread(own, me, size, masks, base=0):
    masks = [mask for mask in masks if mask < size]
    count = 2 << len(masks)
    rank = me & (count - 1)
    rows = own.shape[-2] // count
    held = lax.dynamic_slice_in_dim(own, rank * rows, rows, axis=own.ndim - 2).astype(single)
    pieces = [swap_x(held)[None]]
    offsets = [[0]]
    for mask in masks:
        whole = pieces[0] if len(pieces) == 1 else jnp.concatenate(pieces, axis=0)
        flat = [o for part in offsets for o in part]
        pieces = [whole, swap_dp(whole, mask, size)]
        offsets = [flat, [o ^ mask for o in flat]]
    pieces = pieces + [swap_dp(piece, 1, size) for piece in pieces]
    flat = [o for part in offsets for o in part]
    flat = flat + [o ^ 1 for o in flat]
    return pieces, [base + (rank ^ o) * rows for o in flat]


def fetch_direct(own, me, size, base=0):
    rows = own.shape[0] // 2
    core = me & 1
    held = swap_x(lax.dynamic_slice_in_dim(own, core * rows, rows).astype(single))[None]
    return [held, swap_dp(held, 1, size)], [base + core * rows, base + (1 - core) * rows]


def halve(value, mask, size):
    middle = value.shape[-2] // 2
    return value[..., :middle, :] + swap_dp(value[..., middle:, :], mask, size)


def sum_all(value, size):
    for k in range(size.bit_length() - 1):
        value = value + swap_dp(value, 1 << k, size)
    return value


def grad_kernel(sides, terms, split, *refs):
    left_ref = refs[0]
    rights = refs[1 : 1 + sides]
    added = refs[1 + sides : 1 + sides + terms]
    outs = refs[1 + sides + terms :]

    def step(right_ref):
        total = dot(left_ref[...], right_ref[...])
        for term in added:
            total = total + term[...].reshape(total.shape)
        if split:
            middle = total.shape[0] // 2
            outs[0][...] = total[:middle].reshape(outs[0].shape)
            outs[1][...] = total[middle:].reshape(outs[1].shape)
        else:
            outs[0][...] = total.reshape(outs[0].shape)

    if sides == 1:
        step(rights[0])
    else:
        pl.when(pl.program_id(0) == 0)(lambda: step(rights[0]))
        pl.when(pl.program_id(0) == 1)(lambda: step(rights[1]))


def grad_part(left, half, rights, added=(), split=False):
    depth, tokens = left.shape
    rows = depth // 2
    width = rights[0].shape[1]
    tile = 512 if width % 512 == 0 else 384
    steps = width // tile
    sides = len(rights)
    if sides == 1:
        grid = (steps,)
        right_specs = [pl.BlockSpec((tokens, tile), lambda j: (0, j))]
        left_spec = pl.BlockSpec((rows, tokens), lambda j: (half, 0))

        def block(height):
            return pl.BlockSpec((height, tile), lambda j: (0, j))

        def full(height):
            return (height, width)
    else:
        grid = (2, steps)
        right_specs = [
            pl.BlockSpec((tokens, tile), lambda s, j: (0, jnp.where(s == 0, j, steps - 1))),
            pl.BlockSpec((tokens, tile), lambda s, j: (0, jnp.where(s == 0, 0, j))),
        ]
        left_spec = pl.BlockSpec((rows, tokens), lambda s, j: (half, 0))

        def block(height):
            return pl.BlockSpec((1, height, tile), lambda s, j: (s, 0, j))

        def full(height):
            return (2, height, width)

    heights = (rows // 2, rows // 2) if split else (rows,)
    outs = call(
        functools.partial(grad_kernel, sides, len(added), split),
        [shaped(full(height), single) for height in heights],
        left,
        *rights,
        *added,
        grid=grid,
        in_specs=[left_spec, *right_specs, *[block(rows) for _ in added]],
        out_specs=[block(height) for height in heights],
        limit=32,
    )
    return outs if split else outs[0]


def finish(low, high, size):
    total = low + swap_dp(high, 2, size)
    for k in range(2, size.bit_length() - 1):
        total = halve(total, 1 << k, size)
    return total


def scatter_x_first(left, own, other, size):
    other_in = swap_dp(grad_part(left, 1, [other]), 1, size)
    own_in = swap_dp(grad_part(left, 1, [own]), 1, size)
    across = swap_x(grad_part(left, 0, [other], [other_in]))
    low, high = grad_part(left, 0, [own], [own_in, across], split=True)
    return finish(low, high, size)


def scatter_y_first(left, own, other, size):
    arrived = swap_dp(grad_part(left, 1, [own, other]), 1, size)
    low, high = grad_part(left, 0, [own, other], [arrived], split=True)
    total = finish(low, high, size)
    return total[0] + swap_x(total[1])


def relative_kernel(value_ref, source_ref, out_ref):
    depth = value_ref.shape[1]
    tile = depth // 4

    def step(j, carry):
        at = pl.multiple_of(j * tile, 16)
        lanes = lax.broadcasted_iota(jnp.int32, (tile, depth), 1)
        picks = jnp.where(lanes == source_ref[pl.ds(at, tile), :], 1.0, 0.0).astype(bfloat)
        out_ref[pl.ds(at, tile), :] = dot_cols(picks, value_ref[...]).astype(bfloat)
        return carry

    lax.fori_loop(0, 4, step, 0)


def relative(value, source):
    return call(relative_kernel, shaped(value.shape[::-1], bfloat), value, source)


def attend_kernel(length_ref, rows_ref, qkv_ref, bias_ref, out_w_ref, start_ref, parts_ref, chance_ref, context_ref, hidden_ref, turned_ref):
    tokens = rows_ref.shape[0]
    local = qkv_ref.shape[2]
    rows = rows_ref[...]
    for part in range(3):
        projected = dot(rows, qkv_ref[part])
        if part == 0:
            projected = projected + bias_ref[0:1, :]
        elif part == 2:
            projected = projected + bias_ref[1:2, :]
        parts_ref[part] = projected.astype(bfloat)
    tile = 256
    visible = lax.broadcasted_iota(jnp.int32, (tokens, tile), 0) < length_ref[0]

    def pair_step(pair, carry):
        at = pl.multiple_of(pair * PAIR, PAIR)
        keys = parts_ref[1, :, pl.ds(at, PAIR)]
        queries = parts_ref[0, :, pl.ds(at, PAIR)].T
        values = parts_ref[2, :, pl.ds(at, PAIR)].T
        owner = lax.broadcasted_iota(jnp.int32, (PAIR, tile), 0) // HEAD_DIM
        for h in range(2):
            value_rows = values[h * HEAD_DIM : (h + 1) * HEAD_DIM]
            for q in range(tokens // tile):
                picked = queries[:, q * tile : (q + 1) * tile] * HEAD_DIM**-0.5
                picked = jnp.where(owner == h, picked, jnp.zeros_like(picked))
                scores = jnp.where(visible, dot(keys, picked), -1e9)
                raised = jnp.exp(scores - jnp.max(scores, axis=0, keepdims=True))
                chances = raised * (1.0 / jnp.sum(raised, axis=0, keepdims=True))
                chances = chances.astype(bfloat)
                chance_ref[pair * 2 + h, :, q * tile : (q + 1) * tile] = chances
                turned_ref[pl.ds(pl.multiple_of(at + h * HEAD_DIM, HEAD_DIM), HEAD_DIM), q * tile : (q + 1) * tile] = dot(value_rows, chances).astype(bfloat)
        return carry

    lax.fori_loop(0, local // PAIR, pair_step, 0)
    context = turned_ref[...].T
    context_ref[...] = context
    hidden_ref[...] = start_ref[...] + dot(context, out_w_ref[...])


def attend(length, rows, qkv, bias, out, start):
    tokens, width = rows.shape
    local = qkv.shape[2]
    return call(
        attend_kernel,
        [
            shaped((3, tokens, local), bfloat),
            shaped((local // HEAD_DIM, tokens, tokens), bfloat),
            shaped((tokens, local), bfloat),
            shaped((tokens, width), single),
        ],
        rows,
        qkv,
        bias,
        out,
        start,
        scalars=(length,),
        scratch=[pltpu.VMEM((local, tokens), bfloat)],
    )


def unit_of(hidden):
    centred = hidden - jnp.mean(hidden, axis=-1, keepdims=True)
    scale = lax.rsqrt(jnp.mean(centred * centred, axis=-1, keepdims=True) + norm_eps)
    return centred * scale, scale


def norm_back(upstream, unit, scale, gain):
    scaled = upstream * gain
    return scale * (
        scaled
        - jnp.mean(scaled, axis=-1, keepdims=True)
        - unit * jnp.mean(scaled * unit, axis=-1, keepdims=True)
    )


STRIP = 128


def strips(tokens, body):
    def step(j, carry):
        body(pl.ds(pl.multiple_of(j * STRIP, STRIP), STRIP))
        return carry

    lax.fori_loop(0, tokens // STRIP, step, 0)


def norm_kernel(hidden_ref, gain_ref, shift_ref, down_ref, low_ref, next_ref):
    def body(at):
        unit, _ = unit_of(hidden_ref[at, :])
        normed = unit * gain_ref[0:1, :] + shift_ref[0:1, :]
        low_ref[at, :] = normed.astype(bfloat)
        next_ref[at, :] = normed + down_ref[...]

    strips(hidden_ref.shape[0], body)


def feed_kernel(normed_ref, into_ref, bias_ref, down_ref, start_ref, act_ref, slope_ref, hidden_ref):
    hidden_units = into_ref.shape[1]
    tile = 256

    def step(j, carry):
        at = pl.ds(pl.multiple_of(j * tile, tile), tile)
        for k in range(2):
            strip = pl.ds(k * 256, 256)
            pre = dot(normed_ref[strip, :], into_ref[:, at]) + bias_ref[:, at]
            bell = jnp.exp(-0.5 * pre * pre)
            reach = 1.0 / (1.0 + 0.23164189 * jnp.abs(pre))
            tail = reach * (
                0.127414796
                + reach * (-0.142248368 + reach * (0.7107068705 + reach * (-0.7265760135 + reach * 0.5307027145)))
            )
            tail = tail * bell
            chance = jnp.where(pre >= 0, 1.0 - tail, tail)
            act_ref[strip, at] = (pre * chance).astype(bfloat)
            slope_ref[strip, at] = (chance + pre * bell * 0.3989422804014327).astype(bfloat)
        return carry

    lax.fori_loop(0, hidden_units // tile, step, 0)
    hidden_ref[...] = start_ref[...] + dot(act_ref[...], down_ref[...])


def feed(normed, into, bias, down, start):
    tokens, width = normed.shape
    units = into.shape[1]
    return call(
        feed_kernel,
        [shaped((tokens, units), bfloat), shaped((tokens, units), bfloat), shaped((tokens, width), single)],
        normed,
        into,
        bias,
        down,
        start,
    )


def add_columns(ref, row, value):
    ref[row : row + 1, :] += jnp.sum(value, axis=0, keepdims=True)


def turn_kernel(hidden_ref, gain_ref, shift_ref, upstream_ref, unit_ref, result_ref, grad_ref, branch_ref, sums_ref):
    sums_ref[...] = jnp.zeros_like(sums_ref)

    def body(at):
        unit, scale = unit_of(hidden_ref[at, :])
        gain = gain_ref[1:2, :]
        upstream = upstream_ref[at, :].astype(single)
        unit_ref[at, :] = unit
        result_ref[at, :] = (unit * gain + shift_ref[1:2, :]).astype(bfloat)
        grad = norm_back(upstream, unit, scale, gain)
        grad_ref[at, :] = grad
        branch_ref[at, :] = grad.astype(bfloat)
        add_columns(sums_ref, 0, upstream * unit)
        add_columns(sums_ref, 1, upstream)
        add_columns(sums_ref, 2, grad)

    strips(hidden_ref.shape[0], body)


def feed_back_kernel(branch_ref, down_ref, slope_ref, into_ref, start_ref, grad_ref, sums_ref, normed_ref):
    hidden_units = into_ref.shape[1]
    tile = 256

    def step(j, carry):
        at = pl.ds(pl.multiple_of(j * tile, tile), tile)
        pre = dot_cols(branch_ref[...], down_ref[at, :]) * slope_ref[:, at].astype(single)
        low = pre.astype(bfloat)
        grad_ref[:, at] = low
        sums_ref[:, at] = jnp.sum(low.astype(single), axis=0, keepdims=True)
        return carry

    lax.fori_loop(0, hidden_units // tile, step, 0)
    normed_ref[...] = start_ref[...] + dot_cols(grad_ref[...], into_ref[...])


def feed_back(branch, down, slope, into, start):
    tokens, width = branch.shape
    units = into.shape[1]
    return call(
        feed_back_kernel,
        [shaped((tokens, units), bfloat), shaped((1, units), single), shaped((tokens, width), single)],
        branch,
        down,
        slope,
        into,
        start,
    )


def norm_back_kernel(hidden_ref, gain_ref, upstream_ref, grad_ref, low_ref, sums_ref):
    sums_ref[...] = jnp.zeros_like(sums_ref)

    def body(at):
        unit, scale = unit_of(hidden_ref[at, :])
        upstream = upstream_ref[at, :]
        grad = norm_back(upstream, unit, scale, gain_ref[0:1, :])
        grad_ref[at, :] = grad
        low_ref[at, :] = grad.astype(bfloat)
        add_columns(sums_ref, 0, upstream * unit)
        add_columns(sums_ref, 1, upstream)
        add_columns(sums_ref, 2, grad)

    strips(hidden_ref.shape[0], body)


def attend_back_kernel(upstream_ref, out_w_ref, parts_ref, chance_ref, qkv_ref, start_ref, grad_ref, sums_ref, rows_ref, turned_ref):
    tokens = upstream_ref.shape[0]
    local = out_w_ref.shape[0]
    tile = 256
    factor = HEAD_DIM**-0.5

    def pair_step(pair, carry):
        at = pl.multiple_of(pair * PAIR, PAIR)
        lanes = pl.ds(at, PAIR)
        queries = parts_ref[0, :, lanes]
        keys_turned = parts_ref[1, :, lanes].T
        values = parts_ref[2, :, lanes]
        grad_context = dot_cols(upstream_ref[...], out_w_ref[lanes, :]).astype(bfloat)
        context_turned = grad_context.T
        owner = lax.broadcasted_iota(jnp.int32, (PAIR, tile), 0) // HEAD_DIM
        first_lane = lax.broadcasted_iota(jnp.int32, (tokens, PAIR), 1) < HEAD_DIM
        grads_k, grads_v = [], []
        for h in range(2):
            key_rows = keys_turned[h * HEAD_DIM : (h + 1) * HEAD_DIM]
            grad_k = jnp.zeros((tokens, PAIR), single)
            grad_v = jnp.zeros((tokens, PAIR), single)
            for q in range(tokens // tile):
                cut = slice(q * tile, (q + 1) * tile)
                picked = context_turned[:, cut]
                picked = jnp.where(owner == h, picked, jnp.zeros_like(picked))
                chances_low = chance_ref[pair * 2 + h, :, cut]
                chances = chances_low.astype(single)
                grad_chances = dot(values, picked)
                inner = jnp.sum(chances * grad_chances, axis=0, keepdims=True)
                grad_scores = (chances * (grad_chances - inner)).astype(bfloat)
                grad_v = grad_v + dot(chances_low, grad_context[cut, :])
                grad_k = grad_k + dot(grad_scores, queries[cut, :])
                turned_ref[pl.ds(pl.multiple_of(at + h * HEAD_DIM, HEAD_DIM), HEAD_DIM), cut] = (dot(key_rows, grad_scores) * factor).astype(bfloat)
            grads_k.append(grad_k)
            grads_v.append(grad_v)
        grad_k = (jnp.where(first_lane, grads_k[0], grads_k[1]) * factor).astype(bfloat)
        grad_v = jnp.where(first_lane, grads_v[0], grads_v[1]).astype(bfloat)
        grad_ref[:, pl.ds(pl.multiple_of(local + at, PAIR), PAIR)] = grad_k
        grad_ref[:, pl.ds(pl.multiple_of(2 * local + at, PAIR), PAIR)] = grad_v
        return carry

    lax.fori_loop(0, local // PAIR, pair_step, 0)
    grad_ref[:, 0:local] = turned_ref[...].T
    sums_ref[...] = jnp.sum(grad_ref[...].astype(single), axis=0, keepdims=True)
    total = start_ref[...]
    for part in range(3):
        total = total + dot_cols(grad_ref[:, part * local : (part + 1) * local], qkv_ref[part])
    rows_ref[...] = total


def attend_back(upstream, out, parts, chances, qkv, start):
    tokens, width = upstream.shape
    local = out.shape[0]
    return call(
        attend_back_kernel,
        [shaped((tokens, 3 * local), bfloat), shaped((1, 3 * local), single), shaped((tokens, width), single)],
        upstream,
        out,
        parts,
        chances,
        qkv,
        start,
        scratch=[pltpu.VMEM((local, tokens), bfloat)],
    )


def body(
    inputs,
    lengths,
    w_qkv,
    b_qv,
    w_out,
    b_out,
    ln_gains,
    ln_biases,
    w_in,
    b_in,
    w_down,
    b_down,
    cotangent,
):
    size = lax.axis_size("dp")
    me = lax.axis_index("dp")
    side = lax.axis_index("tensor")
    tokens, width = inputs.shape[1:]
    local = w_qkv.shape[2]
    units = w_in.shape[1]
    rows = lax.dynamic_index_in_dim(inputs, side, 0, keepdims=False)
    length = lax.dynamic_slice_in_dim(lengths, side, 1)
    upstream = lax.dynamic_index_in_dim(cotangent, side, 0, keepdims=False)

    qkv_own = jnp.transpose(w_qkv, (1, 0, 2))
    small_other = swap_x(jnp.concatenate([b_qv.reshape(-1), b_in]))
    b_qv_other, b_in_other = small_other[: 2 * local].reshape(2, local), small_other[2 * local :]
    qkv_other = place([fetch_spread(qkv_own, me, size, (4, 2))], qkv_own.shape)
    out_other = place([fetch_direct(w_out, me, size)], w_out.shape)
    in_other = place([fetch_spread(w_in, me, size, (2, 4))], w_in.shape)
    cut, end = units // 2, 3 * units // 4
    down_other = place(
        [
            fetch_spread(w_down[:cut], me, size, (4, 2)),
            fetch_spread(w_down[cut:end], me, size, (2, 4), base=cut),
            fetch_direct(w_down[end:], me, size, base=end),
        ],
        w_down.shape,
    )
    sides = (
        (qkv_own, b_qv, w_out, w_in, b_in.reshape(1, -1), w_down),
        (qkv_other, b_qv_other, out_other, in_other, b_in_other.reshape(1, -1), down_other),
    )

    bits = size.bit_length() - 1
    share = width // size
    block_of = jnp.array([reverse_bits(p, bits) for p in range(size)], jnp.int32) ^ me
    source = (block_of[:, None] * share + jnp.arange(share)[None, :]).reshape(-1, 1)

    heads = []
    hidden_one = rows.astype(single) + b_out
    for qkv, bias, out, _, _, _ in sides:
        parts, chances, context, hidden_one = attend(length, rows, qkv, bias, out, hidden_one)
        heads.append((parts, chances, context))
    normed_low, hidden_two = call(
        norm_kernel,
        [shaped((tokens, width), bfloat), shaped((tokens, width), single)],
        hidden_one,
        ln_gains,
        ln_biases,
        b_down.reshape(1, -1),
    )
    acts = []
    for _, _, _, into, bias, down in sides:
        act, slope, hidden_two = feed(normed_low, into, bias, down, hidden_two)
        acts.append((act, slope))
    unit_two, result, grad_two, branch, sums_two = call(
        turn_kernel,
        [
            shaped((tokens, width), single),
            shaped((tokens, width), bfloat),
            shaped((tokens, width), single),
            shaped((tokens, width), bfloat),
            shaped((3, width), single),
        ],
        hidden_two,
        ln_gains,
        ln_biases,
        upstream,
    )
    result_other = (swap_x(unit_two) * ln_gains[1] + ln_biases[1]).astype(bfloat)

    share_down = scatter_x_first(relative(branch, source), acts[0][0], acts[1][0], size)
    grad_pres, unit_sums = [], []
    grad_normed = grad_two
    for (_, slope), (_, _, _, into, _, down) in zip(acts, sides):
        grad_pre, unit_sum, grad_normed = feed_back(branch, down, slope, into, grad_normed)
        grad_pres.append(grad_pre)
        unit_sums.append(unit_sum)
    share_in = scatter_y_first(relative(normed_low, source), grad_pres[0], grad_pres[1], size)
    grad_one, attended, sums_one = call(
        norm_back_kernel,
        [shaped((tokens, width), single), shaped((tokens, width), bfloat), shaped((3, width), single)],
        hidden_one,
        ln_gains,
        grad_normed,
    )
    share_out = scatter_x_first(relative(attended, source), heads[0][2], heads[1][2], size)
    grad_rows = grad_one
    grad_projs, proj_sums = [], []
    for (parts, chances, _), (qkv, _, out, _, _, _) in zip(heads, sides):
        grad_proj, proj_sum, grad_rows = attend_back(attended, out, parts, chances, qkv, grad_rows)
        grad_projs.append(grad_proj)
        proj_sums.append(proj_sum)
    grad_rows_other = swap_x(grad_rows)
    share_qkv = scatter_y_first(relative(rows, source), grad_projs[0], grad_projs[1], size)

    every = jnp.concatenate([sums_one.reshape(-1), sums_two.reshape(-1)])
    vectors = jnp.concatenate([every, unit_sums[0].reshape(-1)])
    vectors_other = swap_x(jnp.concatenate([every, unit_sums[1].reshape(-1)]))
    vectors = sum_all(vectors + vectors_other, size)
    qv_own, qv_other = (
        jnp.concatenate([part[0, :local], part[0, 2 * local :]]) for part in proj_sums
    )
    grad_b_qv = sum_all(qv_own + swap_x(qv_other), size).reshape(2, local)
    gain_one, shift_one, b_out_g, gain_two, shift_two, b_down_g = (
        vectors[k * width : (k + 1) * width] for k in range(6)
    )

    def both(mine, other):
        mine, other = mine[None], other[None]
        return jnp.where(
            side == 0,
            jnp.concatenate([mine, other], axis=0),
            jnp.concatenate([other, mine], axis=0),
        )

    return (
        both(result, result_other),
        both(grad_rows, grad_rows_other),
        share_qkv.reshape(-1, 3, local),
        grad_b_qv,
        share_out.T,
        b_out_g,
        jnp.stack([gain_one, gain_two]),
        jnp.stack([shift_one, shift_two]),
        share_in,
        vectors[6 * width :],
        share_down.T,
        b_down_g,
    )


def solution(mesh):
    placed = (
        P("dp", None, None),
        P("dp"),
        P(None, None, "tensor"),
        P(None, "tensor"),
        P("tensor", None),
        P(),
        P(),
        P(),
        P(None, "tensor"),
        P("tensor"),
        P("tensor", None),
        P(),
        P("dp", None, None),
    )
    return jax.shard_map(
        body,
        mesh=mesh,
        in_specs=placed,
        out_specs=(
            P("dp", None, None),
            P("dp", None, None),
            P("dp", None, "tensor"),
            P(None, "tensor"),
            P("tensor", "dp"),
            P(),
            P(),
            P(),
            P("dp", "tensor"),
            P("tensor"),
            P("tensor", "dp"),
            P(),
        ),
        check_vma=False,
    )
```

```python
import functools

import jax
import jax.numpy as jnp
from jax import lax
from jax.experimental import pallas as pl
from jax.experimental.pallas import tpu as pltpu
from jax.sharding import PartitionSpec as P

HEAD_DIM = 64
PAIR = 2 * HEAD_DIM
norm_eps = 1e-12
bfloat = jnp.bfloat16
single = jnp.float32
MIB = 1 << 20
COST_UNIT = 0.5e9


def dot(left, right):
    return jnp.dot(left, right, preferred_element_type=single)


def dot_cols(left, right):
    return lax.dot_general(
        left, right, (((1,), (1,)), ((), ())), preferred_element_type=single
    )


def shaped(shape, dtype):
    return jax.ShapeDtypeStruct(shape, dtype)


class Order:
    def __init__(self):
        self.last = None

    def call(self, kernel, outs, *args, scalars=(), scratch=(), grid=(), in_specs=None, out_specs=None, limit=24, aliases=None, cost=1.0):
        many = isinstance(outs, (tuple, list))
        if in_specs is None:
            in_specs = [pl.BlockSpec(memory_space=pltpu.VMEM)] * len(args)
        if out_specs is None:
            out_specs = [pl.BlockSpec(memory_space=pltpu.VMEM)] * len(outs) if many else pl.BlockSpec(memory_space=pltpu.VMEM)
        in_specs = [pl.BlockSpec(memory_space=pltpu.SMEM)] * len(scalars) + list(in_specs)
        operands = list(scalars) + list(args)
        run = kernel
        if self.last is not None:
            before = len(operands)
            operands.append(self.last)
            in_specs.append(pl.BlockSpec(memory_space=pl.ANY))

            def run(*refs):
                kernel(*refs[:before], *refs[before + 1 :])

        made = pl.pallas_call(
            run,
            out_shape=outs,
            grid=grid,
            in_specs=in_specs,
            out_specs=out_specs,
            scratch_shapes=list(scratch),
            input_output_aliases=aliases or {},
            compiler_params=pltpu.CompilerParams(vmem_limit_bytes=limit * MIB),
            cost_estimate=pl.CostEstimate(flops=int(cost * COST_UNIT), bytes_accessed=1000, transcendentals=0),
        )(*operands)
        self.last = made[-1] if many else made
        return made

    def pin(self, value):
        return self.call(
            lambda *refs: None,
            shaped(value.shape, value.dtype),
            value,
            in_specs=[pl.BlockSpec(memory_space=pl.ANY)],
            out_specs=pl.BlockSpec(memory_space=pl.ANY),
            aliases={0: 0},
            cost=0.0,
        )


class Chain:
    def __init__(self, steps):
        self.steps = steps
        self.value = None

    def step(self):
        self.value = next(self.steps, self.value)
        return self.value


def swap_dp(value, mask, size):
    return lax.ppermute(value, "dp", [(i, i ^ mask) for i in range(size)])


def swap_x(value):
    return lax.ppermute(value, "tensor", [(0, 1), (1, 0)])


def reverse_bits(position, bits):
    out = 0
    for k in range(bits):
        out |= ((position >> k) & 1) << (bits - 1 - k)
    return out


def place_kernel(groups, rows, order_ref, *refs):
    out_ref = refs[-1]
    at = 0
    for piece, count in zip(refs[:-1], groups):
        for b in range(count):
            start = pl.multiple_of(order_ref[at], 16)
            height = rows[at]
            if out_ref.ndim == 3:
                out_ref[:, pl.ds(start, height), :] = piece[b].astype(out_ref.dtype)
            else:
                out_ref[pl.ds(start, height), :] = piece[b].astype(out_ref.dtype)
            at += 1


def place(order, parts, shape):
    pieces, rows, starts = [], [], []
    for held, begin in parts:
        pieces += held
        starts += begin
        rows += [held[0].shape[-2]] * len(begin)
    groups = tuple(piece.shape[0] for piece in pieces)
    kernel = functools.partial(place_kernel, groups, tuple(rows))
    return order.call(kernel, shaped(shape, bfloat), *pieces, scalars=(jnp.stack(starts),), cost=2.4)


def pack_kernel(first_ref, second_ref, out_ref):
    out_ref[0] = first_ref[0]
    out_ref[1] = second_ref[0]


def fetch_spread(order, own, me, size, masks, base=0):
    first, second = masks
    rank = me & 7
    rows = own.shape[-2] // 8
    held = lax.dynamic_slice_in_dim(own, rank * rows, rows, axis=own.ndim - 2).astype(single)
    held = swap_x(held[None])
    yield
    held = order.pin(held)
    arrived = swap_dp(held, first, size)
    yield
    both = order.call(pack_kernel, shaped((2,) + held.shape[1:], single), held, arrived, cost=2.0)
    arrived = swap_dp(both, second, size)
    both_core = swap_dp(both, 1, size)
    yield
    arrived = order.pin(arrived)
    arrived_core = swap_dp(arrived, 1, size)
    offsets = [0, first, second, first ^ second]
    offsets = offsets + [o ^ 1 for o in offsets]
    yield [both, arrived, both_core, arrived_core], [base + (rank ^ o) * rows for o in offsets]


def fetch_direct(order, own, me, size, base=0):
    rows = own.shape[0] // 2
    core = me & 1
    held = swap_x(lax.dynamic_slice_in_dim(own, core * rows, rows).astype(single)[None])
    yield
    held = order.pin(held)
    yield [held, swap_dp(held, 1, size)], [base + core * rows, base + (1 - core) * rows]


def sum_all(value, size):
    for k in range(size.bit_length() - 1):
        value = value + swap_dp(value, 1 << k, size)
    return value


def product_kernel(sides, terms, cuts, *refs):
    left_ref = refs[0]
    rights = refs[1 : 1 + sides]
    added = refs[1 + sides : 1 + sides + terms]
    outs = refs[1 + sides + terms :]
    parts = len(outs)
    for s, right_ref in enumerate(rights):
        total = dot(left_ref[...], right_ref[...])
        for term in added:
            total = total + term[s]
        height = total.shape[0] // parts
        for k, out_ref in enumerate(outs):
            out_ref[s] = total[k * height : (k + 1) * height]


def product(order, left, half, rights, added=(), parts=1):
    depth, tokens = left.shape
    rows = depth // 2
    width = rights[0][2]
    tile = 384 if width % 384 == 0 else 128
    sides = len(rights)

    def right_spec(first):
        return pl.BlockSpec((tokens, tile), lambda j: (0, j + first // tile))

    def block(height):
        return pl.BlockSpec((sides, height, tile), lambda j: (0, 0, j))

    outs = order.call(
        functools.partial(product_kernel, sides, len(added), parts),
        [shaped((sides, rows // parts, width), single)] * parts,
        left,
        *[right[0] for right in rights],
        *added,
        grid=(width // tile,),
        in_specs=[
            pl.BlockSpec((rows, tokens), lambda j: (half, 0)),
            *[right_spec(right[1]) for right in rights],
            *[block(rows) for _ in added],
        ],
        out_specs=[block(rows // parts)] * parts,
        cost=sides * width / 1024,
    )
    return outs


def sum_kernel(parts, first_ref, second_ref, *outs):
    if first_ref.shape == outs[0].shape:
        outs[0][...] = first_ref[...] + second_ref[...]
        return
    height = first_ref.shape[1] // 2
    for k in range(2):
        outs[k][...] = first_ref[:, k * height : (k + 1) * height] + second_ref[:, k * height : (k + 1) * height]


def add_split(order, first, second):
    sides, rows, width = first.shape
    half = shaped((sides, rows // 2, width), single)
    return order.call(functools.partial(sum_kernel, 2), [half, half], first, second, cost=0.7)


def add_whole(order, first, second):
    return order.call(functools.partial(sum_kernel, 1), shaped(first.shape, single), first, second, cost=0.5)


def scatter_x_first(order, left, own, other, size):
    (sent,) = product(order, left, 1, [other, own])
    arrived = swap_dp(sent, 1, size)
    yield
    (across,) = product(order, left, 0, [other], [arrived])
    across = swap_x(across)
    yield
    low, high = product(order, left, 0, [own], [arrived[1:], across], parts=2)
    for k in range(1, size.bit_length() - 1):
        arrived = swap_dp(high, 1 << k, size)
        yield
        if k + 2 < size.bit_length():
            low, high = add_split(order, low, arrived)
    yield add_whole(order, low, arrived)[0]


def scatter_y_first(order, left, own, other, size):
    (sent,) = product(order, left, 1, [own, other])
    arrived = swap_dp(sent, 1, size)
    yield
    low, high = product(order, left, 0, [own, other], [arrived], parts=2)
    for k in range(1, size.bit_length() - 1):
        arrived = swap_dp(high, 1 << k, size)
        yield
        if k + 2 < size.bit_length():
            low, high = add_split(order, low, arrived)
    total = add_whole(order, low, arrived)
    arrived = swap_x(total[1:])
    yield
    yield add_whole(order, total[:1], arrived)[0]


def relative_kernel(value_ref, source_ref, out_ref):
    depth = value_ref.shape[1]
    tile = depth // 4

    def step(j, carry):
        at = pl.multiple_of(j * tile, 16)
        lanes = lax.broadcasted_iota(jnp.int32, (tile, depth), 1)
        picks = jnp.where(lanes == source_ref[pl.ds(at, tile), :], 1.0, 0.0).astype(bfloat)
        out_ref[pl.ds(at, tile), :] = dot_cols(picks, value_ref[...]).astype(bfloat)
        return carry

    lax.fori_loop(0, 4, step, 0)


def relative(order, value, source):
    return order.call(relative_kernel, shaped(value.shape[::-1], bfloat), value, source, cost=1.7)


def attend_kernel(length_ref, rows_ref, qkv_ref, bias_ref, out_w_ref, start_ref, parts_ref, chance_ref, context_ref, hidden_ref, turned_ref):
    tokens = rows_ref.shape[0]
    local = qkv_ref.shape[2]
    rows = rows_ref[...]
    for part in range(3):
        projected = dot(rows, qkv_ref[part])
        if part == 0:
            projected = projected + bias_ref[0:1, :]
        elif part == 2:
            projected = projected + bias_ref[1:2, :]
        parts_ref[part] = projected.astype(bfloat)
    tile = 256
    visible = lax.broadcasted_iota(jnp.int32, (tokens, tile), 0) < length_ref[0]

    def pair_step(pair, carry):
        at = pl.multiple_of(pair * PAIR, PAIR)
        keys = parts_ref[1, :, pl.ds(at, PAIR)]
        queries = parts_ref[0, :, pl.ds(at, PAIR)].T
        values = parts_ref[2, :, pl.ds(at, PAIR)].T
        owner = lax.broadcasted_iota(jnp.int32, (PAIR, tile), 0) // HEAD_DIM
        for h in range(2):
            value_rows = values[h * HEAD_DIM : (h + 1) * HEAD_DIM]
            for q in range(tokens // tile):
                picked = queries[:, q * tile : (q + 1) * tile] * HEAD_DIM**-0.5
                picked = jnp.where(owner == h, picked, jnp.zeros_like(picked))
                scores = jnp.where(visible, dot(keys, picked), -1e9)
                raised = jnp.exp(scores - jnp.max(scores, axis=0, keepdims=True))
                chances = raised * (1.0 / jnp.sum(raised, axis=0, keepdims=True))
                chances = chances.astype(bfloat)
                chance_ref[pair * 2 + h, :, q * tile : (q + 1) * tile] = chances
                turned_ref[pl.ds(pl.multiple_of(at + h * HEAD_DIM, HEAD_DIM), HEAD_DIM), q * tile : (q + 1) * tile] = dot(value_rows, chances).astype(bfloat)
        return carry

    lax.fori_loop(0, local // PAIR, pair_step, 0)
    context = turned_ref[...].T
    context_ref[...] = context
    hidden_ref[...] = start_ref[...] + dot(context, out_w_ref[...])


def attend(order, length, rows, qkv, bias, out, start):
    tokens, width = rows.shape
    local = qkv.shape[2]
    return order.call(
        attend_kernel,
        [
            shaped((3, tokens, local), bfloat),
            shaped((local // HEAD_DIM, tokens, tokens), bfloat),
            shaped((tokens, local), bfloat),
            shaped((tokens, width), single),
        ],
        rows,
        qkv,
        bias,
        out,
        start,
        scalars=(length,),
        scratch=[pltpu.VMEM((local, tokens), bfloat)],
        cost=9.0,
    )


def unit_of(hidden):
    centred = hidden - jnp.mean(hidden, axis=-1, keepdims=True)
    scale = lax.rsqrt(jnp.mean(centred * centred, axis=-1, keepdims=True) + norm_eps)
    return centred * scale, scale


def norm_back(upstream, unit, scale, gain):
    scaled = upstream * gain
    return scale * (
        scaled
        - jnp.mean(scaled, axis=-1, keepdims=True)
        - unit * jnp.mean(scaled * unit, axis=-1, keepdims=True)
    )


STRIP = 128


def strips(tokens, body):
    def step(j, carry):
        body(pl.ds(pl.multiple_of(j * STRIP, STRIP), STRIP))
        return carry

    lax.fori_loop(0, tokens // STRIP, step, 0)


def norm_kernel(hidden_ref, gain_ref, shift_ref, down_ref, low_ref, next_ref):
    def body(at):
        unit, _ = unit_of(hidden_ref[at, :])
        normed = unit * gain_ref[0:1, :] + shift_ref[0:1, :]
        low_ref[at, :] = normed.astype(bfloat)
        next_ref[at, :] = normed + down_ref[...]

    strips(hidden_ref.shape[0], body)


def feed_kernel(normed_ref, into_ref, bias_ref, down_ref, start_ref, act_ref, slope_ref, hidden_ref):
    hidden_units = into_ref.shape[1]
    tile = 256

    def step(j, carry):
        at = pl.ds(pl.multiple_of(j * tile, tile), tile)
        for k in range(2):
            strip = pl.ds(k * 256, 256)
            pre = dot(normed_ref[strip, :], into_ref[:, at]) + bias_ref[:, at]
            bell = jnp.exp(-0.5 * pre * pre)
            reach = 1.0 / (1.0 + 0.23164189 * jnp.abs(pre))
            tail = reach * (
                0.127414796
                + reach * (-0.142248368 + reach * (0.7107068705 + reach * (-0.7265760135 + reach * 0.5307027145)))
            )
            tail = tail * bell
            chance = jnp.where(pre >= 0, 1.0 - tail, tail)
            act_ref[strip, at] = (pre * chance).astype(bfloat)
            slope_ref[strip, at] = (chance + pre * bell * 0.3989422804014327).astype(bfloat)
        return carry

    lax.fori_loop(0, hidden_units // tile, step, 0)
    hidden_ref[...] = start_ref[...] + dot(act_ref[...], down_ref[...])


def feed(order, normed, into, bias, down, start):
    tokens, width = normed.shape
    units = into.shape[1]
    return order.call(
        feed_kernel,
        [shaped((tokens, units), bfloat), shaped((tokens, units), bfloat), shaped((tokens, width), single)],
        normed,
        into,
        bias,
        down,
        start,
        cost=6.0,
    )


def add_columns(ref, row, value):
    ref[row : row + 1, :] += jnp.sum(value, axis=0, keepdims=True)


def turn_kernel(hidden_ref, gain_ref, shift_ref, upstream_ref, result_ref, grad_ref, sums_ref, unit_ref, branch_ref):
    sums_ref[...] = jnp.zeros_like(sums_ref)

    def body(at):
        unit, scale = unit_of(hidden_ref[at, :])
        gain = gain_ref[1:2, :]
        upstream = upstream_ref[at, :].astype(single)
        unit_ref[at, :] = unit
        result_ref[at, :] = (unit * gain + shift_ref[1:2, :]).astype(bfloat)
        grad = norm_back(upstream, unit, scale, gain)
        grad_ref[at, :] = grad
        branch_ref[at, :] = grad.astype(bfloat)
        add_columns(sums_ref, 0, upstream * unit)
        add_columns(sums_ref, 1, upstream)
        add_columns(sums_ref, 2, grad)

    strips(hidden_ref.shape[0], body)


def feed_back_kernel(branch_ref, down_ref, slope_ref, into_ref, start_ref, grad_ref, sums_ref, normed_ref):
    hidden_units = into_ref.shape[1]
    tile = 256

    def step(j, carry):
        at = pl.ds(pl.multiple_of(j * tile, tile), tile)
        pre = dot_cols(branch_ref[...], down_ref[at, :]) * slope_ref[:, at].astype(single)
        low = pre.astype(bfloat)
        grad_ref[:, at] = low
        sums_ref[:, at] = jnp.sum(low.astype(single), axis=0, keepdims=True)
        return carry

    lax.fori_loop(0, hidden_units // tile, step, 0)
    normed_ref[...] = start_ref[...] + dot_cols(grad_ref[...], into_ref[...])


def feed_back(order, branch, down, slope, into, start):
    tokens, width = branch.shape
    units = into.shape[1]
    return order.call(
        feed_back_kernel,
        [shaped((tokens, units), bfloat), shaped((1, units), single), shaped((tokens, width), single)],
        branch,
        down,
        slope,
        into,
        start,
        cost=3.9,
    )


def norm_back_kernel(hidden_ref, gain_ref, upstream_ref, grad_ref, sums_ref, low_ref):
    sums_ref[...] = jnp.zeros_like(sums_ref)

    def body(at):
        unit, scale = unit_of(hidden_ref[at, :])
        upstream = upstream_ref[at, :]
        grad = norm_back(upstream, unit, scale, gain_ref[0:1, :])
        grad_ref[at, :] = grad
        low_ref[at, :] = grad.astype(bfloat)
        add_columns(sums_ref, 0, upstream * unit)
        add_columns(sums_ref, 1, upstream)
        add_columns(sums_ref, 2, grad)

    strips(hidden_ref.shape[0], body)


def attend_back_kernel(upstream_ref, out_w_ref, parts_ref, chance_ref, qkv_ref, start_ref, grad_ref, sums_ref, rows_ref, turned_ref):
    tokens = upstream_ref.shape[0]
    local = out_w_ref.shape[0]
    tile = 256
    factor = HEAD_DIM**-0.5

    def pair_step(pair, carry):
        at = pl.multiple_of(pair * PAIR, PAIR)
        lanes = pl.ds(at, PAIR)
        queries = parts_ref[0, :, lanes]
        keys_turned = parts_ref[1, :, lanes].T
        values = parts_ref[2, :, lanes]
        grad_context = dot_cols(upstream_ref[...], out_w_ref[lanes, :]).astype(bfloat)
        context_turned = grad_context.T
        owner = lax.broadcasted_iota(jnp.int32, (PAIR, tile), 0) // HEAD_DIM
        first_lane = lax.broadcasted_iota(jnp.int32, (tokens, PAIR), 1) < HEAD_DIM
        grads_k, grads_v = [], []
        for h in range(2):
            key_rows = keys_turned[h * HEAD_DIM : (h + 1) * HEAD_DIM]
            grad_k = jnp.zeros((tokens, PAIR), single)
            grad_v = jnp.zeros((tokens, PAIR), single)
            for q in range(tokens // tile):
                cut = slice(q * tile, (q + 1) * tile)
                picked = context_turned[:, cut]
                picked = jnp.where(owner == h, picked, jnp.zeros_like(picked))
                chances_low = chance_ref[pair * 2 + h, :, cut]
                chances = chances_low.astype(single)
                grad_chances = dot(values, picked)
                inner = jnp.sum(chances * grad_chances, axis=0, keepdims=True)
                grad_scores = (chances * (grad_chances - inner)).astype(bfloat)
                grad_v = grad_v + dot(chances_low, grad_context[cut, :])
                grad_k = grad_k + dot(grad_scores, queries[cut, :])
                turned_ref[pl.ds(pl.multiple_of(at + h * HEAD_DIM, HEAD_DIM), HEAD_DIM), cut] = (dot(key_rows, grad_scores) * factor).astype(bfloat)
            grads_k.append(grad_k)
            grads_v.append(grad_v)
        grad_k = (jnp.where(first_lane, grads_k[0], grads_k[1]) * factor).astype(bfloat)
        grad_v = jnp.where(first_lane, grads_v[0], grads_v[1]).astype(bfloat)
        grad_ref[:, pl.ds(pl.multiple_of(local + at, PAIR), PAIR)] = grad_k
        grad_ref[:, pl.ds(pl.multiple_of(2 * local + at, PAIR), PAIR)] = grad_v
        return carry

    lax.fori_loop(0, local // PAIR, pair_step, 0)
    grad_ref[:, 0:local] = turned_ref[...].T
    sums_ref[...] = jnp.sum(grad_ref[...].astype(single), axis=0, keepdims=True)
    total = start_ref[...]
    for part in range(3):
        total = total + dot_cols(grad_ref[:, part * local : (part + 1) * local], qkv_ref[part])
    rows_ref[...] = total


def attend_back(order, upstream, out, parts, chances, qkv, start):
    tokens, width = upstream.shape
    local = out.shape[0]
    return order.call(
        attend_back_kernel,
        [shaped((tokens, 3 * local), bfloat), shaped((1, 3 * local), single), shaped((tokens, width), single)],
        upstream,
        out,
        parts,
        chances,
        qkv,
        start,
        scratch=[pltpu.VMEM((local, tokens), bfloat)],
        cost=9.4,
    )


def vectors_kernel(first_ref, second_ref, units_own, units_other, proj_own, proj_other, own_ref, other_ref):
    width = first_ref.shape[1]
    local = proj_own.shape[1] // 3
    for units, proj, out in ((units_own, proj_own, own_ref), (units_other, proj_other, other_ref)):
        out[...] = jnp.zeros_like(out)
        out[0:3, :] = first_ref[...]
        out[3:6, :] = second_ref[...]
        for k in range(units.shape[1] // width):
            out[6 + k : 7 + k, :] = units[:, k * width : (k + 1) * width]
        row = 6 + units.shape[1] // width
        out[row : row + 1, 0:local] = proj[:, 0:local]
        out[row : row + 1, local : 2 * local] = proj[:, 2 * local :]


def sum_vectors(order, own, other, size):
    arrived = swap_x(other)
    yield
    total = order.call(vector_add_kernel, shaped(own.shape, single), own, arrived, cost=0.1)
    for k in range(size.bit_length() - 1):
        arrived = swap_dp(total, 1 << k, size)
        yield
        total = order.call(vector_add_kernel, shaped(own.shape, single), total, arrived, cost=0.1)
    yield total


def vector_add_kernel(first_ref, second_ref, out_ref):
    out_ref[...] = first_ref[...] + second_ref[...]


def both_result_kernel(side_ref, mine_ref, unit_ref, gain_ref, shift_ref, out_ref):
    side = side_ref[0]
    out_ref[side] = mine_ref[...]

    def body(at):
        out_ref[1 - side, at, :] = (unit_ref[at, :] * gain_ref[1:2, :] + shift_ref[1:2, :]).astype(bfloat)

    strips(mine_ref.shape[0], body)


def both_kernel(side_ref, mine_ref, other_ref, out_ref):
    side = side_ref[0]
    out_ref[side] = mine_ref[...]
    out_ref[1 - side] = other_ref[...]


def body(
    inputs,
    lengths,
    w_qkv,
    b_qv,
    w_out,
    b_out,
    ln_gains,
    ln_biases,
    w_in,
    b_in,
    w_down,
    b_down,
    cotangent,
):
    size = lax.axis_size("dp")
    me = lax.axis_index("dp")
    side = lax.axis_index("tensor")
    side_index = side.astype(jnp.int32).reshape(1)
    tokens, width = inputs.shape[1:]
    local = w_qkv.shape[2]
    units = w_in.shape[1]
    rows = lax.dynamic_index_in_dim(inputs, side, 0, keepdims=False)
    length = lax.dynamic_slice_in_dim(lengths, side, 1)
    upstream = lax.dynamic_index_in_dim(cotangent, side, 0, keepdims=False)

    order = Order()

    bits = size.bit_length() - 1
    share = width // size
    block_of = jnp.array([reverse_bits(p, bits) for p in range(size)], jnp.int32) ^ me
    source = (block_of[:, None] * share + jnp.arange(share)[None, :]).reshape(-1, 1)

    qkv_own = jnp.transpose(w_qkv, (1, 0, 2))
    cut = width // 2
    middle = units // 2
    get_qkv = fetch_spread(order, qkv_own, me, size, (4, 2))
    get_in_z = fetch_spread(order, w_in[:cut], me, size, (4, 2))
    get_in_y = fetch_spread(order, w_in[cut:], me, size, (2, 4), base=cut)
    get_down_y = fetch_spread(order, w_down[:middle], me, size, (2, 4))
    get_out = fetch_direct(order, w_out, me, size)
    get_down_x = fetch_direct(order, w_down[middle:], me, size, base=middle)
    for chain in (get_qkv, get_in_z, get_in_y, get_down_y, get_out, get_down_x):
        next(chain)
    small_other = swap_x(jnp.concatenate([b_qv.reshape(-1), b_in]))
    b_qv_other, b_in_other = small_other[: 2 * local].reshape(2, local), small_other[2 * local :]

    heads = []
    hidden_one = rows.astype(single) + b_out
    parts, chances, context, hidden_one = attend(order, length, rows, qkv_own, b_qv, w_out, hidden_one)
    heads.append((parts, chances, context))
    next(get_qkv)
    next(get_in_z)
    next(get_in_y)
    next(get_qkv)
    next(get_down_y)
    next(get_in_y)
    next(get_in_z)
    parts_out = next(get_out)
    rows_rel = relative(order, rows, source)
    parts_qkv = next(get_qkv)
    parts_in_y = next(get_in_y)
    out_other = place(order, [parts_out], w_out.shape)
    qkv_other = place(order, [parts_qkv], qkv_own.shape)
    next(get_down_y)
    parts, chances, context, hidden_one = attend(order, length, rows, qkv_other, b_qv_other, out_other, hidden_one)
    heads.append((parts, chances, context))
    parts_in_z = next(get_in_z)
    parts_down_y = next(get_down_y)
    parts_down_x = next(get_down_x)
    normed_low, hidden_two = order.call(
        norm_kernel,
        [shaped((tokens, width), bfloat), shaped((tokens, width), single)],
        hidden_one,
        ln_gains,
        ln_biases,
        b_down.reshape(1, -1),
    )
    acts = []
    act, slope, hidden_two = feed(order, normed_low, w_in, b_in.reshape(1, -1), w_down, hidden_two)
    acts.append((act, slope))
    normed_rel = relative(order, normed_low, source)
    in_other = place(order, [parts_in_z, parts_in_y], w_in.shape)
    down_other = place(order, [parts_down_y, parts_down_x], w_down.shape)
    act, slope, hidden_two = feed(order, normed_low, in_other, b_in_other.reshape(1, -1), down_other, hidden_two)
    acts.append((act, slope))
    result, grad_two, sums_two, unit_two, branch = order.call(
        turn_kernel,
        [
            shaped((tokens, width), bfloat),
            shaped((tokens, width), single),
            shaped((3, width), single),
            shaped((tokens, width), single),
            shaped((tokens, width), bfloat),
        ],
        hidden_two,
        ln_gains,
        ln_biases,
        upstream,
    )

    half = units // 2
    branch_rel = relative(order, branch, source)
    down_x = Chain(scatter_x_first(order, branch_rel, (acts[0][0], 0, half), (acts[1][0], 0, half), size))
    down_y = Chain(scatter_y_first(order, branch_rel, (acts[0][0], half, half), (acts[1][0], half, half), size))
    down_x.step()
    down_y.step()
    unit_other = swap_x(unit_two)
    pre_other, unit_sum_other, grad_normed = feed_back(order, branch, down_other, acts[1][1], in_other, grad_two)
    down_x.step()
    pre_own, unit_sum_own, grad_normed = feed_back(order, branch, w_down, acts[0][1], w_in, grad_normed)
    down_y.step()
    in_y = Chain(scatter_y_first(order, normed_rel, (pre_own, half, half), (pre_other, half, half), size))
    in_x = Chain(scatter_x_first(order, normed_rel, (pre_own, 0, half), (pre_other, 0, half), size))
    in_x.step()
    in_y.step()
    grad_one, sums_one, attended = order.call(
        norm_back_kernel,
        [shaped((tokens, width), single), shaped((3, width), single), shaped((tokens, width), bfloat)],
        hidden_one,
        ln_gains,
        grad_normed,
    )
    attended_rel = relative(order, attended, source)
    out_x = Chain(scatter_x_first(order, attended_rel, (heads[0][2], 0, local), (heads[1][2], 0, local), size))
    out_x.step()
    in_x.step()
    down_x.step()
    in_y.step()
    out_x.step()
    grad_rows = grad_one
    proj_other, proj_sum_other, grad_rows = attend_back(order, attended, out_other, heads[1][0], heads[1][1], qkv_other, grad_rows)
    down_y.step()
    down_x.step()
    proj_own, proj_sum_own, grad_rows = attend_back(order, attended, w_out, heads[0][0], heads[0][1], qkv_own, grad_rows)
    cut = 768 if local == 384 else local
    last = 3 * local
    qkv_x = Chain(scatter_x_first(order, rows_rel, (proj_own, 0, cut), (proj_other, 0, cut), size))
    qkv_y = Chain(scatter_y_first(order, rows_rel, (proj_own, cut, last - cut), (proj_other, cut, last - cut), size))
    own_vectors, other_vectors = order.call(
        vectors_kernel,
        [shaped((16, width), single)] * 2,
        sums_one,
        sums_two,
        unit_sum_own,
        unit_sum_other,
        proj_sum_own,
        proj_sum_other,
        cost=0.5,
    )
    vectors = Chain(sum_vectors(order, own_vectors, other_vectors, size))
    qkv_x.step()
    qkv_y.step()
    grad_rows_other = swap_x(grad_rows)
    in_x.step()
    down_y.step()
    down_x.step()
    out_x.step()
    results = order.call(
        both_result_kernel,
        shaped((2, tokens, width), bfloat),
        result,
        unit_other,
        ln_gains,
        ln_biases,
        scalars=(side_index,),
        cost=1.5,
    )
    vectors.step()
    qkv_x.step()
    qkv_y.step()
    in_y.step()
    chains = (down_x, in_x, out_x, down_y, in_y, qkv_x, qkv_y, vectors)
    while any(chain.value is None for chain in chains):
        for chain in chains:
            if chain.value is None:
                chain.step()
    grads = order.call(
        both_kernel,
        shaped((2, tokens, width), single),
        grad_rows,
        grad_rows_other,
        scalars=(side_index,),
        cost=2.0,
    )
    share_down = jnp.concatenate([down_x.value, down_y.value], axis=1)
    share_in = jnp.concatenate([in_x.value, in_y.value], axis=1)
    share_qkv = jnp.concatenate([qkv_x.value, qkv_y.value], axis=1)

    total = vectors.value
    grad_b_in = total[6 : 6 + units // width].reshape(-1)
    grad_b_qv = total[6 + units // width].reshape(2, local)

    return (
        results,
        grads,
        share_qkv.reshape(-1, 3, local),
        grad_b_qv,
        out_x.value.T,
        total[2],
        jnp.stack([total[0], total[3]]),
        jnp.stack([total[1], total[4]]),
        share_in,
        grad_b_in,
        share_down.T,
        total[5],
    )


def solution(mesh):
    placed = (
        P("dp", None, None),
        P("dp"),
        P(None, None, "tensor"),
        P(None, "tensor"),
        P("tensor", None),
        P(),
        P(),
        P(),
        P(None, "tensor"),
        P("tensor"),
        P("tensor", None),
        P(),
        P("dp", None, None),
    )
    return jax.shard_map(
        body,
        mesh=mesh,
        in_specs=placed,
        out_specs=(
            P("dp", None, None),
            P("dp", None, None),
            P("dp", None, "tensor"),
            P(None, "tensor"),
            P("tensor", "dp"),
            P(),
            P(),
            P(),
            P("dp", "tensor"),
            P("tensor"),
            P("tensor", "dp"),
            P(),
        ),
        check_vma=False,
    )
```

```python
import functools

import jax
import jax.numpy as jnp
from jax import lax
from jax.experimental import pallas as pl
from jax.experimental.pallas import tpu as pltpu
from jax.sharding import PartitionSpec as P

HEAD_DIM = 64
PAIR = 2 * HEAD_DIM
norm_eps = 1e-12
bfloat = jnp.bfloat16
single = jnp.float32
MIB = 1 << 20
COST_UNIT = 1.0e9


def dot(left, right):
    return jnp.dot(left, right, preferred_element_type=single)


def dot_cols(left, right):
    return lax.dot_general(
        left, right, (((1,), (1,)), ((), ())), preferred_element_type=single
    )


def shaped(shape, dtype):
    return jax.ShapeDtypeStruct(shape, dtype)


class Order:
    def __init__(self):
        self.last = None

    def call(self, kernel, outs, *args, scalars=(), scratch=(), grid=(), in_specs=None, out_specs=None, limit=20, aliases=None, cost=1.0):
        many = isinstance(outs, (tuple, list))
        if in_specs is None:
            in_specs = [pl.BlockSpec(memory_space=pltpu.VMEM)] * len(args)
        if out_specs is None:
            out_specs = [pl.BlockSpec(memory_space=pltpu.VMEM)] * len(outs) if many else pl.BlockSpec(memory_space=pltpu.VMEM)
        in_specs = [pl.BlockSpec(memory_space=pltpu.SMEM)] * len(scalars) + list(in_specs)
        operands = list(scalars) + list(args)
        run = kernel
        if self.last is not None:
            before = len(operands)
            operands.append(self.last)
            in_specs.append(pl.BlockSpec(memory_space=pl.ANY))

            def run(*refs):
                kernel(*refs[:before], *refs[before + 1 :])

        made = pl.pallas_call(
            run,
            out_shape=outs,
            grid=grid,
            in_specs=in_specs,
            out_specs=out_specs,
            scratch_shapes=list(scratch),
            input_output_aliases=aliases or {},
            compiler_params=pltpu.CompilerParams(vmem_limit_bytes=limit * MIB),
            cost_estimate=pl.CostEstimate(flops=int(cost * COST_UNIT), bytes_accessed=1000, transcendentals=0),
        )(*operands)
        self.last = made[-1] if many else made
        return made

    def pin(self, value):
        return self.call(
            lambda *refs: None,
            shaped(value.shape, value.dtype),
            value,
            in_specs=[pl.BlockSpec(memory_space=pl.ANY)],
            out_specs=pl.BlockSpec(memory_space=pl.ANY),
            aliases={0: 0},
            cost=0.0,
        )


class Chain:
    def __init__(self, steps):
        self.steps = steps
        self.value = None

    def step(self):
        self.value = next(self.steps, self.value)
        return self.value

    def run(self, count):
        for _ in range(count):
            self.step()


def swap_dp(value, mask, size):
    return lax.ppermute(value, "dp", [(i, i ^ mask) for i in range(size)])


def swap_x(value):
    return lax.ppermute(value, "tensor", [(0, 1), (1, 0)])


def reverse_bits(position, bits):
    out = 0
    for k in range(bits):
        out |= ((position >> k) & 1) << (bits - 1 - k)
    return out


def place_kernel(groups, rows, order_ref, *refs):
    out_ref = refs[-1]
    at = 0
    for piece, count in zip(refs[:-1], groups):
        for b in range(count):
            start = pl.multiple_of(order_ref[at], 16)
            height = rows[at]
            for c in range(piece.shape[1]):
                if out_ref.ndim == 3:
                    out_ref[c, pl.ds(start, height), :] = piece[b, c].astype(out_ref.dtype)
                else:
                    lanes = slice(c * piece.shape[3], (c + 1) * piece.shape[3])
                    out_ref[pl.ds(start, height), lanes] = piece[b, c].astype(out_ref.dtype)
            at += 1


def place(order, parts, shape):
    pieces, rows, starts = [], [], []
    for held, begin in parts:
        pieces += held
        starts.append(begin)
        rows += [held[0].shape[-2]] * begin.shape[0]
    groups = tuple(piece.shape[0] for piece in pieces)
    kernel = functools.partial(place_kernel, groups, tuple(rows))
    return order.call(kernel, shaped(shape, bfloat), *pieces, scalars=(jnp.concatenate(starts).astype(jnp.int32),), cost=2.4)


def pack_kernel(first_ref, second_ref, out_ref):
    out_ref[0] = first_ref[0]
    out_ref[1] = second_ref[0]


def swap_mixed(value, first, second, size):
    pairs = []
    for d in range(size):
        mask = second if d & 1 else first
        for t in range(2):
            to = (d, 1 - t) if mask is None else (d ^ mask, t)
            pairs.append((2 * d + t, 2 * to[0] + to[1]))
    return lax.ppermute(value, ("dp", "tensor"), pairs)


def swap_x_core(value, core, size):
    pairs = [(2 * d + t, 2 * d + 1 - t) for d in range(core, size, 2) for t in range(2)]
    return lax.ppermute(value, ("dp", "tensor"), pairs)


def fetch_spread(order, held, me, size, pack_cost):
    rank = me & 7
    core = me & 1
    arrived = swap_mixed(held, 4, 2, size)
    yield
    both = order.call(pack_kernel, shaped((2,) + held.shape[1:], single), held, arrived, cost=pack_cost)
    arrived = swap_mixed(both, 2, 4, size)
    both_core = swap_dp(both, 1, size)
    yield
    both_core = order.pin(both_core)
    yield
    arrived = order.pin(arrived)
    arrived_core = swap_dp(arrived, 1, size)
    even, odd = jnp.array([0, 4, 2, 6], jnp.int32), jnp.array([0, 2, 4, 6], jnp.int32)
    mine = rank ^ jnp.where(core == 0, even, odd)
    sibling = rank ^ 1 ^ jnp.where(core == 0, odd, even)
    yield [both, arrived, both_core, arrived_core], jnp.concatenate([mine, sibling]) * held.shape[-2]


def unpack_kernel(all_ref, into_ref, down_ref):
    rows = into_ref.shape[2]
    for c in range(2):
        into_ref[0, c] = all_ref[c * rows : (c + 1) * rows, :]
    down_ref[0, 0] = all_ref[2 * rows :, :]


def product_kernel(groups, places, extras, core_ref, *refs):
    lefts, rights = refs[: len(groups)], refs[len(groups) : 3 * len(groups)]
    rest = refs[3 * len(groups) :]
    tile = pl.program_id(0)
    first = core_ref[0] == 0

    def spread(side, total, low_ref, high_ref, table, height):
        half = len(table[0])
        for block in range(half):
            at = table[side][block]
            out_ref, at = (low_ref, at) if at < half else (high_ref, at - half)
            out_ref[at * height : (at + 1) * height, :] = total[block * height : (block + 1) * height]

    def run(k, j):
        for side in range(2):
            total = dot(lefts[k][...], rights[2 * k + side][...])
            if places is None:
                rest[j][side] = total
                continue
            total = total + rest[j][side]
            low_ref, high_ref = rest[sum(groups) + extras :][:2]
            even, odd, height = places
            pl.when(first)(lambda: spread(side, total, low_ref, high_ref, even, height))
            pl.when(jnp.logical_not(first))(lambda: spread(side, total, low_ref, high_ref, odd, height))

    j = 0
    for k, tiles in enumerate(groups):
        for _ in range(tiles):
            pl.when(tile == j)(functools.partial(run, k, j))
            j += 1
    if extras:
        total = rest[j][...] + rest[j + 1][...]
        low_ref, high_ref, extra_ref = rest[j + 2 :]
        extra_ref[...] = total
        high_ref[low_ref.shape[0] :, :] = total


TILE = 384


def product(order, core, half, terms, added=(), places=None, extras=()):
    rows = terms[0][0].shape[0] // 2
    tokens = terms[0][0].shape[1]
    groups = tuple(term[1].shape[1] // TILE for term in terms)
    begins = [sum(groups[:k]) for k in range(len(groups))]
    tiles = sum(groups)

    def right_spec(k):
        return pl.BlockSpec((tokens, TILE), lambda j: (0, jnp.clip(j - begins[k], 0, groups[k] - 1)))

    def tall(height):
        return shaped((height, tiles * TILE), single), pl.BlockSpec((height, TILE), lambda j: (0, j))

    piece = pl.BlockSpec((2, rows, TILE), lambda j: (0, 0, 0))
    if places is None:
        outs, out_specs = [shaped((2, rows, TILE), single)] * tiles, [piece] * tiles
    else:
        height = len(places[0][0]) * places[2]
        heights = [height, height] + [part.shape[0] for part in extras[:1]]
        if extras:
            heights[1] += heights[2]
        outs, out_specs = zip(*[tall(height) for height in heights])
    return order.call(
        functools.partial(product_kernel, groups, places, len(extras)),
        list(outs),
        *[term[0] for term in terms],
        *[side for term in terms for side in term[1:3]],
        *added,
        *extras,
        scalars=(core,),
        grid=(tiles,),
        in_specs=[
            *[pl.BlockSpec((rows, tokens), lambda j: (half, 0)) for _ in terms],
            *[right_spec(k) for k in range(len(terms)) for _ in range(2)],
            *[piece for _ in added],
            *[tall(part.shape[0])[1] for part in extras],
        ],
        out_specs=list(out_specs),
        cost=tiles * 0.8 if places is None else tiles * 1.2,
    )


def sum_kernel(whole, low_ref, arrived_ref, *refs):
    rows = low_ref.shape[0]
    extra = refs[0][...] + arrived_ref[rows:, :] if arrived_ref.shape[0] > rows else None
    outs = refs if extra is None else refs[1:]
    if whole:
        outs[0][...] = low_ref[...] + arrived_ref[:rows, :]
    else:
        half = rows // 2
        outs[0][...] = low_ref[:half, :] + arrived_ref[:half, :]
        outs[1][:half, :] = low_ref[half:, :] + arrived_ref[half:rows, :]
    if extra is not None:
        outs[-1][...] = extra
        if not whole:
            outs[1][rows // 2 :, :] = extra


def add_arrived(order, low, arrived, extra, whole):
    rows, width = low.shape
    beyond = arrived.shape[0] - rows
    heights = [rows] if whole else [rows // 2, rows // 2 + beyond]
    heights += [beyond] if beyond else []
    outs = order.call(
        functools.partial(sum_kernel, whole),
        [shaped((height, width), single) for height in heights],
        low,
        arrived,
        *([extra] if beyond else []),
        cost=0.7,
    )
    return outs if beyond else [*outs, None]


def scatter(order, core, terms, orders, size, extra=None):
    masks = [1 << k for k in range(1, size.bit_length() - 1)]
    count = len(masks)

    def place_of(side, block, dims):
        at = 0
        for dim in dims:
            bit = side if dim is None else (block >> (count - 1 - masks.index(dim))) & 1
            at = 2 * at + bit
        return at

    tables = [
        [[place_of(side, block, dims) for block in range(1 << count)] for side in range(2)]
        for dims in orders
    ]
    sent = product(order, core, 1, terms)
    arrived = [swap_dp(part, 1, size) for part in sent]
    extras = () if extra is None else (extra, swap_dp(extra, 1, size))
    yield
    height = terms[0][0].shape[0] // size
    low, high, *extra = product(order, core, 0, terms, arrived, (*tables, height), extras)
    extra = extra[0] if extras else None
    for k in range(count + 1):
        arrived = swap_mixed(high, orders[0][k], orders[1][k], size)
        yield
        if k < count:
            low, high, extra = add_arrived(order, low, arrived, extra, False)
    total, extra = add_arrived(order, low, arrived, extra, True)
    yield (total, extra)


def relative_kernel(value_ref, source_ref, out_ref):
    depth = value_ref.shape[1]
    tile = depth // 4

    def step(j, carry):
        at = pl.multiple_of(j * tile, 16)
        lanes = lax.broadcasted_iota(jnp.int32, (tile, depth), 1)
        picks = jnp.where(lanes == source_ref[pl.ds(at, tile), :], 1.0, 0.0).astype(bfloat)
        out_ref[pl.ds(at, tile), :] = dot_cols(picks, value_ref[...]).astype(bfloat)
        return carry

    lax.fori_loop(0, 4, step, 0)


def relative(order, value, source):
    return order.call(relative_kernel, shaped(value.shape[::-1], bfloat), value, source, cost=1.7)


def attend_kernel(length_ref, rows_ref, qkv_ref, bias_ref, start_ref, *refs):
    *out_w, parts_ref, chance_ref, context_ref, hidden_ref, turned_ref = refs
    tokens = rows_ref.shape[0]
    local = qkv_ref.shape[2]
    rows = rows_ref[...]
    for part in range(3):
        projected = dot(rows, qkv_ref[part])
        if part == 0:
            projected = projected + bias_ref[0:1, :]
        elif part == 2:
            projected = projected + bias_ref[1:2, :]
        parts_ref[part] = projected.astype(bfloat)
    tile = 256
    visible = lax.broadcasted_iota(jnp.int32, (tokens, tile), 0) < length_ref[0]

    def pair_step(pair, carry):
        at = pl.multiple_of(pair * PAIR, PAIR)
        keys = parts_ref[1, :, pl.ds(at, PAIR)]
        queries = parts_ref[0, :, pl.ds(at, PAIR)].T
        values = parts_ref[2, :, pl.ds(at, PAIR)].T
        owner = lax.broadcasted_iota(jnp.int32, (PAIR, tile), 0) // HEAD_DIM
        for h in range(2):
            value_rows = values[h * HEAD_DIM : (h + 1) * HEAD_DIM]
            for q in range(tokens // tile):
                picked = queries[:, q * tile : (q + 1) * tile] * HEAD_DIM**-0.5
                picked = jnp.where(owner == h, picked, jnp.zeros_like(picked))
                scores = jnp.where(visible, dot(keys, picked), -1e9)
                raised = jnp.exp(scores - jnp.max(scores, axis=0, keepdims=True))
                chances = raised * (1.0 / jnp.sum(raised, axis=0, keepdims=True))
                chances = chances.astype(bfloat)
                chance_ref[pair * 2 + h, :, q * tile : (q + 1) * tile] = chances
                turned_ref[pl.ds(pl.multiple_of(at + h * HEAD_DIM, HEAD_DIM), HEAD_DIM), q * tile : (q + 1) * tile] = dot(value_rows, chances).astype(bfloat)
        return carry

    lax.fori_loop(0, local // PAIR, pair_step, 0)
    context = turned_ref[...].T
    context_ref[...] = context
    if out_w:
        hidden_ref[...] = rows_ref[...].astype(single) + start_ref[...] + dot(context, out_w[0][...])
    else:
        middle = hidden_ref.shape[1] // 2
        hidden_ref[:, :middle] = start_ref[:, :middle] + dot(context, qkv_ref[3, :local, :])
        hidden_ref[:, middle:] = start_ref[:, middle:] + dot(context, qkv_ref[3, local:, :])


def attend(order, length, rows, qkv, bias, start, out=None):
    tokens, width = rows.shape
    local = qkv.shape[2]
    return order.call(
        attend_kernel,
        [
            shaped((3, tokens, local), bfloat),
            shaped((local // HEAD_DIM, tokens, tokens), bfloat),
            shaped((tokens, local), bfloat),
            shaped((tokens, width), single),
        ],
        rows,
        qkv,
        bias,
        start,
        *([] if out is None else [out]),
        scalars=(length,),
        scratch=[pltpu.VMEM((local, tokens), bfloat)],
        cost=9.0,
    )


def unit_of(hidden):
    centred = hidden - jnp.mean(hidden, axis=-1, keepdims=True)
    scale = lax.rsqrt(jnp.mean(centred * centred, axis=-1, keepdims=True) + norm_eps)
    return centred * scale, scale


def norm_back(upstream, unit, scale, gain):
    scaled = upstream * gain
    return scale * (
        scaled
        - jnp.mean(scaled, axis=-1, keepdims=True)
        - unit * jnp.mean(scaled * unit, axis=-1, keepdims=True)
    )


STRIP = 128


def strips(tokens, body):
    def step(j, carry):
        body(pl.ds(pl.multiple_of(j * STRIP, STRIP), STRIP))
        return carry

    lax.fori_loop(0, tokens // STRIP, step, 0)


def norm_kernel(hidden_ref, gain_ref, shift_ref, down_ref, low_ref, next_ref):
    def body(at):
        unit, _ = unit_of(hidden_ref[at, :])
        normed = unit * gain_ref[0:1, :] + shift_ref[0:1, :]
        low_ref[at, :] = normed.astype(bfloat)
        next_ref[at, :] = normed + down_ref[...]

    strips(hidden_ref.shape[0], body)


def feed_kernel(normed_ref, into_ref, bias_ref, down_ref, start_ref, act_ref, slope_ref, hidden_ref):
    hidden_units = into_ref.shape[1]
    tile = 256

    def step(j, carry):
        at = pl.ds(pl.multiple_of(j * tile, tile), tile)
        for k in range(2):
            strip = pl.ds(k * 256, 256)
            pre = dot(normed_ref[strip, :], into_ref[:, at]) + bias_ref[:, at]
            bell = jnp.exp(-0.5 * pre * pre)
            reach = 1.0 / (1.0 + 0.23164189 * jnp.abs(pre))
            tail = reach * (
                0.127414796
                + reach * (-0.142248368 + reach * (0.7107068705 + reach * (-0.7265760135 + reach * 0.5307027145)))
            )
            tail = tail * bell
            chance = jnp.where(pre >= 0, 1.0 - tail, tail)
            act_ref[strip, at] = (pre * chance).astype(bfloat)
            slope_ref[strip, at] = (chance + pre * bell * 0.3989422804014327).astype(bfloat)
        return carry

    lax.fori_loop(0, hidden_units // tile, step, 0)
    hidden_ref[...] = start_ref[...] + dot(act_ref[...], down_ref[...])


def feed(order, normed, into, bias, down, start):
    tokens, width = normed.shape
    units = into.shape[1]
    return order.call(
        feed_kernel,
        [shaped((tokens, units), bfloat), shaped((tokens, units), bfloat), shaped((tokens, width), single)],
        normed,
        into,
        bias,
        down,
        start,
        cost=6.0,
    )


def add_columns(ref, row, value):
    ref[row : row + 1, :] += jnp.sum(value, axis=0, keepdims=True)


def turn_kernel(hidden_ref, gain_ref, upstream_ref, grad_ref, sums_ref, unit_ref, branch_ref):
    sums_ref[...] = jnp.zeros_like(sums_ref)

    def body(at):
        unit, scale = unit_of(hidden_ref[at, :])
        gain = gain_ref[1:2, :]
        upstream = upstream_ref[at, :].astype(single)
        unit_ref[at, :] = unit
        grad = norm_back(upstream, unit, scale, gain)
        grad_ref[at, :] = grad
        branch_ref[at, :] = grad.astype(bfloat)
        add_columns(sums_ref, 0, upstream * unit)
        add_columns(sums_ref, 1, upstream)
        add_columns(sums_ref, 2, grad)

    strips(hidden_ref.shape[0], body)


def feed_back_kernel(branch_ref, down_ref, slope_ref, into_ref, start_ref, grad_ref, sums_ref, normed_ref):
    hidden_units = into_ref.shape[1]
    tile = 256

    def step(j, carry):
        at = pl.ds(pl.multiple_of(j * tile, tile), tile)
        pre = dot_cols(branch_ref[...], down_ref[at, :]) * slope_ref[:, at].astype(single)
        low = pre.astype(bfloat)
        grad_ref[:, at] = low
        sums_ref[:, at] = jnp.sum(low.astype(single), axis=0, keepdims=True)
        return carry

    lax.fori_loop(0, hidden_units // tile, step, 0)
    normed_ref[...] = start_ref[...] + dot_cols(grad_ref[...], into_ref[...])


def feed_back(order, branch, down, slope, into, start):
    tokens, width = branch.shape
    units = into.shape[1]
    return order.call(
        feed_back_kernel,
        [shaped((tokens, units), bfloat), shaped((1, units), single), shaped((tokens, width), single)],
        branch,
        down,
        slope,
        into,
        start,
        cost=3.9,
    )


def norm_back_kernel(hidden_ref, gain_ref, upstream_ref, grad_ref, sums_ref, low_ref):
    sums_ref[...] = jnp.zeros_like(sums_ref)

    def body(at):
        unit, scale = unit_of(hidden_ref[at, :])
        upstream = upstream_ref[at, :]
        grad = norm_back(upstream, unit, scale, gain_ref[0:1, :])
        grad_ref[at, :] = grad
        low_ref[at, :] = grad.astype(bfloat)
        add_columns(sums_ref, 0, upstream * unit)
        add_columns(sums_ref, 1, upstream)
        add_columns(sums_ref, 2, grad)

    strips(hidden_ref.shape[0], body)


def attend_back_kernel(upstream_ref, parts_ref, chance_ref, qkv_ref, start_ref, *refs):
    *out_w, grad_ref, sums_ref, rows_ref, turned_ref = refs
    tokens = upstream_ref.shape[0]
    local = qkv_ref.shape[2]
    middle = upstream_ref.shape[1] // 2
    tile = 256
    factor = HEAD_DIM**-0.5

    def pair_step(pair, carry):
        at = pl.multiple_of(pair * PAIR, PAIR)
        lanes = pl.ds(at, PAIR)
        queries = parts_ref[0, :, lanes]
        keys_turned = parts_ref[1, :, lanes].T
        values = parts_ref[2, :, lanes]
        if out_w:
            grad_context = dot_cols(upstream_ref[...], out_w[0][lanes, :])
        else:
            grad_context = dot_cols(upstream_ref[:, :middle], qkv_ref[3, lanes, :])
            grad_context = grad_context + dot_cols(
                upstream_ref[:, middle:], qkv_ref[3, pl.ds(pl.multiple_of(local + at, PAIR), PAIR), :]
            )
        grad_context = grad_context.astype(bfloat)
        context_turned = grad_context.T
        owner = lax.broadcasted_iota(jnp.int32, (PAIR, tile), 0) // HEAD_DIM
        first_lane = lax.broadcasted_iota(jnp.int32, (tokens, PAIR), 1) < HEAD_DIM
        grads_k, grads_v = [], []
        for h in range(2):
            key_rows = keys_turned[h * HEAD_DIM : (h + 1) * HEAD_DIM]
            grad_k = jnp.zeros((tokens, PAIR), single)
            grad_v = jnp.zeros((tokens, PAIR), single)
            for q in range(tokens // tile):
                cut = slice(q * tile, (q + 1) * tile)
                picked = context_turned[:, cut]
                picked = jnp.where(owner == h, picked, jnp.zeros_like(picked))
                chances_low = chance_ref[pair * 2 + h, :, cut]
                chances = chances_low.astype(single)
                grad_chances = dot(values, picked)
                inner = jnp.sum(chances * grad_chances, axis=0, keepdims=True)
                grad_scores = (chances * (grad_chances - inner)).astype(bfloat)
                grad_v = grad_v + dot(chances_low, grad_context[cut, :])
                grad_k = grad_k + dot(grad_scores, queries[cut, :])
                turned_ref[pl.ds(pl.multiple_of(at + h * HEAD_DIM, HEAD_DIM), HEAD_DIM), cut] = (dot(key_rows, grad_scores) * factor).astype(bfloat)
            grads_k.append(grad_k)
            grads_v.append(grad_v)
        grad_k = (jnp.where(first_lane, grads_k[0], grads_k[1]) * factor).astype(bfloat)
        grad_v = jnp.where(first_lane, grads_v[0], grads_v[1]).astype(bfloat)
        grad_ref[:, pl.ds(pl.multiple_of(local + at, PAIR), PAIR)] = grad_k
        grad_ref[:, pl.ds(pl.multiple_of(2 * local + at, PAIR), PAIR)] = grad_v
        return carry

    lax.fori_loop(0, local // PAIR, pair_step, 0)
    grad_ref[:, 0:local] = turned_ref[...].T
    sums_ref[...] = jnp.sum(grad_ref[...].astype(single), axis=0, keepdims=True)
    total = start_ref[...]
    for part in range(3):
        total = total + dot_cols(grad_ref[:, part * local : (part + 1) * local], qkv_ref[part])
    rows_ref[...] = total


def attend_back(order, upstream, parts, chances, qkv, start, out=None):
    tokens, width = upstream.shape
    local = qkv.shape[2]
    return order.call(
        attend_back_kernel,
        [shaped((tokens, 3 * local), bfloat), shaped((1, 3 * local), single), shaped((tokens, width), single)],
        upstream,
        parts,
        chances,
        qkv,
        start,
        *([] if out is None else [out]),
        scratch=[pltpu.VMEM((local, tokens), bfloat)],
        cost=9.4,
    )


def vectors_kernel(side_ref, first_ref, second_ref, units_own, units_other, proj_own, proj_other, out_ref):
    width = first_ref.shape[1]
    local = proj_own.shape[1] // 3
    out_ref[...] = jnp.zeros_like(out_ref)
    for k in range(3):
        out_ref[k : k + 1, :width] = first_ref[k : k + 1, :]
        out_ref[k : k + 1, width:] = second_ref[k : k + 1, :]
    swapped = side_ref[0] == 1
    for row, units, proj in (
        (3, (units_own, units_other), (proj_own, proj_other)),
        (5, (units_other, units_own), (proj_other, proj_own)),
    ):
        out_ref[row : row + 1, :] = jnp.where(swapped, units[1][...], units[0][...])
        parts = jnp.where(swapped, proj[1][...], proj[0][...])
        out_ref[row + 1 : row + 2, :local] = parts[:, :local]
        out_ref[row + 1 : row + 2, local : 2 * local] = parts[:, 2 * local :]


def both_result_kernel(side_ref, mine_ref, even_ref, odd_ref, gain_ref, shift_ref, out_ref):
    side = side_ref[0]

    def body(at):
        for place, unit in ((side, mine_ref[at, :]), (1 - side, even_ref[at, :] + odd_ref[at, :])):
            out_ref[place, at, :] = (unit * gain_ref[1:2, :] + shift_ref[1:2, :]).astype(bfloat)

    strips(mine_ref.shape[0], body)


def both_kernel(side_ref, mine_ref, even_ref, odd_ref, out_ref):
    side = side_ref[0]
    out_ref[side] = mine_ref[...]
    out_ref[1 - side] = even_ref[...] + odd_ref[...]


def shares_kernel(rank_ref, qkv_ref, out_ref, left_ref, right_ref, down_ref, bias_ref, units_ref, heads_ref, feed_ref, small_ref):
    heads_ref[0, 0:3] = qkv_ref[...].astype(single)
    heads_ref[0, 3] = out_ref[...].astype(single)
    depth = left_ref.shape[0]
    feed_ref[0:depth, :] = left_ref[...].astype(single)
    feed_ref[depth : 2 * depth, :] = right_ref[...].astype(single)
    feed_ref[2 * depth :, :] = down_ref[...].astype(single)
    local = bias_ref.shape[1]
    small_ref[:, 0:local] = bias_ref[0:1, :]
    small_ref[:, local : 2 * local] = bias_ref[1:2, :]
    small_ref[:, 2 * local :] = units_ref[...]


def shares(rank, qkv, out, into, down, bias, units):
    width, local, hidden = qkv.shape[1], qkv.shape[2], into.shape[1]
    depth = width // 8
    quarters = local // depth
    return pl.pallas_call(
        shares_kernel,
        grid_spec=pltpu.PrefetchScalarGridSpec(
            num_scalar_prefetch=1,
            grid=(1,),
            in_specs=[
                pl.BlockSpec((3, depth, local), lambda j, r: (0, r[0], 0)),
                pl.BlockSpec((depth, local), lambda j, r: (r[0] % quarters, r[0] // quarters)),
                pl.BlockSpec((depth, width), lambda j, r: (r[0], 0)),
                pl.BlockSpec((depth, width), lambda j, r: (r[0], 1)),
                pl.BlockSpec((hidden // 8, width), lambda j, r: (r[0], 0)),
                pl.BlockSpec((2, local), lambda j, r: (0, 0)),
                pl.BlockSpec((1, hidden), lambda j, r: (0, 0)),
            ],
            out_specs=[
                pl.BlockSpec((1, 4, depth, local), lambda j, r: (0, 0, 0, 0)),
                pl.BlockSpec((2 * depth + hidden // 8, width), lambda j, r: (0, 0)),
                pl.BlockSpec((1, 2 * local + hidden), lambda j, r: (0, 0)),
            ],
        ),
        out_shape=[
            shaped((1, 4, depth, local), single),
            shaped((2 * depth + hidden // 8, width), single),
            shaped((1, 2 * local + hidden), single),
        ],
        cost_estimate=pl.CostEstimate(flops=1000, bytes_accessed=1000, transcendentals=0),
    )(rank, qkv, out, into, into, down, bias, units)


def body(
    inputs,
    lengths,
    w_qkv,
    b_qv,
    w_out,
    b_out,
    ln_gains,
    ln_biases,
    w_in,
    b_in,
    w_down,
    b_down,
    cotangent,
):
    size = lax.axis_size("dp")
    me = lax.axis_index("dp")
    side = lax.axis_index("tensor")
    side_index = side.astype(jnp.int32).reshape(1)
    tokens, width = inputs.shape[1:]
    local = w_qkv.shape[2]
    units = w_in.shape[1]
    rows = lax.dynamic_index_in_dim(inputs, side, 0, keepdims=False)
    length = lax.dynamic_slice_in_dim(lengths, side, 1)
    upstream = lax.dynamic_index_in_dim(cotangent, side, 0, keepdims=False)

    order = Order()

    bits = size.bit_length() - 1
    share = width // size
    block_of = jnp.array([reverse_bits(p, bits) for p in range(size)], jnp.int32) ^ me
    source = (block_of[:, None] * share + jnp.arange(share)[None, :]).reshape(-1, 1)

    rank, core = me & 7, me & 1
    core_index = core.astype(jnp.int32).reshape(1)
    qkv_own = jnp.transpose(w_qkv, (1, 0, 2))
    depth = width // 8
    heads_share, feed_share, small_other = shares(
        rank.astype(jnp.int32).reshape(1), qkv_own, w_out, w_in, w_down, b_qv, b_in.reshape(1, -1)
    )
    heads_share = swap_x(heads_share)
    feed_share = swap_x(feed_share)
    small_other = swap_x(small_other)

    heads = []
    parts, chances, context, hidden_one = attend(order, length, rows, qkv_own, b_qv, b_out.reshape(1, -1), w_out)
    heads.append((parts, chances, context))
    small_other = order.pin(small_other)
    b_qv_other, b_in_other = small_other[:, : 2 * local].reshape(2, local), small_other[:, 2 * local :]
    get_heads = Chain(fetch_spread(order, order.pin(heads_share), me, size, 2.0))
    get_heads.step()
    get_heads.step()
    into_share, down_share = order.call(
        unpack_kernel,
        [shaped((1, 2, depth, width), single), shaped((1, 1, units // 8, width), single)],
        feed_share,
        cost=10.0,
    )
    get_in = Chain(fetch_spread(order, into_share, me, size, 8.0))
    get_down = Chain(fetch_spread(order, down_share, me, size, 8.0))
    get_in.step()
    get_down.step()
    rows_rel = relative(order, rows, source)
    get_heads.step()
    get_heads.step()
    get_in.step()
    heads_other = place(order, [get_heads.value], (4, width, local))
    parts, chances, context, hidden_one = attend(order, length, rows, heads_other, b_qv_other, hidden_one)
    heads.append((parts, chances, context))
    get_down.step()
    normed_low, hidden_two = order.call(
        norm_kernel,
        [shaped((tokens, width), bfloat), shaped((tokens, width), single)],
        hidden_one,
        ln_gains,
        ln_biases,
        b_down.reshape(1, -1),
    )
    get_in.step()
    get_in.step()
    acts = []
    act, slope, hidden_two = feed(order, normed_low, w_in, b_in.reshape(1, -1), w_down, hidden_two)
    acts.append((act, slope))
    get_down.step()
    get_down.step()
    normed_rel = relative(order, normed_low, source)
    in_other = place(order, [get_in.value], w_in.shape)
    down_other = place(order, [get_down.value], w_down.shape)
    act, slope, hidden_two = feed(order, normed_low, in_other, b_in_other, down_other, hidden_two)
    acts.append((act, slope))
    grad_two, sums_two, unit_two, branch = order.call(
        turn_kernel,
        [
            shaped((tokens, width), single),
            shaped((3, width), single),
            shaped((tokens, width), single),
            shaped((tokens, width), bfloat),
        ],
        hidden_two,
        ln_gains,
        upstream,
        cost=1.6,
    )

    dims = [1 << k for k in range(1, size.bit_length() - 1)]
    x_and_y = ([None] + dims, dims + [None])
    z_and_y = (dims[1:] + dims[:1] + [None], dims + [None])
    branch_rel = relative(order, branch, source)
    unit_even = swap_x_core(unit_two, 0, size)
    unit_odd = swap_x_core(unit_two, 1, size)
    down = Chain(scatter(order, core_index, [(branch_rel, acts[0][0], acts[1][0])], x_and_y, size))
    down.step()
    pre_other, unit_sum_other, grad_normed = feed_back(order, branch, down_other, acts[1][1], in_other, grad_two)
    down.step()
    pre_own, unit_sum_own, grad_normed = feed_back(order, branch, w_down, acts[0][1], w_in, grad_normed)
    grad_one, sums_one, attended = order.call(
        norm_back_kernel,
        [shaped((tokens, width), single), shaped((3, width), single), shaped((tokens, width), bfloat)],
        hidden_one,
        ln_gains,
        grad_normed,
        cost=1.5,
    )
    attended_rel = relative(order, attended, source)
    unit_even = order.pin(unit_even)
    into = Chain(scatter(order, core_index, [(normed_rel, pre_own, pre_other)], z_and_y, size))
    into.step()
    proj_other, proj_sum_other, grad_rows = attend_back(order, attended, heads[1][0], heads[1][1], heads_other, grad_one)
    into.step()
    proj_own, proj_sum_own, grad_rows = attend_back(order, attended, heads[0][0], heads[0][1], qkv_own, grad_rows, w_out)
    vectors = order.call(
        vectors_kernel,
        shaped((8, 2 * width), single),
        sums_one,
        sums_two,
        unit_sum_own,
        unit_sum_other,
        proj_sum_own,
        proj_sum_other,
        scalars=(side_index,),
        cost=0.5,
    )
    grad_even = swap_x_core(grad_rows, 0, size)
    grad_odd = swap_x_core(grad_rows, 1, size)
    down.step()
    project = Chain(
        scatter(
            order,
            core_index,
            [(attended_rel, heads[0][2], heads[1][2]), (rows_rel, proj_own, proj_other)],
            x_and_y,
            size,
            vectors,
        )
    )
    project.step()
    unit_odd = order.pin(unit_odd)
    into.step()
    project.step()
    down.step()
    results = order.call(
        both_result_kernel,
        shaped((2, tokens, width), bfloat),
        unit_two,
        unit_even,
        unit_odd,
        ln_gains,
        ln_biases,
        scalars=(side_index,),
        cost=1.5,
    )
    into.step()
    project.step()
    down.step()
    grad_even = order.pin(grad_even)
    project.step()
    into.step()
    down.step()
    project.step()
    into.step()
    chains = (project, down, into)
    while any(chain.value is None for chain in chains):
        for chain in chains:
            if chain.value is None:
                chain.step()
    grads = order.call(
        both_kernel,
        shaped((2, tokens, width), single),
        grad_rows,
        grad_even,
        grad_odd,
        scalars=(side_index,),
        cost=2.0,
    )
    share_in = into.value[0]
    share_project, sums = project.value
    share_out, share_qkv = share_project[:, :local], share_project[:, local:]
    mine = jnp.where(side == 0, sums[3:5], sums[5:7])
    first_sums, second_sums = sums[:3, :width], sums[:3, width:]
    return (
        results,
        grads,
        share_qkv.reshape(-1, 3, local),
        mine[1, : 2 * local].reshape(2, local),
        share_out.T,
        first_sums[2],
        jnp.stack([first_sums[0], second_sums[0]]),
        jnp.stack([first_sums[1], second_sums[1]]),
        share_in,
        mine[0],
        down.value[0].T,
        second_sums[2],
    )


def solution(mesh):
    placed = (
        P("dp", None, None),
        P("dp"),
        P(None, None, "tensor"),
        P(None, "tensor"),
        P("tensor", None),
        P(),
        P(),
        P(),
        P(None, "tensor"),
        P("tensor"),
        P("tensor", None),
        P(),
        P("dp", None, None),
    )
    return jax.shard_map(
        body,
        mesh=mesh,
        in_specs=placed,
        out_specs=(
            P("dp", None, None),
            P("dp", None, None),
            P("dp", None, "tensor"),
            P(None, "tensor"),
            P("tensor", "dp"),
            P(),
            P(),
            P(),
            P("dp", "tensor"),
            P("tensor"),
            P("tensor", "dp"),
            P(),
        ),
        check_vma=False,
    )
```

```python
import functools

import jax
import jax.numpy as jnp
from jax import lax
from jax.experimental import pallas as pl
from jax.experimental.pallas import tpu as pltpu
from jax.sharding import PartitionSpec as P

HEAD_DIM = 64
PAIR = 2 * HEAD_DIM
norm_eps = 1e-12
bfloat = jnp.bfloat16
single = jnp.float32
MIB = 1 << 20
COST_UNIT = 1.0e9


def dot(left, right):
    return jnp.dot(left, right, preferred_element_type=single)


def dot_cols(left, right):
    return lax.dot_general(
        left, right, (((1,), (1,)), ((), ())), preferred_element_type=single
    )


def shaped(shape, dtype):
    return jax.ShapeDtypeStruct(shape, dtype)


def nothing_kernel(out_ref):
    out_ref[...] = jnp.zeros_like(out_ref)


class Order:
    def __init__(self):
        self.last = None

    def call(self, kernel, outs, *args, scalars=(), scratch=(), grid=(), in_specs=None, out_specs=None, limit=20, aliases=None, cost=1.0, name=None):
        many = isinstance(outs, (tuple, list))
        if in_specs is None:
            in_specs = [pl.BlockSpec(memory_space=pltpu.VMEM)] * len(args)
        if out_specs is None:
            out_specs = [pl.BlockSpec(memory_space=pltpu.VMEM)] * len(outs) if many else pl.BlockSpec(memory_space=pltpu.VMEM)
        in_specs = [pl.BlockSpec(memory_space=pltpu.SMEM)] * len(scalars) + list(in_specs)
        operands = list(scalars) + list(args)
        run = kernel
        if self.last is not None:
            before = len(operands)
            operands.append(self.last)
            in_specs.append(pl.BlockSpec(memory_space=pl.ANY))

            def run(*refs):
                kernel(*refs[:before], *refs[before + 1 :])

        made = pl.pallas_call(
            run,
            out_shape=outs,
            grid=grid,
            in_specs=in_specs,
            out_specs=out_specs,
            scratch_shapes=list(scratch),
            name=name or kernel.__name__,
            input_output_aliases=aliases or {},
            compiler_params=pltpu.CompilerParams(vmem_limit_bytes=limit * MIB),
            cost_estimate=pl.CostEstimate(flops=int(cost * COST_UNIT), bytes_accessed=1000, transcendentals=0),
        )(*operands)
        self.last = made[-1] if many else made
        return made

    def pad(self, cost):
        self.call(nothing_kernel, shaped((8, 128), single), cost=cost)

    def pin(self, value):
        return self.call(
            lambda *refs: None,
            shaped(value.shape, value.dtype),
            value,
            in_specs=[pl.BlockSpec(memory_space=pl.ANY)],
            out_specs=pl.BlockSpec(memory_space=pl.ANY),
            aliases={0: 0},
            cost=0.0,
            name="pin_kernel",
        )


class Chain:
    def __init__(self, steps):
        self.steps = steps
        self.value = None

    def step(self):
        self.value = next(self.steps, self.value)
        return self.value

    def run(self, count):
        for _ in range(count):
            self.step()


def swap_dp(value, mask, size):
    return lax.ppermute(value, "dp", [(i, i ^ mask) for i in range(size)])


def swap_x(value):
    return lax.ppermute(value, "tensor", [(0, 1), (1, 0)])


def reverse_bits(position, bits):
    out = 0
    for k in range(bits):
        out |= ((position >> k) & 1) << (bits - 1 - k)
    return out


def place_kernel(groups, rows, order_ref, *refs):
    out_ref = refs[-1]
    at = 0
    for piece, count in zip(refs[:-1], groups):
        for b in range(count):
            start = pl.multiple_of(order_ref[at], 16)
            height = rows[at]
            for c in range(piece.shape[1]):
                if out_ref.ndim == 3:
                    out_ref[c, pl.ds(start, height), :] = piece[b, c].astype(out_ref.dtype)
                else:
                    lanes = slice(c * piece.shape[3], (c + 1) * piece.shape[3])
                    out_ref[pl.ds(start, height), lanes] = piece[b, c].astype(out_ref.dtype)
            at += 1


def place(order, parts, shape):
    pieces, rows, starts = [], [], []
    for held, begin in parts:
        pieces += held
        starts.append(begin)
        rows += [held[0].shape[-2]] * begin.shape[0]
    groups = tuple(piece.shape[0] for piece in pieces)
    kernel = functools.partial(place_kernel, groups, tuple(rows))
    return order.call(kernel, shaped(shape, bfloat), *pieces, scalars=(jnp.concatenate(starts).astype(jnp.int32),), cost=2.4, name="place_kernel")


def pack_kernel(first_ref, second_ref, out_ref):
    out_ref[0] = first_ref[0]
    out_ref[1] = second_ref[0]


def swap_mixed(value, first, second, size):
    pairs = []
    for d in range(size):
        mask = second if d & 1 else first
        for t in range(2):
            to = (d, 1 - t) if mask is None else (d ^ mask, t)
            pairs.append((2 * d + t, 2 * to[0] + to[1]))
    return lax.ppermute(value, ("dp", "tensor"), pairs)


def fetch_spread(order, held, me, size, pack_cost):
    rank = me & 7
    core = me & 1
    arrived = swap_mixed(held, 4, 2, size)
    yield
    both = order.call(pack_kernel, shaped((2,) + held.shape[1:], single), held, arrived, cost=pack_cost)
    arrived = swap_mixed(both, 2, 4, size)
    both_core = swap_dp(both, 1, size)
    yield
    both_core = order.pin(both_core)
    yield
    arrived = order.pin(arrived)
    arrived_core = swap_dp(arrived, 1, size)
    even, odd = jnp.array([0, 4, 2, 6], jnp.int32), jnp.array([0, 2, 4, 6], jnp.int32)
    mine = rank ^ jnp.where(core == 0, even, odd)
    sibling = rank ^ 1 ^ jnp.where(core == 0, odd, even)
    yield [both, arrived, both_core, arrived_core], jnp.concatenate([mine, sibling]) * held.shape[-2]


def unpack_kernel(all_ref, into_ref, down_ref):
    rows = into_ref.shape[2]
    for c in range(2):
        into_ref[0, c] = all_ref[c * rows : (c + 1) * rows, :]
    down_ref[0, 0] = all_ref[2 * rows :, :]


def product_kernel(groups, cuts, places, extras, core_ref, *refs):
    lefts, rights = refs[: len(groups)], refs[len(groups) : 3 * len(groups)]
    rest = refs[3 * len(groups) :]
    tile = pl.program_id(0)
    first = core_ref[0] == 0

    def spread(side, total, low_ref, high_ref, table, height):
        half = len(table[0])
        for block in range(half):
            at = table[side][block]
            out_ref, at = (low_ref, at) if at < half else (high_ref, at - half)
            out_ref[at * height : (at + 1) * height, :] = total[block * height : (block + 1) * height]

    def run(k, j):
        for side in range(2):
            total = dot(lefts[k][...], rights[2 * k + side][...])
            cut = j * cuts // sum(groups)
            if places is None:
                rest[cut][side] = total
                continue
            total = total + rest[cut][side]
            low_ref, high_ref = rest[cuts + extras :][:2]
            even, odd, height = places
            pl.when(first)(lambda: spread(side, total, low_ref, high_ref, even, height))
            pl.when(jnp.logical_not(first))(lambda: spread(side, total, low_ref, high_ref, odd, height))

    j = 0
    for k, tiles in enumerate(groups):
        for _ in range(tiles):
            pl.when(tile == j)(functools.partial(run, k, j))
            j += 1
    if extras:
        total = rest[cuts][...] + rest[cuts + 1][...]
        low_ref, high_ref, extra_ref = rest[cuts + 2 :]
        extra_ref[...] = total
        high_ref[low_ref.shape[0] :, :] = total


TILE = 384


def product(order, core, half, terms, cuts, added=(), places=None, extras=()):
    rows = terms[0][0].shape[0] // 2
    tokens = terms[0][0].shape[1]
    groups = tuple(term[1].shape[1] // TILE for term in terms)
    begins = [sum(groups[:k]) for k in range(len(groups))]
    tiles = sum(groups)

    def right_spec(k):
        return pl.BlockSpec((tokens, TILE), lambda j: (0, jnp.clip(j - begins[k], 0, groups[k] - 1)))

    def tall(height):
        return shaped((height, tiles * TILE), single), pl.BlockSpec((height, TILE), lambda j: (0, j))

    each = tiles // cuts
    pieces = [
        pl.BlockSpec((2, rows, TILE), lambda j, k=k: (0, 0, jnp.clip(j - k * each, 0, each - 1)))
        for k in range(cuts)
    ]
    if places is None:
        outs, out_specs = [shaped((2, rows, each * TILE), single)] * cuts, pieces
    else:
        height = len(places[0][0]) * places[2]
        heights = [height, height] + [part.shape[0] for part in extras[:1]]
        if extras:
            heights[1] += heights[2]
        outs, out_specs = zip(*[tall(height) for height in heights])
    return order.call(
        functools.partial(product_kernel, groups, cuts, places, len(extras)),
        list(outs),
        *[term[0] for term in terms],
        *[side for term in terms for side in term[1:3]],
        *added,
        *extras,
        scalars=(core,),
        grid=(tiles,),
        in_specs=[
            *[pl.BlockSpec((rows, tokens), lambda j: (half, 0)) for _ in terms],
            *[right_spec(k) for k in range(len(terms)) for _ in range(2)],
            *(pieces if added else []),
            *[tall(part.shape[0])[1] for part in extras],
        ],
        out_specs=list(out_specs),
        cost=tiles * 0.8 if places is None else tiles * 1.2,
        name="send_kernel" if places is None else "keep_kernel",
    )


def sum_kernel(whole, low_ref, arrived_ref, *refs):
    rows = low_ref.shape[0]
    extra = refs[0][...] + arrived_ref[rows:, :] if arrived_ref.shape[0] > rows else None
    outs = refs if extra is None else refs[1:]
    if whole:
        outs[0][...] = low_ref[...] + arrived_ref[:rows, :]
    else:
        half = rows // 2
        outs[0][...] = low_ref[:half, :] + arrived_ref[:half, :]
        outs[1][:half, :] = low_ref[half:, :] + arrived_ref[half:rows, :]
    if extra is not None:
        outs[-1][...] = extra
        if not whole:
            outs[1][rows // 2 :, :] = extra


def add_arrived(order, low, arrived, extra, whole):
    rows, width = low.shape
    beyond = arrived.shape[0] - rows
    heights = [rows] if whole else [rows // 2, rows // 2 + beyond]
    heights += [beyond] if beyond else []
    outs = order.call(
        functools.partial(sum_kernel, whole),
        [shaped((height, width), single) for height in heights],
        low,
        arrived,
        *([extra] if beyond else []),
        cost=0.7,
        name="add_kernel",
    )
    return outs if beyond else [*outs, None]


def scatter(order, core, terms, cuts, orders, size, extra=None):
    masks = [1 << k for k in range(1, size.bit_length() - 1)]
    count = len(masks)

    def place_of(side, block, dims):
        at = 0
        for dim in dims:
            bit = side if dim is None else (block >> (count - 1 - masks.index(dim))) & 1
            at = 2 * at + bit
        return at

    tables = [
        [[place_of(side, block, dims) for block in range(1 << count)] for side in range(2)]
        for dims in orders
    ]
    sent = product(order, core, 1, terms, cuts)
    arrived = [swap_dp(part, 1, size) for part in sent]
    extras = () if extra is None else (extra, swap_dp(extra, 1, size))
    yield
    height = terms[0][0].shape[0] // size
    low, high, *extra = product(order, core, 0, terms, cuts, arrived, (*tables, height), extras)
    extra = extra[0] if extras else None
    for k in range(count + 1):
        arrived = swap_mixed(high, orders[0][k], orders[1][k], size)
        yield
        if k < count:
            low, high, extra = add_arrived(order, low, arrived, extra, False)
    total, extra = add_arrived(order, low, arrived, extra, True)
    yield (total, extra)


def relative_kernel(value_ref, source_ref, out_ref):
    depth = value_ref.shape[1]
    tile = depth // 4

    def step(j, carry):
        at = pl.multiple_of(j * tile, 16)
        lanes = lax.broadcasted_iota(jnp.int32, (tile, depth), 1)
        picks = jnp.where(lanes == source_ref[pl.ds(at, tile), :], 1.0, 0.0).astype(bfloat)
        out_ref[pl.ds(at, tile), :] = dot_cols(picks, value_ref[...]).astype(bfloat)
        return carry

    lax.fori_loop(0, 4, step, 0)


def relative(order, value, source):
    return order.call(relative_kernel, shaped(value.shape[::-1], bfloat), value, source, cost=1.7)


def attend_kernel(length_ref, rows_ref, qkv_ref, bias_ref, start_ref, *refs):
    *out_w, parts_ref, chance_ref, context_ref, hidden_ref, turned_ref = refs
    tokens = rows_ref.shape[0]
    local = qkv_ref.shape[2]
    rows = rows_ref[...]
    for part in range(3):
        projected = dot(rows, qkv_ref[part])
        if part == 0:
            projected = projected + bias_ref[0:1, :]
        elif part == 2:
            projected = projected + bias_ref[1:2, :]
        parts_ref[part] = projected.astype(bfloat)
    tile = 256
    visible = lax.broadcasted_iota(jnp.int32, (tokens, tile), 0) < length_ref[0]

    def pair_step(pair, carry):
        at = pl.multiple_of(pair * PAIR, PAIR)
        keys = parts_ref[1, :, pl.ds(at, PAIR)]
        queries = parts_ref[0, :, pl.ds(at, PAIR)].T
        values = parts_ref[2, :, pl.ds(at, PAIR)].T
        owner = lax.broadcasted_iota(jnp.int32, (PAIR, tile), 0) // HEAD_DIM
        for h in range(2):
            value_rows = values[h * HEAD_DIM : (h + 1) * HEAD_DIM]
            for q in range(tokens // tile):
                picked = queries[:, q * tile : (q + 1) * tile] * HEAD_DIM**-0.5
                picked = jnp.where(owner == h, picked, jnp.zeros_like(picked))
                scores = jnp.where(visible, dot(keys, picked), -1e9)
                raised = jnp.exp(scores - jnp.max(scores, axis=0, keepdims=True))
                chances = raised * (1.0 / jnp.sum(raised, axis=0, keepdims=True))
                chances = chances.astype(bfloat)
                chance_ref[pair * 2 + h, :, q * tile : (q + 1) * tile] = chances
                turned_ref[pl.ds(pl.multiple_of(at + h * HEAD_DIM, HEAD_DIM), HEAD_DIM), q * tile : (q + 1) * tile] = dot(value_rows, chances).astype(bfloat)
        return carry

    lax.fori_loop(0, local // PAIR, pair_step, 0)
    context = turned_ref[...].T
    context_ref[...] = context
    if out_w:
        hidden_ref[...] = rows_ref[...].astype(single) + start_ref[...] + dot(context, out_w[0][...])
    else:
        middle = hidden_ref.shape[1] // 2
        hidden_ref[:, :middle] = start_ref[:, :middle] + dot(context, qkv_ref[3, :local, :])
        hidden_ref[:, middle:] = start_ref[:, middle:] + dot(context, qkv_ref[3, local:, :])


def attend(order, length, rows, qkv, bias, start, out=None):
    tokens, width = rows.shape
    local = qkv.shape[2]
    return order.call(
        attend_kernel,
        [
            shaped((3, tokens, local), bfloat),
            shaped((local // HEAD_DIM, tokens, tokens), bfloat),
            shaped((tokens, local), bfloat),
            shaped((tokens, width), single),
        ],
        rows,
        qkv,
        bias,
        start,
        *([] if out is None else [out]),
        scalars=(length,),
        scratch=[pltpu.VMEM((local, tokens), bfloat)],
        cost=9.0,
    )


def unit_of(hidden):
    centred = hidden - jnp.mean(hidden, axis=-1, keepdims=True)
    scale = lax.rsqrt(jnp.mean(centred * centred, axis=-1, keepdims=True) + norm_eps)
    return centred * scale, scale


def norm_back(upstream, unit, scale, gain):
    scaled = upstream * gain
    return scale * (
        scaled
        - jnp.mean(scaled, axis=-1, keepdims=True)
        - unit * jnp.mean(scaled * unit, axis=-1, keepdims=True)
    )


STRIP = 128


def strips(tokens, body):
    def step(j, carry):
        body(pl.ds(pl.multiple_of(j * STRIP, STRIP), STRIP))
        return carry

    lax.fori_loop(0, tokens // STRIP, step, 0)


def norm_kernel(hidden_ref, gain_ref, shift_ref, down_ref, low_ref, next_ref):
    def body(at):
        unit, _ = unit_of(hidden_ref[at, :])
        normed = unit * gain_ref[0:1, :] + shift_ref[0:1, :]
        low_ref[at, :] = normed.astype(bfloat)
        next_ref[at, :] = normed + down_ref[...]

    strips(hidden_ref.shape[0], body)


def feed_kernel(normed_ref, into_ref, bias_ref, down_ref, start_ref, act_ref, slope_ref, hidden_ref):
    hidden_units = into_ref.shape[1]
    tile = 256

    def step(j, carry):
        at = pl.ds(pl.multiple_of(j * tile, tile), tile)
        for k in range(2):
            strip = pl.ds(k * 256, 256)
            pre = dot(normed_ref[strip, :], into_ref[:, at]) + bias_ref[:, at]
            bell = jnp.exp(-0.5 * pre * pre)
            reach = 1.0 / (1.0 + 0.23164189 * jnp.abs(pre))
            tail = reach * (
                0.127414796
                + reach * (-0.142248368 + reach * (0.7107068705 + reach * (-0.7265760135 + reach * 0.5307027145)))
            )
            tail = tail * bell
            chance = jnp.where(pre >= 0, 1.0 - tail, tail)
            act_ref[strip, at] = (pre * chance).astype(bfloat)
            slope_ref[strip, at] = (chance + pre * bell * 0.3989422804014327).astype(bfloat)
        return carry

    lax.fori_loop(0, hidden_units // tile, step, 0)
    hidden_ref[...] = start_ref[...] + dot(act_ref[...], down_ref[...])


def feed(order, normed, into, bias, down, start):
    tokens, width = normed.shape
    units = into.shape[1]
    return order.call(
        feed_kernel,
        [shaped((tokens, units), bfloat), shaped((tokens, units), bfloat), shaped((tokens, width), single)],
        normed,
        into,
        bias,
        down,
        start,
        cost=6.0,
    )


def add_columns(ref, row, value):
    ref[row : row + 1, :] += jnp.sum(value, axis=0, keepdims=True)


def turn_kernel(hidden_ref, gain_ref, upstream_ref, grad_ref, sums_ref, unit_ref, branch_ref):
    sums_ref[...] = jnp.zeros_like(sums_ref)

    def body(at):
        unit, scale = unit_of(hidden_ref[at, :])
        gain = gain_ref[1:2, :]
        upstream = upstream_ref[at, :].astype(single)
        unit_ref[at, :] = unit
        grad = norm_back(upstream, unit, scale, gain)
        grad_ref[at, :] = grad
        branch_ref[at, :] = grad.astype(bfloat)
        add_columns(sums_ref, 0, upstream * unit)
        add_columns(sums_ref, 1, upstream)
        add_columns(sums_ref, 2, grad)

    strips(hidden_ref.shape[0], body)


def feed_back_kernel(branch_ref, down_ref, slope_ref, into_ref, start_ref, grad_ref, sums_ref, normed_ref):
    hidden_units = into_ref.shape[1]
    tile = 256

    def step(j, carry):
        at = pl.ds(pl.multiple_of(j * tile, tile), tile)
        pre = dot_cols(branch_ref[...], down_ref[at, :]) * slope_ref[:, at].astype(single)
        low = pre.astype(bfloat)
        grad_ref[:, at] = low
        sums_ref[:, at] = jnp.sum(low.astype(single), axis=0, keepdims=True)
        return carry

    lax.fori_loop(0, hidden_units // tile, step, 0)
    normed_ref[...] = start_ref[...] + dot_cols(grad_ref[...], into_ref[...])


def feed_back(order, branch, down, slope, into, start):
    tokens, width = branch.shape
    units = into.shape[1]
    return order.call(
        feed_back_kernel,
        [shaped((tokens, units), bfloat), shaped((1, units), single), shaped((tokens, width), single)],
        branch,
        down,
        slope,
        into,
        start,
        cost=3.9,
    )


def norm_back_kernel(hidden_ref, gain_ref, upstream_ref, grad_ref, sums_ref, low_ref):
    sums_ref[...] = jnp.zeros_like(sums_ref)

    def body(at):
        unit, scale = unit_of(hidden_ref[at, :])
        upstream = upstream_ref[at, :]
        grad = norm_back(upstream, unit, scale, gain_ref[0:1, :])
        grad_ref[at, :] = grad
        low_ref[at, :] = grad.astype(bfloat)
        add_columns(sums_ref, 0, upstream * unit)
        add_columns(sums_ref, 1, upstream)
        add_columns(sums_ref, 2, grad)

    strips(hidden_ref.shape[0], body)


def attend_back_kernel(upstream_ref, parts_ref, chance_ref, qkv_ref, start_ref, *refs):
    *out_w, grad_ref, sums_ref, rows_ref, turned_ref = refs
    tokens = upstream_ref.shape[0]
    local = qkv_ref.shape[2]
    middle = upstream_ref.shape[1] // 2
    tile = 256
    factor = HEAD_DIM**-0.5

    def pair_step(pair, carry):
        at = pl.multiple_of(pair * PAIR, PAIR)
        lanes = pl.ds(at, PAIR)
        queries = parts_ref[0, :, lanes]
        keys_turned = parts_ref[1, :, lanes].T
        values = parts_ref[2, :, lanes]
        if out_w:
            grad_context = dot_cols(upstream_ref[...], out_w[0][lanes, :])
        else:
            grad_context = dot_cols(upstream_ref[:, :middle], qkv_ref[3, lanes, :])
            grad_context = grad_context + dot_cols(
                upstream_ref[:, middle:], qkv_ref[3, pl.ds(pl.multiple_of(local + at, PAIR), PAIR), :]
            )
        grad_context = grad_context.astype(bfloat)
        context_turned = grad_context.T
        owner = lax.broadcasted_iota(jnp.int32, (PAIR, tile), 0) // HEAD_DIM
        first_lane = lax.broadcasted_iota(jnp.int32, (tokens, PAIR), 1) < HEAD_DIM
        grads_k, grads_v = [], []
        for h in range(2):
            key_rows = keys_turned[h * HEAD_DIM : (h + 1) * HEAD_DIM]
            grad_k = jnp.zeros((tokens, PAIR), single)
            grad_v = jnp.zeros((tokens, PAIR), single)
            for q in range(tokens // tile):
                cut = slice(q * tile, (q + 1) * tile)
                picked = context_turned[:, cut]
                picked = jnp.where(owner == h, picked, jnp.zeros_like(picked))
                chances_low = chance_ref[pair * 2 + h, :, cut]
                chances = chances_low.astype(single)
                grad_chances = dot(values, picked)
                inner = jnp.sum(chances * grad_chances, axis=0, keepdims=True)
                grad_scores = (chances * (grad_chances - inner)).astype(bfloat)
                grad_v = grad_v + dot(chances_low, grad_context[cut, :])
                grad_k = grad_k + dot(grad_scores, queries[cut, :])
                turned_ref[pl.ds(pl.multiple_of(at + h * HEAD_DIM, HEAD_DIM), HEAD_DIM), cut] = (dot(key_rows, grad_scores) * factor).astype(bfloat)
            grads_k.append(grad_k)
            grads_v.append(grad_v)
        grad_k = (jnp.where(first_lane, grads_k[0], grads_k[1]) * factor).astype(bfloat)
        grad_v = jnp.where(first_lane, grads_v[0], grads_v[1]).astype(bfloat)
        grad_ref[:, pl.ds(pl.multiple_of(local + at, PAIR), PAIR)] = grad_k
        grad_ref[:, pl.ds(pl.multiple_of(2 * local + at, PAIR), PAIR)] = grad_v
        return carry

    lax.fori_loop(0, local // PAIR, pair_step, 0)
    grad_ref[:, 0:local] = turned_ref[...].T
    sums_ref[...] = jnp.sum(grad_ref[...].astype(single), axis=0, keepdims=True)
    total = start_ref[...]
    for part in range(3):
        total = total + dot_cols(grad_ref[:, part * local : (part + 1) * local], qkv_ref[part])
    rows_ref[...] = total


def attend_back(order, upstream, parts, chances, qkv, start, out=None):
    tokens, width = upstream.shape
    local = qkv.shape[2]
    return order.call(
        attend_back_kernel,
        [shaped((tokens, 3 * local), bfloat), shaped((1, 3 * local), single), shaped((tokens, width), single)],
        upstream,
        parts,
        chances,
        qkv,
        start,
        *([] if out is None else [out]),
        scratch=[pltpu.VMEM((local, tokens), bfloat)],
        cost=9.4,
    )


def vectors_kernel(side_ref, first_ref, second_ref, units_own, units_other, proj_own, proj_other, out_ref):
    width = first_ref.shape[1]
    local = proj_own.shape[1] // 3
    out_ref[...] = jnp.zeros_like(out_ref)
    for k in range(3):
        out_ref[k : k + 1, :width] = first_ref[k : k + 1, :]
        out_ref[k : k + 1, width:] = second_ref[k : k + 1, :]
    swapped = side_ref[0] == 1
    for row, units, proj in (
        (3, (units_own, units_other), (proj_own, proj_other)),
        (5, (units_other, units_own), (proj_other, proj_own)),
    ):
        out_ref[row : row + 1, :] = jnp.where(swapped, units[1][...], units[0][...])
        parts = jnp.where(swapped, proj[1][...], proj[0][...])
        out_ref[row + 1 : row + 2, :local] = parts[:, :local]
        out_ref[row + 1 : row + 2, local : 2 * local] = parts[:, 2 * local :]


def both_result_kernel(side_ref, mine_ref, other_ref, gain_ref, shift_ref, out_ref):
    side = side_ref[0]

    def body(at):
        for place, ref in ((side, mine_ref), (1 - side, other_ref)):
            out_ref[place, at, :] = (ref[at, :] * gain_ref[1:2, :] + shift_ref[1:2, :]).astype(bfloat)

    strips(mine_ref.shape[0], body)


def both_kernel(side_ref, mine_ref, other_ref, out_ref):
    side = side_ref[0]
    out_ref[side] = mine_ref[...]
    out_ref[1 - side] = other_ref[...]


def shares_kernel(rank_ref, qkv_ref, out_ref, left_ref, right_ref, down_ref, bias_ref, units_ref, heads_ref, feed_ref, small_ref):
    heads_ref[0, 0:3] = qkv_ref[...].astype(single)
    heads_ref[0, 3] = out_ref[...].astype(single)
    depth = left_ref.shape[0]
    feed_ref[0:depth, :] = left_ref[...].astype(single)
    feed_ref[depth : 2 * depth, :] = right_ref[...].astype(single)
    feed_ref[2 * depth :, :] = down_ref[...].astype(single)
    local = bias_ref.shape[1]
    small_ref[:, 0:local] = bias_ref[0:1, :]
    small_ref[:, local : 2 * local] = bias_ref[1:2, :]
    small_ref[:, 2 * local :] = units_ref[...]


def shares(rank, qkv, out, into, down, bias, units):
    width, local, hidden = qkv.shape[1], qkv.shape[2], into.shape[1]
    depth = width // 8
    quarters = local // depth
    return pl.pallas_call(
        shares_kernel,
        grid_spec=pltpu.PrefetchScalarGridSpec(
            num_scalar_prefetch=1,
            grid=(1,),
            in_specs=[
                pl.BlockSpec((3, depth, local), lambda j, r: (0, r[0], 0)),
                pl.BlockSpec((depth, local), lambda j, r: (r[0] % quarters, r[0] // quarters)),
                pl.BlockSpec((depth, width), lambda j, r: (r[0], 0)),
                pl.BlockSpec((depth, width), lambda j, r: (r[0], 1)),
                pl.BlockSpec((hidden // 8, width), lambda j, r: (r[0], 0)),
                pl.BlockSpec((2, local), lambda j, r: (0, 0)),
                pl.BlockSpec((1, hidden), lambda j, r: (0, 0)),
            ],
            out_specs=[
                pl.BlockSpec((1, 4, depth, local), lambda j, r: (0, 0, 0, 0)),
                pl.BlockSpec((2 * depth + hidden // 8, width), lambda j, r: (0, 0)),
                pl.BlockSpec((1, 2 * local + hidden), lambda j, r: (0, 0)),
            ],
        ),
        out_shape=[
            shaped((1, 4, depth, local), single),
            shaped((2 * depth + hidden // 8, width), single),
            shaped((1, 2 * local + hidden), single),
        ],
        cost_estimate=pl.CostEstimate(flops=1000, bytes_accessed=1000, transcendentals=0),
    )(rank, qkv, out, into, into, down, bias, units)


SCHEDULE = [8.0, 2.0, "ao", "tH", "H", "tF", "rr", "H", "H", "sm", "I", 10.0, "pH", "D", "at", 20.0, "no", "rn", "I", "I", 2.0, 10.0, "fo", "D", "D", "pI", 20.0, "pD", "ff", "tu", "sd", "bf", "d", "bo", "si", "nb", "ba", "i", "ra", "d", "bs", "sp", "u", 20.0, 30.0, "d", "p", 10.0, "i", 20.0, 2.0, "d", 20.0, "p", "d", "i", "br", "p", 20.0, "i", "g", "p", "i", "bg", "dr"]
KINDS = ["zwyx/xyzw", "zwyx/yzwx", "xyzw/yzwx"]
CUTS = [4, 4, 4]


def body(
    inputs,
    lengths,
    w_qkv,
    b_qv,
    w_out,
    b_out,
    ln_gains,
    ln_biases,
    w_in,
    b_in,
    w_down,
    b_down,
    cotangent,
):
    size = lax.axis_size("dp")
    me = lax.axis_index("dp")
    side = lax.axis_index("tensor")
    side_index = side.astype(jnp.int32).reshape(1)
    tokens, width = inputs.shape[1:]
    local = w_qkv.shape[2]
    units = w_in.shape[1]
    rows = lax.dynamic_index_in_dim(inputs, side, 0, keepdims=False)
    length = lax.dynamic_slice_in_dim(lengths, side, 1)
    upstream = lax.dynamic_index_in_dim(cotangent, side, 0, keepdims=False)

    order = Order()

    bits = size.bit_length() - 1
    share = width // size
    block_of = jnp.array([reverse_bits(p, bits) for p in range(size)], jnp.int32) ^ me
    source = (block_of[:, None] * share + jnp.arange(share)[None, :]).reshape(-1, 1)

    rank, core = me & 7, me & 1
    core_index = core.astype(jnp.int32).reshape(1)
    qkv_own = jnp.transpose(w_qkv, (1, 0, 2))
    depth = width // 8
    heads_share, feed_share, small_other = shares(
        rank.astype(jnp.int32).reshape(1), qkv_own, w_out, w_in, w_down, b_qv, b_in.reshape(1, -1)
    )
    heads_share = swap_x(heads_share)
    feed_share = swap_x(feed_share)
    small_other = swap_x(small_other)

    dims = [1 << k for k in range(1, size.bit_length() - 1)]
    letters = {"x": [None], "y": dims[:1], "z": dims[1:2], "w": dims[2:]}

    def kind(k):
        return [[dim for letter in word for dim in letters[letter]] for word in KINDS[k].split("/")]

    chains = {}
    v = {}

    def step(name):
        return lambda: chains[name].step()

    def attend_own():
        v["own"] = attend(order, length, rows, qkv_own, b_qv, b_out.reshape(1, -1), w_out)

    def take_small():
        pinned = order.pin(small_other)
        v["b_qv"], v["b_in"] = pinned[:, : 2 * local].reshape(2, local), pinned[:, 2 * local :]

    def take_heads():
        chains["H"] = Chain(fetch_spread(order, order.pin(heads_share), me, size, 2.0))
        chains["H"].step()

    def take_feed():
        into_share, down_share = order.call(
            unpack_kernel,
            [shaped((1, 2, depth, width), single), shaped((1, 1, units // 8, width), single)],
            feed_share,
            cost=10.0,
        )
        chains["I"] = Chain(fetch_spread(order, into_share, me, size, 8.0))
        chains["D"] = Chain(fetch_spread(order, down_share, me, size, 8.0))
        chains["I"].step()
        chains["D"].step()

    def place_heads():
        v["w_heads"] = place(order, [chains["H"].value], (4, width, local))

    def place_in():
        v["w_in"] = place(order, [chains["I"].value], w_in.shape)

    def place_down():
        v["w_down"] = place(order, [chains["D"].value], w_down.shape)

    def relative_rows():
        v["rows_rel"] = relative(order, rows, source)

    def attend_other():
        v["other"] = attend(order, length, rows, v["w_heads"], v["b_qv"], v["own"][3])

    def norm():
        v["normed"], v["two_start"] = order.call(
            norm_kernel,
            [shaped((tokens, width), bfloat), shaped((tokens, width), single)],
            v["other"][3],
            ln_gains,
            ln_biases,
            b_down.reshape(1, -1),
        )

    def feed_own():
        v["act_own"], v["slope_own"], v["two_own"] = feed(
            order, v["normed"], w_in, b_in.reshape(1, -1), w_down, v["two_start"]
        )

    def feed_other():
        v["act"], v["slope"], v["two"] = feed(order, v["normed"], v["w_in"], v["b_in"], v["w_down"], v["two_own"])

    def relative_normed():
        v["normed_rel"] = relative(order, v["normed"], source)

    def turn():
        v["grad_two"], v["sums_two"], v["unit"], v["branch"] = order.call(
            turn_kernel,
            [
                shaped((tokens, width), single),
                shaped((3, width), single),
                shaped((tokens, width), single),
                shaped((tokens, width), bfloat),
            ],
            v["two"],
            ln_gains,
            upstream,
            cost=1.6,
        )
        v["unit_other"] = swap_x(v["unit"])

    def start_down():
        left = relative(order, v["branch"], source)
        terms = [(left, v["act_own"], v["act"])]
        chains["d"] = Chain(scatter(order, core_index, terms, CUTS[0], kind(0), size))
        chains["d"].step()

    def feed_back_other():
        v["pre"], v["units_sum"], v["grad_other"] = feed_back(
            order, v["branch"], v["w_down"], v["slope"], v["w_in"], v["grad_two"]
        )

    def feed_back_own():
        v["pre_own"], v["units_sum_own"], v["grad"] = feed_back(
            order, v["branch"], w_down, v["slope_own"], w_in, v["grad_other"]
        )

    def start_into():
        terms = [(v["normed_rel"], v["pre_own"], v["pre"])]
        chains["i"] = Chain(scatter(order, core_index, terms, CUTS[1], kind(1), size))
        chains["i"].step()

    def norm_two():
        v["grad_one"], v["sums_one"], v["attended"] = order.call(
            norm_back_kernel,
            [shaped((tokens, width), single), shaped((3, width), single), shaped((tokens, width), bfloat)],
            v["other"][3],
            ln_gains,
            v["grad"],
            cost=1.5,
        )

    def relative_attended():
        v["attended_rel"] = relative(order, v["attended"], source)

    def attend_back_other():
        v["proj"], v["proj_sum"], v["rows_other"] = attend_back(
            order, v["attended"], v["other"][0], v["other"][1], v["w_heads"], v["grad_one"]
        )

    def attend_back_own():
        v["proj_own"], v["proj_sum_own"], v["grad_rows"] = attend_back(
            order, v["attended"], v["own"][0], v["own"][1], qkv_own, v["rows_other"], w_out
        )
        v["grad_other_rows"] = swap_x(v["grad_rows"])

    def start_project():
        vectors = order.call(
            vectors_kernel,
            shaped((8, 2 * width), single),
            v["sums_one"],
            v["sums_two"],
            v["units_sum_own"],
            v["units_sum"],
            v["proj_sum_own"],
            v["proj_sum"],
            scalars=(side_index,),
            cost=0.5,
        )
        terms = [
            (v["attended_rel"], v["own"][2], v["other"][2]),
            (v["rows_rel"], v["proj_own"], v["proj"]),
        ]
        chains["p"] = Chain(scatter(order, core_index, terms, CUTS[2], kind(2), size, vectors))
        chains["p"].step()

    def pinned(name):
        def run():
            v[name] = order.pin(v[name])

        return run

    def both_results():
        v["results"] = order.call(
            both_result_kernel,
            shaped((2, tokens, width), bfloat),
            v["unit"],
            v["unit_other"],
            ln_gains,
            ln_biases,
            scalars=(side_index,),
            cost=1.5,
        )

    def both_grads():
        v["grads"] = order.call(
            both_kernel,
            shaped((2, tokens, width), single),
            v["grad_rows"],
            v["grad_other_rows"],
            scalars=(side_index,),
            cost=2.0,
        )

    def drain():
        last = [chains[name] for name in ("p", "d", "i")]
        while any(chain.value is None for chain in last):
            for chain in last:
                if chain.value is None:
                    chain.step()

    steps = {
        "ao": attend_own,
        "sm": take_small,
        "tH": take_heads,
        "tF": take_feed,
        "H": step("H"),
        "I": step("I"),
        "D": step("D"),
        "pH": place_heads,
        "pI": place_in,
        "pD": place_down,
        "rr": relative_rows,
        "at": attend_other,
        "no": norm,
        "fo": feed_own,
        "ff": feed_other,
        "rn": relative_normed,
        "tu": turn,
        "sd": start_down,
        "bf": feed_back_other,
        "bo": feed_back_own,
        "si": start_into,
        "nb": norm_two,
        "ra": relative_attended,
        "ba": attend_back_other,
        "bs": attend_back_own,
        "sp": start_project,
        "d": step("d"),
        "i": step("i"),
        "p": step("p"),
        "u": pinned("unit_other"),
        "g": pinned("grad_other_rows"),
        "br": both_results,
        "bg": both_grads,
        "dr": drain,
    }
    for name in SCHEDULE:
        if isinstance(name, str):
            steps[name]()
        else:
            order.pad(float(name))
    results, grads = v["results"], v["grads"]
    down, into, project = chains["d"], chains["i"], chains["p"]
    share_in = into.value[0]
    share_project, sums = project.value
    share_out, share_qkv = share_project[:, :local], share_project[:, local:]
    mine = jnp.where(side == 0, sums[3:5], sums[5:7])
    first_sums, second_sums = sums[:3, :width], sums[:3, width:]
    return (
        results,
        grads,
        share_qkv.reshape(-1, 3, local),
        mine[1, : 2 * local].reshape(2, local),
        share_out.T,
        first_sums[2],
        jnp.stack([first_sums[0], second_sums[0]]),
        jnp.stack([first_sums[1], second_sums[1]]),
        share_in,
        mine[0],
        down.value[0].T,
        second_sums[2],
    )


def solution(mesh):
    placed = (
        P("dp", None, None),
        P("dp"),
        P(None, None, "tensor"),
        P(None, "tensor"),
        P("tensor", None),
        P(),
        P(),
        P(),
        P(None, "tensor"),
        P("tensor"),
        P("tensor", None),
        P(),
        P("dp", None, None),
    )
    return jax.shard_map(
        body,
        mesh=mesh,
        in_specs=placed,
        out_specs=(
            P("dp", None, None),
            P("dp", None, None),
            P("dp", None, "tensor"),
            P(None, "tensor"),
            P("tensor", "dp"),
            P(),
            P(),
            P(),
            P("dp", "tensor"),
            P("tensor"),
            P("tensor", "dp"),
            P(),
        ),
        check_vma=False,
    )
```

```python
import functools
import types

import jax
import jax.numpy as jnp
from jax import lax
from jax.experimental import pallas as pl
from jax.experimental.pallas import tpu as pltpu
from jax.sharding import PartitionSpec as P

HEAD_DIM = 64
PAIR = 2 * HEAD_DIM
norm_eps = 1e-12
bfloat = jnp.bfloat16
single = jnp.float32
MIB = 1 << 20
COST_UNIT = 1.0e9


def dot(left, right):
    return jnp.dot(left, right, preferred_element_type=single)


def dot_cols(left, right):
    return lax.dot_general(
        left, right, (((1,), (1,)), ((), ())), preferred_element_type=single
    )


def shaped(shape, dtype):
    return jax.ShapeDtypeStruct(shape, dtype)


def nothing_kernel(out_ref):
    out_ref[...] = jnp.zeros_like(out_ref)


class Order:
    def __init__(self):
        self.last = None

    def call(self, kernel, outs, *args, scalars=(), scratch=(), grid=(), in_specs=None, out_specs=None, limit=16, aliases=None, cost=1.0, name=None):
        many = isinstance(outs, (tuple, list))
        if in_specs is None:
            in_specs = [pl.BlockSpec(memory_space=pltpu.VMEM)] * len(args)
        if out_specs is None:
            out_specs = [pl.BlockSpec(memory_space=pltpu.VMEM)] * len(outs) if many else pl.BlockSpec(memory_space=pltpu.VMEM)
        in_specs = [pl.BlockSpec(memory_space=pltpu.SMEM)] * len(scalars) + list(in_specs)
        operands = list(scalars) + list(args)
        run = kernel
        if self.last is not None:
            before = len(operands)
            operands.append(self.last)
            in_specs.append(pl.BlockSpec(memory_space=pl.ANY))

            def run(*refs):
                kernel(*refs[:before], *refs[before + 1 :])

        made = pl.pallas_call(
            run,
            out_shape=outs,
            grid=grid,
            in_specs=in_specs,
            out_specs=out_specs,
            scratch_shapes=list(scratch),
            name=name or kernel.__name__,
            input_output_aliases=aliases or {},
            compiler_params=pltpu.CompilerParams(vmem_limit_bytes=limit * MIB),
            cost_estimate=pl.CostEstimate(flops=int(cost * COST_UNIT), bytes_accessed=1000, transcendentals=0),
        )(*operands)
        self.last = made[-1] if many else made
        return made

    def pad(self, cost):
        self.call(nothing_kernel, shaped((8, 128), single), cost=cost)

    def pin(self, value):
        return self.call(
            lambda *refs: None,
            shaped(value.shape, value.dtype),
            value,
            in_specs=[pl.BlockSpec(memory_space=pl.ANY)],
            out_specs=pl.BlockSpec(memory_space=pl.ANY),
            aliases={0: 0},
            cost=0.0,
            name="pin_kernel",
        )


class Chain:
    def __init__(self, steps):
        self.steps = steps
        self.value = None

    def step(self):
        self.value = next(self.steps, self.value)
        return self.value

    def run(self, count):
        for _ in range(count):
            self.step()


def swap_dp(value, mask, size):
    return lax.ppermute(value, "dp", [(i, i ^ mask) for i in range(size)])


def swap_x(value):
    return lax.ppermute(value, "tensor", [(0, 1), (1, 0)])


def reverse_bits(position, bits):
    out = 0
    for k in range(bits):
        out |= ((position >> k) & 1) << (bits - 1 - k)
    return out


def place_kernel(starts, me_ref, *refs):
    out_ref = refs[-1]
    me = me_ref[0]
    at = 0
    for piece in refs[:-1]:
        height = piece.shape[2]
        for b in range(piece.shape[0]):
            start = pl.multiple_of(starts[at](me), 16)
            for c in range(piece.shape[1]):
                if out_ref.ndim == 3:
                    out_ref[c, pl.ds(start, height), :] = piece[b, c].astype(out_ref.dtype)
                else:
                    lanes = slice(c * piece.shape[3], (c + 1) * piece.shape[3])
                    out_ref[pl.ds(start, height), lanes] = piece[b, c].astype(out_ref.dtype)
            at += 1


def place(order, me, parts, shape):
    pieces, starts = [], []
    for held, begin in parts:
        pieces += held
        starts += begin
    kernel = functools.partial(place_kernel, tuple(starts))
    return order.call(kernel, shaped(shape, bfloat), *pieces, scalars=(me,), cost=2.4, name="place_kernel")


def pack_kernel(first_ref, second_ref, out_ref):
    out_ref[0] = first_ref[0]
    out_ref[1] = second_ref[0]


def swap_mixed(value, first, second, size):
    pairs = []
    for d in range(size):
        mask = second if d & 1 else first
        for t in range(2):
            to = (d, 1 - t) if mask is None else (d ^ mask, t)
            pairs.append((2 * d + t, 2 * to[0] + to[1]))
    return lax.ppermute(value, ("dp", "tensor"), pairs)


def fetch_spread(order, held, size, pack_cost):
    arrived = swap_mixed(held, 4, 2, size)
    yield
    both = order.call(pack_kernel, shaped((2,) + held.shape[1:], single), held, arrived, cost=pack_cost)
    arrived = swap_mixed(both, 2, 4, size)
    both_core = swap_dp(both, 1, size)
    yield
    both_core = order.pin(both_core)
    yield
    arrived = order.pin(arrived)
    arrived_core = swap_dp(arrived, 1, size)
    rows = held.shape[-2]

    def start(even, odd, flip):
        return lambda index: ((index & 7) ^ flip ^ jnp.where(index & 1 == flip, even, odd)) * rows

    offsets = list(zip((0, 4, 2, 6), (0, 2, 4, 6)))
    yield [both, arrived, both_core, arrived_core], [
        start(even, odd, flip) for flip in range(2) for even, odd in offsets
    ]


def fetch_direct(order, held, size, base):
    held = order.pin(held)
    rows = held.shape[-2]
    yield [held, swap_dp(held, 1, size)], [
        lambda index: base + (index & 1) * rows,
        lambda index: base + (1 - (index & 1)) * rows,
    ]


def unpack_kernel(all_ref, into_ref, down_ref):
    rows = into_ref.shape[2]
    for c in range(2):
        into_ref[0, c] = all_ref[c * rows : (c + 1) * rows, :]
    down_ref[0, 0] = all_ref[2 * rows :, :]


def product_kernel(groups, cuts, places, extras, core_ref, *refs):
    lefts, rights = refs[: len(groups)], refs[len(groups) : 3 * len(groups)]
    rest = refs[3 * len(groups) :]
    tile = pl.program_id(0)
    first = core_ref[0] == 0

    def spread(side, total, low_ref, high_ref, table, height):
        half = len(table[0])
        for block in range(half):
            at = table[side][block]
            out_ref, at = (low_ref, at) if at < half else (high_ref, at - half)
            out_ref[at * height : (at + 1) * height, :] = total[block * height : (block + 1) * height]

    def run(k, j):
        for side in range(2):
            total = dot(lefts[k][...], rights[2 * k + side][...])
            cut = j * cuts // sum(groups)
            if places is None:
                rest[cut][side] = total
                continue
            total = total + rest[cut][side]
            low_ref, high_ref = rest[cuts + extras :][:2]
            even, odd, height = places
            pl.when(first)(lambda: spread(side, total, low_ref, high_ref, even, height))
            pl.when(jnp.logical_not(first))(lambda: spread(side, total, low_ref, high_ref, odd, height))

    j = 0
    for k, tiles in enumerate(groups):
        for _ in range(tiles):
            pl.when(tile == j)(functools.partial(run, k, j))
            j += 1
    if extras:
        total = rest[cuts][...] + rest[cuts + 1][...]
        low_ref, high_ref, extra_ref = rest[cuts + 2 :]
        extra_ref[...] = total
        high_ref[low_ref.shape[0] :, :] = total


TILE = 384


def product(order, core, half, terms, cuts, added=(), places=None, extras=()):
    rows = terms[0][0].shape[0] // 2
    tokens = terms[0][0].shape[1]
    groups = tuple(term[4] // TILE for term in terms)
    begins = [sum(groups[:k]) for k in range(len(groups))]
    tiles = sum(groups)

    def right_spec(k):
        first = terms[k][3] // TILE
        return pl.BlockSpec((tokens, TILE), lambda j: (0, first + jnp.clip(j - begins[k], 0, groups[k] - 1)))

    def tall(height):
        return shaped((height, tiles * TILE), single), pl.BlockSpec((height, TILE), lambda j: (0, j))

    each = tiles // cuts
    pieces = [
        pl.BlockSpec((2, rows, TILE), lambda j, k=k: (0, 0, jnp.clip(j - k * each, 0, each - 1)))
        for k in range(cuts)
    ]
    if places is None:
        outs, out_specs = [shaped((2, rows, each * TILE), single)] * cuts, pieces
    else:
        height = len(places[0][0]) * places[2]
        heights = [height, height] + [part.shape[0] for part in extras[:1]]
        if extras:
            heights[1] += heights[2]
        outs, out_specs = zip(*[tall(height) for height in heights])
    return order.call(
        functools.partial(product_kernel, groups, cuts, places, len(extras)),
        list(outs),
        *[term[0] for term in terms],
        *[side for term in terms for side in term[1:3]],
        *added,
        *extras,
        scalars=(core,),
        grid=(tiles,),
        in_specs=[
            *[pl.BlockSpec((rows, tokens), lambda j: (half, 0)) for _ in terms],
            *[right_spec(k) for k in range(len(terms)) for _ in range(2)],
            *(pieces if added else []),
            *[tall(part.shape[0])[1] for part in extras],
        ],
        out_specs=list(out_specs),
        cost=tiles * 0.8 if places is None else tiles * 1.2,
        name="send_kernel" if places is None else "keep_kernel",
    )


def sum_kernel(whole, low_ref, arrived_ref, *refs):
    rows = low_ref.shape[0]
    extra = refs[0][...] + arrived_ref[rows:, :] if arrived_ref.shape[0] > rows else None
    outs = refs if extra is None else refs[1:]
    if whole:
        outs[0][...] = low_ref[...] + arrived_ref[:rows, :]
    else:
        half = rows // 2
        outs[0][...] = low_ref[:half, :] + arrived_ref[:half, :]
        outs[1][:half, :] = low_ref[half:, :] + arrived_ref[half:rows, :]
    if extra is not None:
        outs[-1][...] = extra
        if not whole:
            outs[1][rows // 2 :, :] = extra


def add_arrived(order, low, arrived, extra, whole):
    rows, width = low.shape
    beyond = arrived.shape[0] - rows
    heights = [rows] if whole else [rows // 2, rows // 2 + beyond]
    heights += [beyond] if beyond else []
    outs = order.call(
        functools.partial(sum_kernel, whole),
        [shaped((height, width), single) for height in heights],
        low,
        arrived,
        *([extra] if beyond else []),
        cost=0.7,
        name="add_kernel",
    )
    return outs if beyond else [*outs, None]


def scatter(order, core, terms, cuts, orders, size, extra=None):
    masks = [1 << k for k in range(1, size.bit_length() - 1)]
    count = len(masks)

    def place_of(side, block, dims):
        at = 0
        for dim in dims:
            bit = side if dim is None else (block >> (count - 1 - masks.index(dim))) & 1
            at = 2 * at + bit
        return at

    tables = [
        [[place_of(side, block, dims) for block in range(1 << count)] for side in range(2)]
        for dims in orders
    ]
    sent = product(order, core, 1, terms, cuts)
    arrived = [swap_dp(part, 1, size) for part in sent]
    extras = () if extra is None else (extra, swap_dp(extra, 1, size))
    yield
    height = terms[0][0].shape[0] // size
    low, high, *extra = product(order, core, 0, terms, cuts, arrived, (*tables, height), extras)
    extra = extra[0] if extras else None
    for k in range(count + 1):
        arrived = swap_mixed(high, orders[0][k], orders[1][k], size)
        yield
        if k < count:
            low, high, extra = add_arrived(order, low, arrived, extra, False)
    total, extra = add_arrived(order, low, arrived, extra, True)
    yield (total, extra)


def relative_kernel(size, side_ref, me_ref, value_ref, blocks_ref, within_ref, out_ref):
    value = value_ref[side_ref[0]] if len(value_ref.shape) == 3 else value_ref[...]
    depth = value.shape[1]
    tile = depth // 4
    me = me_ref[0]

    def step(j, carry):
        at = pl.multiple_of(j * tile, 16)
        lanes = lax.broadcasted_iota(jnp.int32, (tile, depth), 1)
        source = (blocks_ref[pl.ds(at, tile), :] ^ me) * (depth // size) + within_ref[pl.ds(at, tile), :]
        picks = jnp.where(lanes == source, 1.0, 0.0).astype(bfloat)
        out_ref[pl.ds(at, tile), :] = dot_cols(picks, value).astype(bfloat)
        return carry

    lax.fori_loop(0, 4, step, 0)


def relative(order, side, me, size, value):
    depth = value.shape[-1]
    share = depth // size
    bits = size.bit_length() - 1
    blocks = [[reverse_bits(row // share, bits)] for row in range(depth)]
    within = [[row % share] for row in range(depth)]
    return order.call(
        functools.partial(relative_kernel, size),
        shaped(value.shape[-2:][::-1], bfloat),
        value,
        jnp.array(blocks, jnp.int32),
        jnp.array(within, jnp.int32),
        scalars=(side, me),
        cost=1.7,
        name="relative_kernel",
    )


def attend_kernel(side_ref, lengths_ref, inputs_ref, qkv_ref, bias_ref, start_ref, *refs):
    *out_w, parts_ref, chance_ref, context_ref, hidden_ref, turned_ref = refs
    tokens = inputs_ref.shape[1]
    local = qkv_ref.shape[2]
    side = side_ref[0]
    rows = inputs_ref[side]
    flat = bias_ref.shape[0] == 1
    for part in range(3):
        projected = dot(rows, qkv_ref[part])
        if part != 1:
            k = part // 2
            projected = projected + (bias_ref[:, k * local : (k + 1) * local] if flat else bias_ref[k : k + 1, :])
        parts_ref[part] = projected.astype(bfloat)
    tile = 256
    visible = lax.broadcasted_iota(jnp.int32, (tokens, tile), 0) < lengths_ref[side]

    def pair_step(pair, carry):
        at = pl.multiple_of(pair * PAIR, PAIR)
        keys = parts_ref[1, :, pl.ds(at, PAIR)]
        queries = parts_ref[0, :, pl.ds(at, PAIR)].T
        values = parts_ref[2, :, pl.ds(at, PAIR)].T
        owner = lax.broadcasted_iota(jnp.int32, (PAIR, tile), 0) // HEAD_DIM
        for h in range(2):
            value_rows = values[h * HEAD_DIM : (h + 1) * HEAD_DIM]
            for q in range(tokens // tile):
                picked = queries[:, q * tile : (q + 1) * tile] * HEAD_DIM**-0.5
                picked = jnp.where(owner == h, picked, jnp.zeros_like(picked))
                scores = jnp.where(visible, dot(keys, picked), -1e9)
                raised = jnp.exp(scores - jnp.max(scores, axis=0, keepdims=True))
                chances = raised * (1.0 / jnp.sum(raised, axis=0, keepdims=True))
                chances = chances.astype(bfloat)
                chance_ref[pair * 2 + h, :, q * tile : (q + 1) * tile] = chances
                turned_ref[pl.ds(pl.multiple_of(at + h * HEAD_DIM, HEAD_DIM), HEAD_DIM), q * tile : (q + 1) * tile] = dot(value_rows, chances).astype(bfloat)
        return carry

    lax.fori_loop(0, local // PAIR, pair_step, 0)
    context = turned_ref[...].T
    context_ref[...] = context
    if out_w:
        hidden_ref[...] = rows.astype(single) + start_ref[...] + dot(context, out_w[0][...])
    else:
        middle = hidden_ref.shape[1] // 2
        hidden_ref[:, :middle] = start_ref[:, :middle] + dot(context, qkv_ref[3, :local, :])
        hidden_ref[:, middle:] = start_ref[:, middle:] + dot(context, qkv_ref[3, local:, :])


def attend(order, side, lengths, inputs, qkv, bias, start, out=None):
    tokens, width = inputs.shape[1:]
    local = qkv.shape[2]
    return order.call(
        attend_kernel,
        [
            shaped((3, tokens, local), bfloat),
            shaped((local // HEAD_DIM, tokens, tokens), bfloat),
            shaped((tokens, local), bfloat),
            shaped((tokens, width), single),
        ],
        inputs,
        qkv,
        bias,
        start,
        *([] if out is None else [out]),
        scalars=(side, lengths),
        scratch=[pltpu.VMEM((local, tokens), bfloat)],
        cost=9.0,
    )


def unit_of(hidden):
    centred = hidden - jnp.mean(hidden, axis=-1, keepdims=True)
    scale = lax.rsqrt(jnp.mean(centred * centred, axis=-1, keepdims=True) + norm_eps)
    return centred * scale, scale


def norm_back(upstream, unit, scale, gain):
    scaled = upstream * gain
    return scale * (
        scaled
        - jnp.mean(scaled, axis=-1, keepdims=True)
        - unit * jnp.mean(scaled * unit, axis=-1, keepdims=True)
    )


STRIP = 128


def strips(tokens, body):
    def step(j, carry):
        body(pl.ds(pl.multiple_of(j * STRIP, STRIP), STRIP))
        return carry

    lax.fori_loop(0, tokens // STRIP, step, 0)


def norm_kernel(hidden_ref, gain_ref, shift_ref, down_ref, low_ref, next_ref):
    def body(at):
        unit, _ = unit_of(hidden_ref[at, :])
        normed = unit * gain_ref[0:1, :] + shift_ref[0:1, :]
        low_ref[at, :] = normed.astype(bfloat)
        next_ref[at, :] = normed + down_ref[...]

    strips(hidden_ref.shape[0], body)


def gelu_tiles(normed_ref, into_ref, bias_ref, act_ref, slope_ref):
    hidden_units = into_ref.shape[1]
    tile = 256
    before = bias_ref.shape[1] - hidden_units

    def step(j, carry):
        at = pl.ds(pl.multiple_of(j * tile, tile), tile)
        bias_at = pl.ds(pl.multiple_of(before + j * tile, tile), tile)
        for k in range(2):
            strip = pl.ds(k * 256, 256)
            pre = dot(normed_ref[strip, :], into_ref[:, at]) + bias_ref[:, bias_at]
            bell = jnp.exp(-0.5 * pre * pre)
            reach = 1.0 / (1.0 + 0.23164189 * jnp.abs(pre))
            tail = reach * (
                0.127414796
                + reach * (-0.142248368 + reach * (0.7107068705 + reach * (-0.7265760135 + reach * 0.5307027145)))
            )
            tail = tail * bell
            chance = jnp.where(pre >= 0, 1.0 - tail, tail)
            act_ref[strip, at] = (pre * chance).astype(bfloat)
            slope_ref[strip, at] = (chance + pre * bell * 0.3989422804014327).astype(bfloat)
        return carry

    lax.fori_loop(0, hidden_units // tile, step, 0)


def feed_kernel(normed_ref, into_ref, bias_ref, down_ref, start_ref, act_ref, slope_ref, hidden_ref):
    gelu_tiles(normed_ref, into_ref, bias_ref, act_ref, slope_ref)
    hidden_ref[...] = start_ref[...] + dot(act_ref[...], down_ref[...])


def feed(order, normed, into, bias, down, start):
    tokens, width = normed.shape
    units = into.shape[1]
    return order.call(
        feed_kernel,
        [shaped((tokens, units), bfloat), shaped((tokens, units), bfloat), shaped((tokens, width), single)],
        normed,
        into,
        bias,
        down,
        start,
        cost=6.0,
    )


def feed_up(order, normed, into, bias):
    units = into.shape[1]
    return order.call(
        gelu_tiles,
        [shaped((normed.shape[0], units), bfloat)] * 2,
        normed,
        into,
        bias,
        cost=4.5,
        name="feed_up_kernel",
    )


def add_columns(ref, row, value):
    ref[row : row + 1, :] += jnp.sum(value, axis=0, keepdims=True)


def turn_kernel(side_ref, act_ref, down_ref, start_ref, gain_ref, upstream_ref, grad_ref, sums_ref, unit_ref, branch_ref):
    sums_ref[...] = jnp.zeros_like(sums_ref)

    def body(at):
        unit, scale = unit_of(start_ref[at, :] + dot(act_ref[at, :], down_ref[...]))
        gain = gain_ref[1:2, :]
        upstream = upstream_ref[side_ref[0], at, :].astype(single)
        unit_ref[at, :] = unit
        grad = norm_back(upstream, unit, scale, gain)
        grad_ref[at, :] = grad
        branch_ref[at, :] = grad.astype(bfloat)
        add_columns(sums_ref, 0, upstream * unit)
        add_columns(sums_ref, 1, upstream)
        add_columns(sums_ref, 2, grad)

    strips(start_ref.shape[0], body)


def feed_back_kernel(branch_ref, down_ref, slope_ref, into_ref, start_ref, grad_ref, sums_ref, normed_ref):
    hidden_units = into_ref.shape[1]
    tile = 256

    def step(j, carry):
        at = pl.ds(pl.multiple_of(j * tile, tile), tile)
        pre = dot_cols(branch_ref[...], down_ref[at, :]) * slope_ref[:, at].astype(single)
        low = pre.astype(bfloat)
        grad_ref[:, at] = low
        sums_ref[:, at] = jnp.sum(low.astype(single), axis=0, keepdims=True)
        return carry

    lax.fori_loop(0, hidden_units // tile, step, 0)
    normed_ref[...] = start_ref[...] + dot_cols(grad_ref[...], into_ref[...])


def feed_back(order, branch, down, slope, into, start):
    tokens, width = branch.shape
    units = into.shape[1]
    return order.call(
        feed_back_kernel,
        [shaped((tokens, units), bfloat), shaped((1, units), single), shaped((tokens, width), single)],
        branch,
        down,
        slope,
        into,
        start,
        cost=3.9,
    )


def norm_back_kernel(hidden_ref, gain_ref, upstream_ref, grad_ref, sums_ref, low_ref):
    sums_ref[...] = jnp.zeros_like(sums_ref)

    def body(at):
        unit, scale = unit_of(hidden_ref[at, :])
        upstream = upstream_ref[at, :]
        grad = norm_back(upstream, unit, scale, gain_ref[0:1, :])
        grad_ref[at, :] = grad
        low_ref[at, :] = grad.astype(bfloat)
        add_columns(sums_ref, 0, upstream * unit)
        add_columns(sums_ref, 1, upstream)
        add_columns(sums_ref, 2, grad)

    strips(hidden_ref.shape[0], body)


def attend_back_kernel(upstream_ref, parts_ref, chance_ref, qkv_ref, start_ref, *refs):
    *out_w, grad_ref, sums_ref, rows_ref, turned_ref = refs
    tokens = upstream_ref.shape[0]
    local = qkv_ref.shape[2]
    middle = upstream_ref.shape[1] // 2
    tile = 256
    factor = HEAD_DIM**-0.5

    def pair_step(pair, carry):
        at = pl.multiple_of(pair * PAIR, PAIR)
        lanes = pl.ds(at, PAIR)
        queries = parts_ref[0, :, lanes]
        keys_turned = parts_ref[1, :, lanes].T
        values = parts_ref[2, :, lanes]
        if out_w:
            grad_context = dot_cols(upstream_ref[...], out_w[0][lanes, :])
        else:
            grad_context = dot_cols(upstream_ref[:, :middle], qkv_ref[3, lanes, :])
            grad_context = grad_context + dot_cols(
                upstream_ref[:, middle:], qkv_ref[3, pl.ds(pl.multiple_of(local + at, PAIR), PAIR), :]
            )
        grad_context = grad_context.astype(bfloat)
        context_turned = grad_context.T
        owner = lax.broadcasted_iota(jnp.int32, (PAIR, tile), 0) // HEAD_DIM
        first_lane = lax.broadcasted_iota(jnp.int32, (tokens, PAIR), 1) < HEAD_DIM
        grads_k, grads_v = [], []
        for h in range(2):
            key_rows = keys_turned[h * HEAD_DIM : (h + 1) * HEAD_DIM]
            grad_k = jnp.zeros((tokens, PAIR), single)
            grad_v = jnp.zeros((tokens, PAIR), single)
            for q in range(tokens // tile):
                cut = slice(q * tile, (q + 1) * tile)
                picked = context_turned[:, cut]
                picked = jnp.where(owner == h, picked, jnp.zeros_like(picked))
                chances_low = chance_ref[pair * 2 + h, :, cut]
                chances = chances_low.astype(single)
                grad_chances = dot(values, picked)
                inner = jnp.sum(chances * grad_chances, axis=0, keepdims=True)
                grad_scores = (chances * (grad_chances - inner)).astype(bfloat)
                grad_v = grad_v + dot(chances_low, grad_context[cut, :])
                grad_k = grad_k + dot(grad_scores, queries[cut, :])
                turned_ref[pl.ds(pl.multiple_of(at + h * HEAD_DIM, HEAD_DIM), HEAD_DIM), cut] = (dot(key_rows, grad_scores) * factor).astype(bfloat)
            grads_k.append(grad_k)
            grads_v.append(grad_v)
        grad_k = (jnp.where(first_lane, grads_k[0], grads_k[1]) * factor).astype(bfloat)
        grad_v = jnp.where(first_lane, grads_v[0], grads_v[1]).astype(bfloat)
        grad_ref[:, pl.ds(pl.multiple_of(local + at, PAIR), PAIR)] = grad_k
        grad_ref[:, pl.ds(pl.multiple_of(2 * local + at, PAIR), PAIR)] = grad_v
        return carry

    lax.fori_loop(0, local // PAIR, pair_step, 0)
    grad_ref[:, 0:local] = turned_ref[...].T
    sums_ref[...] = jnp.sum(grad_ref[...].astype(single), axis=0, keepdims=True)
    total = start_ref[...]
    for part in range(3):
        total = total + dot_cols(grad_ref[:, part * local : (part + 1) * local], qkv_ref[part])
    rows_ref[...] = total


def attend_back(order, upstream, parts, chances, qkv, start, out=None):
    tokens, width = upstream.shape
    local = qkv.shape[2]
    return order.call(
        attend_back_kernel,
        [shaped((tokens, 3 * local), bfloat), shaped((1, 3 * local), single), shaped((tokens, width), single)],
        upstream,
        parts,
        chances,
        qkv,
        start,
        *([] if out is None else [out]),
        scratch=[pltpu.VMEM((local, tokens), bfloat)],
        cost=9.4,
    )


def vectors_kernel(side_ref, first_ref, second_ref, units_own, units_other, proj_own, proj_other, out_ref):
    width = first_ref.shape[1]
    local = proj_own.shape[1] // 3
    out_ref[...] = jnp.zeros_like(out_ref)
    out_ref[0:3, :] = first_ref[...]
    out_ref[3:6, :] = second_ref[...]
    swapped = side_ref[0] == 1
    for row, units, proj in (
        (6, (units_own, units_other), (proj_own, proj_other)),
        (9, (units_other, units_own), (proj_other, proj_own)),
    ):
        both = jnp.where(swapped, units[1][...], units[0][...])
        for k in range(2):
            out_ref[row + k : row + k + 1, :] = both[:, k * width : (k + 1) * width]
        parts = jnp.where(swapped, proj[1][...], proj[0][...])
        out_ref[row + 2 : row + 3, :local] = parts[:, :local]
        out_ref[row + 2 : row + 3, local : 2 * local] = parts[:, 2 * local :]


def both_result_kernel(side_ref, mine_ref, other_ref, gain_ref, shift_ref, out_ref):
    side = side_ref[0]

    def body(at):
        for place, ref in ((side, mine_ref), (1 - side, other_ref)):
            out_ref[place, at, :] = (ref[at, :] * gain_ref[1:2, :] + shift_ref[1:2, :]).astype(bfloat)

    strips(mine_ref.shape[0], body)


def both_kernel(side_ref, mine_ref, other_ref, out_ref):
    side = side_ref[0]
    out_ref[side] = mine_ref[...]
    out_ref[1 - side] = other_ref[...]


def shares_kernel(rank_ref, qkv_ref, out_ref, left_ref, right_ref, down_ref, last_ref, heads_ref, feed_ref, direct_ref):
    heads_ref[0, 0:3] = qkv_ref[...].astype(single)
    heads_ref[0, 3] = out_ref[...].astype(single)
    depth = left_ref.shape[0]
    feed_ref[0:depth, :] = left_ref[...].astype(single)
    feed_ref[depth : 2 * depth, :] = right_ref[...].astype(single)
    feed_ref[2 * depth :, :] = down_ref[...].astype(single)
    direct_ref[0, 0] = last_ref[...].astype(single)


def small_kernel(bias_ref, units_ref, small_ref):
    local = bias_ref.shape[1]
    small_ref[:, 0:local] = bias_ref[0:1, :]
    small_ref[:, local : 2 * local] = bias_ref[1:2, :]
    small_ref[:, 2 * local :] = units_ref[...]


def shares(rank, qkv, out, into, down):
    width, local, hidden = qkv.shape[1], qkv.shape[2], into.shape[1]
    depth = width // 8
    quarters = local // depth
    rows, last = hidden // 12, hidden // 6
    shapes = [(1, 4, depth, local), (2 * depth + rows, width), (1, 1, last, width)]
    return pl.pallas_call(
        shares_kernel,
        grid_spec=pltpu.PrefetchScalarGridSpec(
            num_scalar_prefetch=1,
            grid=(1,),
            in_specs=[
                pl.BlockSpec((3, depth, local), lambda j, r: (0, r[0], 0)),
                pl.BlockSpec((depth, local), lambda j, r: (r[0] % quarters, r[0] // quarters)),
                pl.BlockSpec((depth, width), lambda j, r: (r[0], 0)),
                pl.BlockSpec((depth, width), lambda j, r: (r[0], 1)),
                pl.BlockSpec((rows, width), lambda j, r: (r[0], 0)),
                pl.BlockSpec((last, width), lambda j, r: (4 + r[0] % 2, 0)),
            ],
            out_specs=[pl.BlockSpec(shape, lambda j, r, n=len(shape): (0,) * n) for shape in shapes],
        ),
        out_shape=[shaped(shape, single) for shape in shapes],
        cost_estimate=pl.CostEstimate(flops=1000, bytes_accessed=1000, transcendentals=0),
    )(rank, qkv, out, into, into, down, down)


SCHEDULE = [8.0, 2.0, "ao", "ss", "tH", "H", "tF", "rr", "H", "H", "I", 2.0, "sm", 10.0, "pH", "D", "at", 20.0, "no", "rn", "I", "I", 2.0, 10.0, "tX", "fo", "D", "D", "pI", "ff", 20.0, "pD", "tu", "rb", "sd", "bf", "d", "bo", "si", "nb", "ba", "i", "ra", "d", "bs", "sq", 20.0, 30.0, 2.0, "d", "u", "q", 10.0, "i", 20.0, "d", "q", "d", "i", "br", "q", 20.0, 20.0, "i", "g", "q", "i", "bg", "dr"]
KINDS = ["zwyx/xyzw", "zwyx/xyzw", "zwyx/yzwx", "zwyx/yzwx", "xyzw/yzwx", "xyzw/yzwx"]
CUTS = [4, 4, 4, 4, 4, 4]
SPLITS = [1, 1, 1]


def body(
    inputs,
    lengths,
    w_qkv,
    b_qv,
    w_out,
    b_out,
    ln_gains,
    ln_biases,
    w_in,
    b_in,
    w_down,
    b_down,
    cotangent,
):
    size = lax.axis_size("dp")
    me = lax.axis_index("dp")
    side = lax.axis_index("tensor")
    side_index = side.astype(jnp.int32).reshape(1)
    tokens, width = inputs.shape[1:]
    local = w_qkv.shape[2]
    units = w_in.shape[1]
    order = Order()

    rank, core = me & 7, me & 1
    core_index = core.astype(jnp.int32).reshape(1)
    me_index = me.astype(jnp.int32).reshape(1)
    qkv_own = jnp.transpose(w_qkv, (1, 0, 2))
    depth = width // 8
    heads_share, feed_share, direct_share = shares(rank.astype(jnp.int32).reshape(1), qkv_own, w_out, w_in, w_down)
    heads_share = swap_x(heads_share)
    feed_share = swap_x(feed_share)
    direct_share = swap_x(direct_share)

    dims = [1 << k for k in range(1, size.bit_length() - 1)]
    letters = {"x": [None], "y": dims[:1], "z": dims[1:2], "w": dims[2:]}

    def kind(k):
        return [[dim for letter in word for dim in letters[letter]] for word in KINDS[k].split("/")]

    chains = {}
    v = types.SimpleNamespace()

    def step(name):
        return lambda: chains[name].step()

    def attend_own():
        v.own = attend(order, side_index, lengths, inputs, qkv_own, b_qv, b_out.reshape(1, -1), w_out)

    def send_small():
        hidden = b_in.reshape(1, -1)
        v.small_own = order.call(small_kernel, shaped((1, 2 * local + units), single), b_qv, hidden, cost=0.3)
        v.small_sent = swap_x(v.small_own)

    def take_small():
        v.small = order.pin(v.small_sent)

    def take_heads():
        chains["H"] = Chain(fetch_spread(order, order.pin(heads_share), size, 2.0))
        chains["H"].step()

    def take_feed():
        into_share, down_share = order.call(
            unpack_kernel,
            [shaped((1, 2, depth, width), single), shaped((1, 1, units // 12, width), single)],
            feed_share,
            cost=10.0,
        )
        chains["I"] = Chain(fetch_spread(order, into_share, size, 8.0))
        chains["D"] = Chain(fetch_spread(order, down_share, size, 8.0))
        chains["I"].step()
        chains["D"].step()

    def take_direct():
        chains["X"] = Chain(fetch_direct(order, direct_share, size, units // 3 * 2))
        chains["X"].step()

    def place_heads():
        v.w_heads = place(order, me_index, [chains["H"].value], (4, width, local))

    def place_in():
        v.w_in = place(order, me_index, [chains["I"].value], w_in.shape)

    def place_down():
        v.w_down = place(order, me_index, [chains["D"].value, chains["X"].value], w_down.shape)

    def relative_rows():
        v.rows_rel = relative(order, side_index, me_index, size, inputs)

    def attend_other():
        v.other = attend(order, side_index, lengths, inputs, v.w_heads, v.small, v.own[3])

    def norm():
        v.normed, v.two_start = order.call(
            norm_kernel,
            [shaped((tokens, width), bfloat), shaped((tokens, width), single)],
            v.other[3],
            ln_gains,
            ln_biases,
            b_down.reshape(1, -1),
        )

    def feed_own():
        v.act_own, v.slope_own, v.two_own = feed(
            order, v.normed, w_in, b_in.reshape(1, -1), w_down, v.two_start
        )

    def feed_other():
        v.act, v.slope = feed_up(order, v.normed, v.w_in, v.small)

    def relative_normed():
        v.normed_rel = relative(order, side_index, me_index, size, v.normed)

    def turn():
        v.grad_two, v.sums_two, v.unit, v.branch = order.call(
            turn_kernel,
            [
                shaped((tokens, width), single),
                shaped((3, width), single),
                shaped((tokens, width), single),
                shaped((tokens, width), bfloat),
            ],
            v.act,
            v.w_down,
            v.two_own,
            ln_gains,
            cotangent,
            scalars=(side_index,),
            cost=3.0,
        )
        v.unit_other = swap_x(v.unit)

    def start(name, k, terms, extra=None):
        chains[name] = Chain(scatter(order, core_index, terms, CUTS[k], kind(k), size, extra))
        chains[name].step()

    def piece(count, k):
        return k * units // count, units // count

    def relative_branch():
        v.branch_rel = relative(order, side_index, me_index, size, v.branch)

    def start_down(k):
        return lambda: start("de"[k], k, [(v.branch_rel, v.act_own, v.act, *piece(SPLITS[0], k))])

    def feed_back_other():
        v.pre, v.units_sum, v.grad_other = feed_back(
            order, v.branch, v.w_down, v.slope, v.w_in, v.grad_two
        )

    def feed_back_own():
        v.pre_own, v.units_sum_own, v.grad = feed_back(
            order, v.branch, w_down, v.slope_own, w_in, v.grad_other
        )

    def start_into(k):
        return lambda: start("ij"[k], 2 + k, [(v.normed_rel, v.pre_own, v.pre, *piece(SPLITS[1], k))])

    def norm_two():
        v.grad_one, v.sums_one, v.attended = order.call(
            norm_back_kernel,
            [shaped((tokens, width), single), shaped((3, width), single), shaped((tokens, width), bfloat)],
            v.other[3],
            ln_gains,
            v.grad,
            cost=1.5,
        )

    def relative_attended():
        v.attended_rel = relative(order, side_index, me_index, size, v.attended)

    def attend_back_other():
        v.proj, v.proj_sum, v.rows_other = attend_back(
            order, v.attended, v.other[0], v.other[1], v.w_heads, v.grad_one
        )

    def attend_back_own():
        v.proj_own, v.proj_sum_own, v.grad_rows = attend_back(
            order, v.attended, v.own[0], v.own[1], qkv_own, v.rows_other, w_out
        )
        v.grad_other_rows = swap_x(v.grad_rows)

    def start_out():
        terms = [
            (v.attended_rel, v.own[2], v.other[2], 0, local),
            (v.rows_rel, v.proj_own, v.proj, 0, local),
        ]
        start("p", 4, terms)

    def start_project():
        vectors = order.call(
            vectors_kernel,
            shaped((16, width), single),
            v.sums_one,
            v.sums_two,
            v.units_sum_own,
            v.units_sum,
            v.proj_sum_own,
            v.proj_sum,
            scalars=(side_index,),
            cost=0.5,
        )
        terms = [(v.rows_rel, v.proj_own, v.proj, local, 2 * local)]
        if SPLITS[2] == 1:
            terms = [
                (v.attended_rel, v.own[2], v.other[2], 0, local),
                (v.rows_rel, v.proj_own, v.proj, 0, 3 * local),
            ]
            vectors = jnp.concatenate([vectors[:8], vectors[8:]], axis=1)
        start("q", 5, terms, vectors)

    def take_unit():
        v.unit_other = order.pin(v.unit_other)

    def take_grad():
        v.grad_other_rows = order.pin(v.grad_other_rows)

    def both_results():
        v.results = order.call(
            both_result_kernel,
            shaped((2, tokens, width), bfloat),
            v.unit,
            v.unit_other,
            ln_gains,
            ln_biases,
            scalars=(side_index,),
            cost=1.5,
        )

    def both_grads():
        v.grads = order.call(
            both_kernel,
            shaped((2, tokens, width), single),
            v.grad_rows,
            v.grad_other_rows,
            scalars=(side_index,),
            cost=2.0,
        )

    def drain():
        last = list(chains.values())[-sum(SPLITS) :]
        while any(chain.value is None for chain in last):
            for chain in last:
                if chain.value is None:
                    chain.step()

    steps = {
        "ao": attend_own,
        "ss": send_small,
        "sm": take_small,
        "tH": take_heads,
        "tF": take_feed,
        "tX": take_direct,
        "H": step("H"),
        "I": step("I"),
        "D": step("D"),
        "pH": place_heads,
        "pI": place_in,
        "pD": place_down,
        "rr": relative_rows,
        "at": attend_other,
        "no": norm,
        "fo": feed_own,
        "ff": feed_other,
        "rn": relative_normed,
        "tu": turn,
        "rb": relative_branch,
        "sd": start_down(0),
        "se": start_down(1),
        "bf": feed_back_other,
        "bo": feed_back_own,
        "si": start_into(0),
        "sj": start_into(1),
        "nb": norm_two,
        "ra": relative_attended,
        "ba": attend_back_other,
        "bs": attend_back_own,
        "sp": start_out,
        "sq": start_project,
        **{name: step(name) for name in "deijpq"},
        "u": take_unit,
        "g": take_grad,
        "br": both_results,
        "bg": both_grads,
        "dr": drain,
    }
    for name in SCHEDULE:
        if isinstance(name, str):
            steps[name]()
        else:
            order.pad(float(name))
    results, grads = v.results, v.grads
    parts = [[chains[name].value[0] for name in names if name in chains] for names in ("de", "ij", "pq")]
    share_down, share_in, share_project = (jnp.concatenate(part, axis=1) for part in parts)
    share_out, share_qkv = share_project[:, :local], share_project[:, local:]
    sums = chains["q"].value[1]
    if SPLITS[2] == 1:
        sums = jnp.concatenate([sums[:, :width], sums[:, width:]], axis=0)
    mine = jnp.where(side == 0, sums[6:9], sums[9:12])

    return (
        results,
        grads,
        share_qkv.reshape(-1, 3, local),
        mine[2].reshape(2, local),
        share_out.T,
        sums[2],
        jnp.stack([sums[0], sums[3]]),
        jnp.stack([sums[1], sums[4]]),
        share_in,
        mine[:2].reshape(-1),
        share_down.T,
        sums[5],
    )


def solution(mesh):
    placed = (
        P("dp", None, None),
        P("dp"),
        P(None, None, "tensor"),
        P(None, "tensor"),
        P("tensor", None),
        P(),
        P(),
        P(),
        P(None, "tensor"),
        P("tensor"),
        P("tensor", None),
        P(),
        P("dp", None, None),
    )
    return jax.shard_map(
        body,
        mesh=mesh,
        in_specs=placed,
        out_specs=(
            P("dp", None, None),
            P("dp", None, None),
            P("dp", None, "tensor"),
            P(None, "tensor"),
            P("tensor", "dp"),
            P(),
            P(),
            P(),
            P("dp", "tensor"),
            P("tensor"),
            P("tensor", "dp"),
            P(),
        ),
        check_vma=False,
    )
```

```python
import functools
import types

import jax
import jax.numpy as jnp
from jax import lax
from jax.experimental import pallas as pl
from jax.experimental.pallas import tpu as pltpu
from jax.sharding import PartitionSpec as P

HEAD_DIM = 64
PAIR = 2 * HEAD_DIM
norm_eps = 1e-12
bfloat = jnp.bfloat16
single = jnp.float32
MIB = 1 << 20
COST_UNIT = 1.0e9


def dot(left, right):
    return jnp.dot(left, right, preferred_element_type=single)


def dot_cols(left, right):
    return lax.dot_general(
        left, right, (((1,), (1,)), ((), ())), preferred_element_type=single
    )


def shaped(shape, dtype):
    return jax.ShapeDtypeStruct(shape, dtype)


def nothing_kernel(out_ref):
    out_ref[...] = jnp.zeros_like(out_ref)


class Order:
    def __init__(self):
        self.last = None

    def call(self, kernel, outs, *args, scalars=(), scratch=(), grid=(), in_specs=None, out_specs=None, limit=16, aliases=None, cost=1.0, name=None):
        many = isinstance(outs, (tuple, list))
        if in_specs is None:
            in_specs = [pl.BlockSpec(memory_space=pltpu.VMEM)] * len(args)
        if out_specs is None:
            out_specs = [pl.BlockSpec(memory_space=pltpu.VMEM)] * len(outs) if many else pl.BlockSpec(memory_space=pltpu.VMEM)
        in_specs = [pl.BlockSpec(memory_space=pltpu.SMEM)] * len(scalars) + list(in_specs)
        operands = list(scalars) + list(args)
        run = kernel
        if self.last is not None:
            before = len(operands)
            operands.append(self.last)
            in_specs.append(pl.BlockSpec(memory_space=pl.ANY))

            def run(*refs):
                kernel(*refs[:before], *refs[before + 1 :])

        made = pl.pallas_call(
            run,
            out_shape=outs,
            grid=grid,
            in_specs=in_specs,
            out_specs=out_specs,
            scratch_shapes=list(scratch),
            name=name or kernel.__name__,
            input_output_aliases=aliases or {},
            compiler_params=pltpu.CompilerParams(vmem_limit_bytes=limit * MIB),
            cost_estimate=pl.CostEstimate(flops=int(cost * COST_UNIT), bytes_accessed=1000, transcendentals=0),
        )(*operands)
        self.last = made[-1] if many else made
        return made

    def pad(self, cost):
        self.call(nothing_kernel, shaped((8, 128), single), cost=cost)

    def pin(self, value):
        return self.call(
            lambda *refs: None,
            shaped(value.shape, value.dtype),
            value,
            in_specs=[pl.BlockSpec(memory_space=pl.ANY)],
            out_specs=pl.BlockSpec(memory_space=pl.ANY),
            aliases={0: 0},
            cost=0.0,
            name="pin_kernel",
        )


class Chain:
    def __init__(self, steps):
        self.steps = steps
        self.value = None

    def step(self):
        self.value = next(self.steps, self.value)
        return self.value

    def run(self, count):
        for _ in range(count):
            self.step()


def swap_dp(value, mask, size):
    return lax.ppermute(value, "dp", [(i, i ^ mask) for i in range(size)])


def swap_x(value):
    return lax.ppermute(value, "tensor", [(0, 1), (1, 0)])


def reverse_bits(position, bits):
    out = 0
    for k in range(bits):
        out |= ((position >> k) & 1) << (bits - 1 - k)
    return out


def place_kernel(starts, me_ref, *refs):
    out_ref = refs[-1]
    me = me_ref[0]
    at = 0
    for piece in refs[:-1]:
        height = piece.shape[2]
        for b in range(piece.shape[0]):
            start = pl.multiple_of(starts[at](me), 16)
            for c in range(piece.shape[1]):
                if out_ref.ndim == 3:
                    out_ref[c, pl.ds(start, height), :] = piece[b, c].astype(out_ref.dtype)
                else:
                    lanes = slice(c * piece.shape[3], (c + 1) * piece.shape[3])
                    out_ref[pl.ds(start, height), lanes] = piece[b, c].astype(out_ref.dtype)
            at += 1


def place(order, me, parts, shape):
    pieces, starts = [], []
    for held, begin in parts:
        pieces += held
        starts += begin
    kernel = functools.partial(place_kernel, tuple(starts))
    return order.call(kernel, shaped(shape, bfloat), *pieces, scalars=(me,), cost=2.4, name="place_kernel")


def pack_kernel(first_ref, second_ref, out_ref):
    out_ref[0] = first_ref[0]
    out_ref[1] = second_ref[0]


def swap_mixed(value, first, second, size):
    pairs = []
    for d in range(size):
        mask = second if d & 1 else first
        for t in range(2):
            to = (d, 1 - t) if mask is None else (d ^ mask, t)
            pairs.append((2 * d + t, 2 * to[0] + to[1]))
    return lax.ppermute(value, ("dp", "tensor"), pairs)


def fetch_spread(order, held, size, pack_cost):
    arrived = swap_mixed(held, 4, 2, size)
    yield
    both = order.call(pack_kernel, shaped((2,) + held.shape[1:], single), held, arrived, cost=pack_cost)
    arrived = swap_mixed(both, 2, 4, size)
    both_core = swap_dp(both, 1, size)
    yield
    both_core = order.pin(both_core)
    yield
    arrived = order.pin(arrived)
    arrived_core = swap_dp(arrived, 1, size)
    rows = held.shape[-2]

    def start(even, odd, flip):
        return lambda index: ((index & 7) ^ flip ^ jnp.where(index & 1 == flip, even, odd)) * rows

    offsets = list(zip((0, 4, 2, 6), (0, 2, 4, 6)))
    yield [both, arrived, both_core, arrived_core], [
        start(even, odd, flip) for flip in range(2) for even, odd in offsets
    ]


def fetch_direct(order, held, size, base):
    held = order.pin(held)
    rows = held.shape[-2]
    yield [held, swap_dp(held, 1, size)], [
        lambda index: base + (index & 1) * rows,
        lambda index: base + (1 - (index & 1)) * rows,
    ]


def unpack_kernel(all_ref, into_ref, down_ref):
    rows = into_ref.shape[2]
    for c in range(2):
        into_ref[0, c] = all_ref[c * rows : (c + 1) * rows, :]
    down_ref[0, 0] = all_ref[2 * rows :, :]


def product_kernel(groups, cuts, places, extras, core_ref, *refs):
    lefts, rights = refs[: len(groups)], refs[len(groups) : 3 * len(groups)]
    rest = refs[3 * len(groups) :]
    tile = pl.program_id(0)
    first = core_ref[0] == 0

    def spread(side, total, low_ref, high_ref, table, height):
        half = len(table[0])
        for block in range(half):
            at = table[side][block]
            out_ref, at = (low_ref, at) if at < half else (high_ref, at - half)
            out_ref[at * height : (at + 1) * height, :] = total[block * height : (block + 1) * height]

    def run(k, j):
        for side in range(2):
            total = dot(lefts[k][...], rights[2 * k + side][...])
            cut = j * cuts // sum(groups)
            if places is None:
                rest[extras + cut][side, : total.shape[0], :] = total
                if extras:
                    rest[extras + cut][side, total.shape[0] :, :] = rest[0][...]
                continue
            total = total + rest[cut][side, : total.shape[0], :]
            low_ref, high_ref = rest[cuts + extras :][:2]
            even, odd, height = places
            pl.when(first)(lambda: spread(side, total, low_ref, high_ref, even, height))
            pl.when(jnp.logical_not(first))(lambda: spread(side, total, low_ref, high_ref, odd, height))
            if extras and side == 0:
                beyond = rest[cuts].shape[0]
                extra = rest[cuts][...] + rest[cut][0, -beyond:, :]
                rest[-1][...] = extra
                high_ref[low_ref.shape[0] :, :] = extra

    j = 0
    for k, tiles in enumerate(groups):
        for _ in range(tiles):
            pl.when(tile == j)(functools.partial(run, k, j))
            j += 1


TILE = 384


def product(order, core, half, terms, cuts, added=(), places=None, extras=()):
    rows = terms[0][0].shape[0] // 2
    tokens = terms[0][0].shape[1]
    groups = tuple(term[4] // TILE for term in terms)
    begins = [sum(groups[:k]) for k in range(len(groups))]
    tiles = sum(groups)

    def right_spec(k):
        first = terms[k][3] // TILE
        return pl.BlockSpec((tokens, TILE), lambda j: (0, first + jnp.clip(j - begins[k], 0, groups[k] - 1)))

    def tall(height):
        return shaped((height, tiles * TILE), single), pl.BlockSpec((height, TILE), lambda j: (0, j))

    each = tiles // cuts
    beyond = sum(part.shape[0] for part in extras)
    pieces = [
        pl.BlockSpec((2, rows + beyond, TILE), lambda j, k=k: (0, 0, jnp.clip(j - k * each, 0, each - 1)))
        for k in range(cuts)
    ]
    if places is None:
        outs, out_specs = [shaped((2, rows + beyond, each * TILE), single)] * cuts, pieces
    else:
        height = len(places[0][0]) * places[2]
        heights = [height, height] + [part.shape[0] for part in extras[:1]]
        if extras:
            heights[1] += heights[2]
        outs, out_specs = zip(*[tall(height) for height in heights])
    return order.call(
        functools.partial(product_kernel, groups, cuts, places, len(extras)),
        list(outs),
        *[term[0] for term in terms],
        *[side for term in terms for side in term[1:3]],
        *added,
        *extras,
        scalars=(core,),
        grid=(tiles,),
        in_specs=[
            *[pl.BlockSpec((rows, tokens), lambda j: (half, 0)) for _ in terms],
            *[right_spec(k) for k in range(len(terms)) for _ in range(2)],
            *(pieces if added else []),
            *[tall(part.shape[0])[1] for part in extras],
        ],
        out_specs=list(out_specs),
        cost=tiles * 0.8 if places is None else tiles * 1.2,
        name="send_kernel" if places is None else "keep_kernel",
    )


def sum_kernel(whole, low_ref, arrived_ref, *refs):
    rows = low_ref.shape[0]
    extra = refs[0][...] + arrived_ref[rows:, :] if arrived_ref.shape[0] > rows else None
    outs = refs if extra is None else refs[1:]
    if whole:
        outs[0][...] = low_ref[...] + arrived_ref[:rows, :]
    else:
        half = rows // 2
        outs[0][...] = low_ref[:half, :] + arrived_ref[:half, :]
        outs[1][:half, :] = low_ref[half:, :] + arrived_ref[half:rows, :]
    if extra is not None:
        outs[-1][...] = extra
        if not whole:
            outs[1][rows // 2 :, :] = extra


def add_arrived(order, low, arrived, extra, whole):
    rows, width = low.shape
    beyond = arrived.shape[0] - rows
    heights = [rows] if whole else [rows // 2, rows // 2 + beyond]
    heights += [beyond] if beyond else []
    outs = order.call(
        functools.partial(sum_kernel, whole),
        [shaped((height, width), single) for height in heights],
        low,
        arrived,
        *([extra] if beyond else []),
        cost=0.7,
        name="add_kernel",
    )
    return outs if beyond else [*outs, None]


def scatter(order, core, terms, cuts, orders, size, extra=None):
    masks = [1 << k for k in range(1, size.bit_length() - 1)]
    count = len(masks)

    def place_of(side, block, dims):
        at = 0
        for dim in dims:
            bit = side if dim is None else (block >> (count - 1 - masks.index(dim))) & 1
            at = 2 * at + bit
        return at

    tables = [
        [[place_of(side, block, dims) for block in range(1 << count)] for side in range(2)]
        for dims in orders
    ]
    extras = () if extra is None else (extra,)
    sent = product(order, core, 1, terms, cuts, extras=extras)
    arrived = [swap_dp(part, 1, size) for part in sent]
    yield
    height = terms[0][0].shape[0] // size
    low, high, *extra = product(order, core, 0, terms, cuts, arrived, (*tables, height), extras)
    extra = extra[0] if extras else None
    for k in range(count + 1):
        arrived = swap_mixed(high, orders[0][k], orders[1][k], size)
        yield
        if k < count:
            low, high, extra = add_arrived(order, low, arrived, extra, False)
    total, extra = add_arrived(order, low, arrived, extra, True)
    yield (total, extra)


def relative_kernel(size, side_ref, me_ref, value_ref, out_ref, turned_ref):
    value = value_ref[side_ref[0]] if len(value_ref.shape) == 3 else value_ref[...]
    depth = value.shape[1]
    share = depth // size
    bits = size.bit_length() - 1
    me = me_ref[0]
    if share % 16 == 0:
        turned_ref[...] = value.T
        for p in range(size):
            block = pl.multiple_of((reverse_bits(p, bits) ^ me) * share, 16)
            out_ref[p * share : (p + 1) * share, :] = turned_ref[pl.ds(block, share), :]
        return
    tile = 96
    lanes = lax.broadcasted_iota(jnp.int32, (tile, depth), 1)
    local = lax.broadcasted_iota(jnp.int32, (tile, depth), 0)
    for j in range(0, depth, tile):
        source = jnp.zeros_like(local)
        for p in range(j // share, (j + tile) // share):
            here = (local >= p * share - j) & (local < (p + 1) * share - j)
            source = jnp.where(here, (reverse_bits(p, bits) ^ me) * share + local + (j - p * share), source)
        picks = jnp.where(lanes == source, 1.0, 0.0).astype(bfloat)
        out_ref[j : j + tile, :] = dot_cols(picks, value).astype(bfloat)


def relative(order, side, me, size, value):
    shape = value.shape[-2:][::-1]
    return order.call(
        functools.partial(relative_kernel, size),
        shaped(shape, bfloat),
        value,
        scalars=(side, me),
        scratch=[pltpu.VMEM(shape, bfloat)],
        cost=0.8,
        name="relative_kernel",
    )


def attend_kernel(side_ref, lengths_ref, inputs_ref, qkv_ref, bias_ref, start_ref, *refs):
    *out_w, parts_ref, chance_ref, context_ref, hidden_ref, turned_ref = refs
    tokens = inputs_ref.shape[1]
    local = qkv_ref.shape[2]
    side = side_ref[0]
    rows = inputs_ref[side]
    flat = bias_ref.shape[0] == 1
    for part in range(3):
        projected = dot(rows, qkv_ref[part])
        if part != 1:
            k = part // 2
            projected = projected + (bias_ref[:, k * local : (k + 1) * local] if flat else bias_ref[k : k + 1, :])
        parts_ref[part] = projected.astype(bfloat)
    tile = tokens
    visible = lax.broadcasted_iota(jnp.int32, (tokens, tile), 0) < lengths_ref[side]

    def pair_step(pair):
        at = pair * PAIR
        keys = parts_ref[1, :, pl.ds(at, PAIR)]
        queries = parts_ref[0, :, pl.ds(at, PAIR)].T
        values = parts_ref[2, :, pl.ds(at, PAIR)].T
        owner = lax.broadcasted_iota(jnp.int32, (PAIR, tile), 0) // HEAD_DIM
        for h in range(2):
            value_rows = values[h * HEAD_DIM : (h + 1) * HEAD_DIM]
            for q in range(tokens // tile):
                picked = queries[:, q * tile : (q + 1) * tile] * HEAD_DIM**-0.5
                picked = jnp.where(owner == h, picked, jnp.zeros_like(picked))
                scores = jnp.where(visible, dot(keys, picked), -1e9)
                raised = jnp.exp(scores - jnp.max(scores, axis=0, keepdims=True))
                chances = raised * (1.0 / jnp.sum(raised, axis=0, keepdims=True))
                chances = chances.astype(bfloat)
                chance_ref[pair * 2 + h, :, q * tile : (q + 1) * tile] = chances
                turned_ref[pl.ds(at + h * HEAD_DIM, HEAD_DIM), q * tile : (q + 1) * tile] = dot(value_rows, chances).astype(bfloat)

    for pair in range(local // PAIR):
        pair_step(pair)
    context = turned_ref[...].T
    context_ref[...] = context
    if out_w:
        hidden_ref[...] = rows.astype(single) + start_ref[...] + dot(context, out_w[0][...])
    else:
        middle = hidden_ref.shape[1] // 2
        hidden_ref[:, :middle] = start_ref[:, :middle] + dot(context, qkv_ref[3, :local, :])
        hidden_ref[:, middle:] = start_ref[:, middle:] + dot(context, qkv_ref[3, local:, :])


def attend(order, side, lengths, inputs, qkv, bias, start, out=None):
    tokens, width = inputs.shape[1:]
    local = qkv.shape[2]
    return order.call(
        attend_kernel,
        [
            shaped((3, tokens, local), bfloat),
            shaped((local // HEAD_DIM, tokens, tokens), bfloat),
            shaped((tokens, local), bfloat),
            shaped((tokens, width), single),
        ],
        inputs,
        qkv,
        bias,
        start,
        *([] if out is None else [out]),
        scalars=(side, lengths),
        scratch=[pltpu.VMEM((local, tokens), bfloat)],
        cost=6.6,
    )


def unit_of(hidden):
    centred = hidden - jnp.mean(hidden, axis=-1, keepdims=True)
    scale = lax.rsqrt(jnp.mean(centred * centred, axis=-1, keepdims=True) + norm_eps)
    return centred * scale, scale


def norm_back(upstream, unit, scale, gain):
    scaled = upstream * gain
    return scale * (
        scaled
        - jnp.mean(scaled, axis=-1, keepdims=True)
        - unit * jnp.mean(scaled * unit, axis=-1, keepdims=True)
    )


STRIP = 256


def strips(tokens, body):
    def step(j, carry):
        body(pl.ds(pl.multiple_of(j * STRIP, STRIP), STRIP))
        return carry

    lax.fori_loop(0, tokens // STRIP, step, 0)


def norm_kernel(hidden_ref, gain_ref, shift_ref, down_ref, low_ref, next_ref):
    def body(at):
        unit, _ = unit_of(hidden_ref[at, :])
        normed = unit * gain_ref[0:1, :] + shift_ref[0:1, :]
        low_ref[at, :] = normed.astype(bfloat)
        next_ref[at, :] = normed + down_ref[...]

    strips(hidden_ref.shape[0], body)


def gelu_tiles(normed_ref, into_ref, bias_ref, act_ref, slope_ref):
    tokens, hidden_units = normed_ref.shape[0], into_ref.shape[1]
    tile, height = 512, 128
    before = bias_ref.shape[1] - hidden_units
    for j in range(0, hidden_units, tile):
        at = pl.ds(j, tile)
        for k in range(0, tokens, height):
            strip = pl.ds(k, height)
            pre = dot(normed_ref[strip, :], into_ref[:, at]) + bias_ref[:, pl.ds(before + j, tile)]
            bell = jnp.exp(-0.5 * pre * pre)
            reach = 1.0 / (1.0 + 0.23164189 * jnp.abs(pre))
            tail = reach * (
                0.127414796
                + reach * (-0.142248368 + reach * (0.7107068705 + reach * (-0.7265760135 + reach * 0.5307027145)))
            )
            tail = tail * bell
            chance = jnp.where(pre >= 0, 1.0 - tail, tail)
            act_ref[strip, at] = (pre * chance).astype(bfloat)
            slope_ref[strip, at] = (chance + pre * bell * 0.3989422804014327).astype(bfloat)


def feed_kernel(normed_ref, into_ref, bias_ref, down_ref, start_ref, act_ref, slope_ref, hidden_ref):
    gelu_tiles(normed_ref, into_ref, bias_ref, act_ref, slope_ref)
    hidden_ref[...] = start_ref[...] + dot(act_ref[...], down_ref[...])


def feed(order, normed, into, bias, down, start):
    tokens, width = normed.shape
    units = into.shape[1]
    return order.call(
        feed_kernel,
        [shaped((tokens, units), bfloat), shaped((tokens, units), bfloat), shaped((tokens, width), single)],
        normed,
        into,
        bias,
        down,
        start,
        cost=4.4,
    )


def feed_up(order, normed, into, bias):
    units = into.shape[1]
    return order.call(
        gelu_tiles,
        [shaped((normed.shape[0], units), bfloat)] * 2,
        normed,
        into,
        bias,
        cost=4.0,
        name="feed_up_kernel",
    )


def add_columns(ref, row, value):
    ref[row : row + 1, :] += jnp.sum(value, axis=0, keepdims=True)


def turn_kernel(side_ref, act_ref, down_ref, start_ref, gain_ref, upstream_ref, grad_ref, sums_ref, unit_ref, branch_ref):
    sums_ref[...] = jnp.zeros_like(sums_ref)

    def body(at):
        unit, scale = unit_of(start_ref[at, :] + dot(act_ref[at, :], down_ref[...]))
        gain = gain_ref[1:2, :]
        upstream = upstream_ref[side_ref[0], at, :].astype(single)
        unit_ref[at, :] = unit
        grad = norm_back(upstream, unit, scale, gain)
        grad_ref[at, :] = grad
        branch_ref[at, :] = grad.astype(bfloat)
        add_columns(sums_ref, 0, upstream * unit)
        add_columns(sums_ref, 1, upstream)
        add_columns(sums_ref, 2, grad)

    strips(start_ref.shape[0], body)


def feed_back_kernel(branch_ref, down_ref, slope_ref, into_ref, start_ref, grad_ref, sums_ref, normed_ref):
    tile = 512
    for j in range(0, into_ref.shape[1], tile):
        at = pl.ds(j, tile)
        pre = dot_cols(branch_ref[...], down_ref[at, :]) * slope_ref[:, at].astype(single)
        low = pre.astype(bfloat)
        grad_ref[:, at] = low
        sums_ref[:, at] = jnp.sum(low.astype(single), axis=0, keepdims=True)
    normed_ref[...] = start_ref[...] + dot_cols(grad_ref[...], into_ref[...])


def feed_back(order, branch, down, slope, into, start):
    tokens, width = branch.shape
    units = into.shape[1]
    return order.call(
        feed_back_kernel,
        [shaped((tokens, units), bfloat), shaped((1, units), single), shaped((tokens, width), single)],
        branch,
        down,
        slope,
        into,
        start,
        cost=3.0,
    )


def norm_back_kernel(hidden_ref, gain_ref, upstream_ref, grad_ref, sums_ref, low_ref):
    sums_ref[...] = jnp.zeros_like(sums_ref)

    def body(at):
        unit, scale = unit_of(hidden_ref[at, :])
        upstream = upstream_ref[at, :]
        grad = norm_back(upstream, unit, scale, gain_ref[0:1, :])
        grad_ref[at, :] = grad
        low_ref[at, :] = grad.astype(bfloat)
        add_columns(sums_ref, 0, upstream * unit)
        add_columns(sums_ref, 1, upstream)
        add_columns(sums_ref, 2, grad)

    strips(hidden_ref.shape[0], body)


def attend_back_kernel(upstream_ref, parts_ref, chance_ref, qkv_ref, start_ref, *refs):
    *out_w, grad_ref, sums_ref, rows_ref, turned_ref = refs
    tokens = upstream_ref.shape[0]
    local = qkv_ref.shape[2]
    middle = upstream_ref.shape[1] // 2
    tile = tokens
    factor = HEAD_DIM**-0.5

    def pair_step(pair):
        at = pair * PAIR
        lanes = pl.ds(at, PAIR)
        queries = parts_ref[0, :, lanes]
        keys_turned = parts_ref[1, :, lanes].T
        values = parts_ref[2, :, lanes]
        if out_w:
            grad_context = dot_cols(upstream_ref[...], out_w[0][lanes, :])
        else:
            grad_context = dot_cols(upstream_ref[:, :middle], qkv_ref[3, lanes, :])
            grad_context = grad_context + dot_cols(
                upstream_ref[:, middle:], qkv_ref[3, pl.ds(local + at, PAIR), :]
            )
        grad_context = grad_context.astype(bfloat)
        context_turned = grad_context.T
        owner = lax.broadcasted_iota(jnp.int32, (PAIR, tile), 0) // HEAD_DIM
        first_lane = lax.broadcasted_iota(jnp.int32, (tokens, PAIR), 1) < HEAD_DIM
        grads_k, grads_v = [], []
        for h in range(2):
            key_rows = keys_turned[h * HEAD_DIM : (h + 1) * HEAD_DIM]
            grad_k = jnp.zeros((tokens, PAIR), single)
            grad_v = jnp.zeros((tokens, PAIR), single)
            for q in range(tokens // tile):
                cut = slice(q * tile, (q + 1) * tile)
                picked = context_turned[:, cut]
                picked = jnp.where(owner == h, picked, jnp.zeros_like(picked))
                chances_low = chance_ref[pair * 2 + h, :, cut]
                chances = chances_low.astype(single)
                grad_chances = dot(values, picked)
                inner = jnp.sum(chances * grad_chances, axis=0, keepdims=True)
                grad_scores = (chances * (grad_chances - inner)).astype(bfloat)
                grad_v = grad_v + dot(chances_low, grad_context[cut, :])
                grad_k = grad_k + dot(grad_scores, queries[cut, :])
                turned_ref[pl.ds(at + h * HEAD_DIM, HEAD_DIM), cut] = (dot(key_rows, grad_scores) * factor).astype(bfloat)
            grads_k.append(grad_k)
            grads_v.append(grad_v)
        grad_k = (jnp.where(first_lane, grads_k[0], grads_k[1]) * factor).astype(bfloat)
        grad_v = jnp.where(first_lane, grads_v[0], grads_v[1]).astype(bfloat)
        grad_ref[:, pl.ds(local + at, PAIR)] = grad_k
        grad_ref[:, pl.ds(2 * local + at, PAIR)] = grad_v

    for pair in range(local // PAIR):
        pair_step(pair)
    grad_ref[:, 0:local] = turned_ref[...].T
    sums_ref[...] = jnp.sum(grad_ref[...].astype(single), axis=0, keepdims=True)
    total = start_ref[...]
    for part in range(3):
        total = total + dot_cols(grad_ref[:, part * local : (part + 1) * local], qkv_ref[part])
    rows_ref[...] = total


def attend_back(order, upstream, parts, chances, qkv, start, out=None):
    tokens, width = upstream.shape
    local = qkv.shape[2]
    return order.call(
        attend_back_kernel,
        [shaped((tokens, 3 * local), bfloat), shaped((1, 3 * local), single), shaped((tokens, width), single)],
        upstream,
        parts,
        chances,
        qkv,
        start,
        *([] if out is None else [out]),
        scratch=[pltpu.VMEM((local, tokens), bfloat)],
        cost=7.4,
    )


def vectors_kernel(side_ref, first_ref, second_ref, units_own, units_other, proj_own, proj_other, out_ref):
    width = first_ref.shape[1]
    local = proj_own.shape[1] // 3
    out_ref[...] = jnp.zeros_like(out_ref)
    out_ref[0:3, :] = first_ref[...]
    out_ref[3:6, :] = second_ref[...]
    swapped = side_ref[0] == 1
    for row, units, proj in (
        (6, (units_own, units_other), (proj_own, proj_other)),
        (9, (units_other, units_own), (proj_other, proj_own)),
    ):
        both = jnp.where(swapped, units[1][...], units[0][...])
        for k in range(2):
            out_ref[row + k : row + k + 1, :] = both[:, k * width : (k + 1) * width]
        parts = jnp.where(swapped, proj[1][...], proj[0][...])
        out_ref[row + 2 : row + 3, :local] = parts[:, :local]
        out_ref[row + 2 : row + 3, local : 2 * local] = parts[:, 2 * local :]


def both_result_kernel(side_ref, mine_ref, other_ref, gain_ref, shift_ref, out_ref):
    side = side_ref[0]

    def body(at):
        for place, ref in ((side, mine_ref), (1 - side, other_ref)):
            out_ref[place, at, :] = (ref[at, :] * gain_ref[1:2, :] + shift_ref[1:2, :]).astype(bfloat)

    strips(mine_ref.shape[0], body)


def both_kernel(side_ref, mine_ref, other_ref, out_ref):
    side = side_ref[0]
    out_ref[side] = mine_ref[...]
    out_ref[1 - side] = other_ref[...]


def shares_kernel(rank_ref, qkv_ref, out_ref, left_ref, right_ref, down_ref, last_ref, heads_ref, feed_ref, direct_ref):
    heads_ref[0, 0:3] = qkv_ref[...].astype(single)
    heads_ref[0, 3] = out_ref[...].astype(single)
    depth = left_ref.shape[0]
    feed_ref[0:depth, :] = left_ref[...].astype(single)
    feed_ref[depth : 2 * depth, :] = right_ref[...].astype(single)
    feed_ref[2 * depth :, :] = down_ref[...].astype(single)
    direct_ref[0, 0] = last_ref[...].astype(single)


def small_kernel(bias_ref, units_ref, small_ref):
    local = bias_ref.shape[1]
    small_ref[:, 0:local] = bias_ref[0:1, :]
    small_ref[:, local : 2 * local] = bias_ref[1:2, :]
    small_ref[:, 2 * local :] = units_ref[...]


def shares(rank, qkv, out, into, down):
    width, local, hidden = qkv.shape[1], qkv.shape[2], into.shape[1]
    depth = width // 8
    quarters = local // depth
    rows, last = hidden // 12, hidden // 6
    shapes = [(1, 4, depth, local), (2 * depth + rows, width), (1, 1, last, width)]
    return pl.pallas_call(
        shares_kernel,
        grid_spec=pltpu.PrefetchScalarGridSpec(
            num_scalar_prefetch=1,
            grid=(1,),
            in_specs=[
                pl.BlockSpec((3, depth, local), lambda j, r: (0, r[0], 0)),
                pl.BlockSpec((depth, local), lambda j, r: (r[0] % quarters, r[0] // quarters)),
                pl.BlockSpec((depth, width), lambda j, r: (r[0], 0)),
                pl.BlockSpec((depth, width), lambda j, r: (r[0], 1)),
                pl.BlockSpec((rows, width), lambda j, r: (r[0], 0)),
                pl.BlockSpec((last, width), lambda j, r: (4 + r[0] % 2, 0)),
            ],
            out_specs=[pl.BlockSpec(shape, lambda j, r, n=len(shape): (0,) * n) for shape in shapes],
        ),
        out_shape=[shaped(shape, single) for shape in shapes],
        cost_estimate=pl.CostEstimate(flops=1000, bytes_accessed=1000, transcendentals=0),
    )(rank, qkv, out, into, into, down, down)


SCHEDULE = [8.0, 2.0, "ao", "ss", 20.0, "tH", "H", "tF", 2.0, "rr", "H", "H", "I", "sm", 10.0, "pH", "D", "at", "no", 5.0, "rn", "I", "I", 2.0, 10.0, "D", "tX", "fo", "D", "pI", "ff", 20.0, "pD", "tu", "rb", "sd", "bf", "d", "bo", "si", "nb", "ba", "i", "ra", "d", "bs", "sq", 20.0, "u", 30.0, 2.0, "d", "q", 10.0, "i", 20.0, "d", "q", "d", "i", "br", "q", 20.0, 20.0, "i", "g", "q", "i", "bg", "dr"]
KINDS = ["zwyx/xyzw", "yzxw/zwyx", "zwyx/yzwx", "zwyx/yzwx", "xyzw/yzwx", "xyzw/yzwx"]
CUTS = [4, 4, 4, 4, 4, 4]
SPLITS = [1, 1, 1]


def body(
    inputs,
    lengths,
    w_qkv,
    b_qv,
    w_out,
    b_out,
    ln_gains,
    ln_biases,
    w_in,
    b_in,
    w_down,
    b_down,
    cotangent,
):
    size = lax.axis_size("dp")
    me = lax.axis_index("dp")
    side = lax.axis_index("tensor")
    side_index = side.astype(jnp.int32).reshape(1)
    tokens, width = inputs.shape[1:]
    local = w_qkv.shape[2]
    units = w_in.shape[1]
    order = Order()

    rank, core = me & 7, me & 1
    core_index = core.astype(jnp.int32).reshape(1)
    me_index = me.astype(jnp.int32).reshape(1)
    qkv_own = jnp.transpose(w_qkv, (1, 0, 2))
    depth = width // 8
    heads_share, feed_share, direct_share = shares(rank.astype(jnp.int32).reshape(1), qkv_own, w_out, w_in, w_down)
    heads_share = swap_x(heads_share)
    feed_share = swap_x(feed_share)
    direct_share = swap_x(direct_share)

    dims = [1 << k for k in range(1, size.bit_length() - 1)]
    letters = {"x": [None], "y": dims[:1], "z": dims[1:2], "w": dims[2:]}

    def kind(k):
        return [[dim for letter in word for dim in letters[letter]] for word in KINDS[k].split("/")]

    chains = {}
    v = types.SimpleNamespace()

    def step(name):
        return lambda: chains[name].step()

    def attend_own():
        v.own = attend(order, side_index, lengths, inputs, qkv_own, b_qv, b_out.reshape(1, -1), w_out)

    def send_small():
        hidden = b_in.reshape(1, -1)
        v.small_own = order.call(small_kernel, shaped((1, 2 * local + units), single), b_qv, hidden, cost=0.3)
        v.small_sent = swap_x(v.small_own)

    def take_small():
        v.small = order.pin(v.small_sent)

    def take_heads():
        chains["H"] = Chain(fetch_spread(order, order.pin(heads_share), size, 2.0))
        chains["H"].step()

    def take_feed():
        into_share, down_share = order.call(
            unpack_kernel,
            [shaped((1, 2, depth, width), single), shaped((1, 1, units // 12, width), single)],
            feed_share,
            cost=10.0,
        )
        chains["I"] = Chain(fetch_spread(order, into_share, size, 8.0))
        chains["D"] = Chain(fetch_spread(order, down_share, size, 8.0))
        chains["I"].step()
        chains["D"].step()

    def take_direct():
        chains["X"] = Chain(fetch_direct(order, direct_share, size, units // 3 * 2))
        chains["X"].step()

    def place_heads():
        v.w_heads = place(order, me_index, [chains["H"].value], (4, width, local))

    def place_in():
        v.w_in = place(order, me_index, [chains["I"].value], w_in.shape)

    def place_down():
        v.w_down = place(order, me_index, [chains["D"].value, chains["X"].value], w_down.shape)

    def relative_rows():
        v.rows_rel = relative(order, side_index, me_index, size, inputs)

    def attend_other():
        v.other = attend(order, side_index, lengths, inputs, v.w_heads, v.small, v.own[3])

    def norm():
        v.normed, v.two_start = order.call(
            norm_kernel,
            [shaped((tokens, width), bfloat), shaped((tokens, width), single)],
            v.other[3],
            ln_gains,
            ln_biases,
            b_down.reshape(1, -1),
        )

    def feed_own():
        v.act_own, v.slope_own, v.two_own = feed(
            order, v.normed, w_in, b_in.reshape(1, -1), w_down, v.two_start
        )

    def feed_other():
        v.act, v.slope = feed_up(order, v.normed, v.w_in, v.small)

    def relative_normed():
        v.normed_rel = relative(order, side_index, me_index, size, v.normed)

    def turn():
        v.grad_two, v.sums_two, v.unit, v.branch = order.call(
            turn_kernel,
            [
                shaped((tokens, width), single),
                shaped((3, width), single),
                shaped((tokens, width), single),
                shaped((tokens, width), bfloat),
            ],
            v.act,
            v.w_down,
            v.two_own,
            ln_gains,
            cotangent,
            scalars=(side_index,),
            cost=2.6,
        )
        v.unit_other = swap_x(v.unit)

    def start(name, k, terms, extra=None):
        chains[name] = Chain(scatter(order, core_index, terms, CUTS[k], kind(k), size, extra))
        chains[name].step()

    def piece(count, k):
        return k * units // count, units // count

    def relative_branch():
        v.branch_rel = relative(order, side_index, me_index, size, v.branch)

    def start_down(k):
        return lambda: start("de"[k], k, [(v.branch_rel, v.act_own, v.act, *piece(SPLITS[0], k))])

    def feed_back_other():
        v.pre, v.units_sum, v.grad_other = feed_back(
            order, v.branch, v.w_down, v.slope, v.w_in, v.grad_two
        )

    def feed_back_own():
        v.pre_own, v.units_sum_own, v.grad = feed_back(
            order, v.branch, w_down, v.slope_own, w_in, v.grad_other
        )

    def start_into(k):
        return lambda: start("ij"[k], 2 + k, [(v.normed_rel, v.pre_own, v.pre, *piece(SPLITS[1], k))])

    def norm_two():
        v.grad_one, v.sums_one, v.attended = order.call(
            norm_back_kernel,
            [shaped((tokens, width), single), shaped((3, width), single), shaped((tokens, width), bfloat)],
            v.other[3],
            ln_gains,
            v.grad,
            cost=1.5,
        )

    def relative_attended():
        v.attended_rel = relative(order, side_index, me_index, size, v.attended)

    def attend_back_other():
        v.proj, v.proj_sum, v.rows_other = attend_back(
            order, v.attended, v.other[0], v.other[1], v.w_heads, v.grad_one
        )

    def attend_back_own():
        v.proj_own, v.proj_sum_own, v.grad_rows = attend_back(
            order, v.attended, v.own[0], v.own[1], qkv_own, v.rows_other, w_out
        )
        v.grad_other_rows = swap_x(v.grad_rows)

    def start_out():
        terms = [
            (v.attended_rel, v.own[2], v.other[2], 0, local),
            (v.rows_rel, v.proj_own, v.proj, 0, local),
        ]
        start("p", 4, terms)

    def start_project():
        vectors = order.call(
            vectors_kernel,
            shaped((16, width), single),
            v.sums_one,
            v.sums_two,
            v.units_sum_own,
            v.units_sum,
            v.proj_sum_own,
            v.proj_sum,
            scalars=(side_index,),
            cost=0.5,
        )
        terms = [(v.rows_rel, v.proj_own, v.proj, local, 2 * local)]
        if SPLITS[2] == 1:
            terms = [
                (v.attended_rel, v.own[2], v.other[2], 0, local),
                (v.rows_rel, v.proj_own, v.proj, 0, 3 * local),
            ]
            vectors = jnp.concatenate([vectors[:8], vectors[8:]], axis=1)
        start("q", 5, terms, vectors)

    def take_unit():
        v.unit_other = order.pin(v.unit_other)

    def take_grad():
        v.grad_other_rows = order.pin(v.grad_other_rows)

    def both_results():
        v.results = order.call(
            both_result_kernel,
            shaped((2, tokens, width), bfloat),
            v.unit,
            v.unit_other,
            ln_gains,
            ln_biases,
            scalars=(side_index,),
            cost=1.5,
        )

    def both_grads():
        v.grads = order.call(
            both_kernel,
            shaped((2, tokens, width), single),
            v.grad_rows,
            v.grad_other_rows,
            scalars=(side_index,),
            cost=2.0,
        )

    def drain():
        last = list(chains.values())[-sum(SPLITS) :]
        while any(chain.value is None for chain in last):
            for chain in last:
                if chain.value is None:
                    chain.step()

    steps = {
        "ao": attend_own,
        "ss": send_small,
        "sm": take_small,
        "tH": take_heads,
        "tF": take_feed,
        "tX": take_direct,
        "H": step("H"),
        "I": step("I"),
        "D": step("D"),
        "pH": place_heads,
        "pI": place_in,
        "pD": place_down,
        "rr": relative_rows,
        "at": attend_other,
        "no": norm,
        "fo": feed_own,
        "ff": feed_other,
        "rn": relative_normed,
        "tu": turn,
        "rb": relative_branch,
        "sd": start_down(0),
        "se": start_down(1),
        "bf": feed_back_other,
        "bo": feed_back_own,
        "si": start_into(0),
        "sj": start_into(1),
        "nb": norm_two,
        "ra": relative_attended,
        "ba": attend_back_other,
        "bs": attend_back_own,
        "sp": start_out,
        "sq": start_project,
        **{name: step(name) for name in "deijpq"},
        "u": take_unit,
        "g": take_grad,
        "br": both_results,
        "bg": both_grads,
        "dr": drain,
    }
    for name in SCHEDULE:
        if isinstance(name, str):
            steps[name]()
        else:
            order.pad(float(name))
    results, grads = v.results, v.grads
    parts = [[chains[name].value[0] for name in names if name in chains] for names in ("de", "ij", "pq")]
    share_down, share_in, share_project = (jnp.concatenate(part, axis=1) for part in parts)
    share_out, share_qkv = share_project[:, :local], share_project[:, local:]
    sums = chains["q"].value[1]
    if SPLITS[2] == 1:
        sums = jnp.concatenate([sums[:, :width], sums[:, width:]], axis=0)
    mine = jnp.where(side == 0, sums[6:9], sums[9:12])

    return (
        results,
        grads,
        share_qkv.reshape(-1, 3, local),
        mine[2].reshape(2, local),
        share_out.T,
        sums[2],
        jnp.stack([sums[0], sums[3]]),
        jnp.stack([sums[1], sums[4]]),
        share_in,
        mine[:2].reshape(-1),
        share_down.T,
        sums[5],
    )


def solution(mesh):
    placed = (
        P("dp", None, None),
        P("dp"),
        P(None, None, "tensor"),
        P(None, "tensor"),
        P("tensor", None),
        P(),
        P(),
        P(),
        P(None, "tensor"),
        P("tensor"),
        P("tensor", None),
        P(),
        P("dp", None, None),
    )
    return jax.shard_map(
        body,
        mesh=mesh,
        in_specs=placed,
        out_specs=(
            P("dp", None, None),
            P("dp", None, None),
            P("dp", None, "tensor"),
            P(None, "tensor"),
            P("tensor", "dp"),
            P(),
            P(),
            P(),
            P("dp", "tensor"),
            P("tensor"),
            P("tensor", "dp"),
            P(),
        ),
        check_vma=False,
    )
```

```python
import functools
import types

import jax
import jax.numpy as jnp
from jax import lax
from jax.experimental import pallas as pl
from jax.experimental.pallas import tpu as pltpu
from jax.sharding import PartitionSpec as P

HEAD_DIM = 64
PAIR = 2 * HEAD_DIM
norm_eps = 1e-12
bfloat = jnp.bfloat16
single = jnp.float32
MIB = 1 << 20
COST_UNIT = 1.0e9


def dot(left, right):
    return jnp.dot(left, right, preferred_element_type=single)


def dot_cols(left, right):
    return lax.dot_general(
        left, right, (((1,), (1,)), ((), ())), preferred_element_type=single
    )


def shaped(shape, dtype):
    return jax.ShapeDtypeStruct(shape, dtype)


def nothing_kernel(out_ref):
    out_ref[...] = jnp.zeros_like(out_ref)


class Order:
    def __init__(self):
        self.last = None

    def call(self, kernel, outs, *args, scalars=(), scratch=(), grid=(), in_specs=None, out_specs=None, limit=16, aliases=None, cost=1.0, name=None):
        many = isinstance(outs, (tuple, list))
        if in_specs is None:
            in_specs = [pl.BlockSpec(memory_space=pltpu.VMEM)] * len(args)
        if out_specs is None:
            out_specs = [pl.BlockSpec(memory_space=pltpu.VMEM)] * len(outs) if many else pl.BlockSpec(memory_space=pltpu.VMEM)
        in_specs = [pl.BlockSpec(memory_space=pltpu.SMEM)] * len(scalars) + list(in_specs)
        operands = list(scalars) + list(args)
        run = kernel
        if self.last is not None:
            before = len(operands)
            operands.append(self.last)
            in_specs.append(pl.BlockSpec(memory_space=pl.ANY))

            def run(*refs):
                kernel(*refs[:before], *refs[before + 1 :])

        made = pl.pallas_call(
            run,
            out_shape=outs,
            grid=grid,
            in_specs=in_specs,
            out_specs=out_specs,
            scratch_shapes=list(scratch),
            name=name or kernel.__name__,
            input_output_aliases=aliases or {},
            compiler_params=pltpu.CompilerParams(vmem_limit_bytes=limit * MIB),
            cost_estimate=pl.CostEstimate(flops=int(cost * COST_UNIT), bytes_accessed=1000, transcendentals=0),
        )(*operands)
        self.last = made[-1] if many else made
        return made

    def pad(self, cost):
        self.call(nothing_kernel, shaped((8, 128), single), cost=cost)

    def pin(self, value):
        return self.call(
            lambda *refs: None,
            shaped(value.shape, value.dtype),
            value,
            in_specs=[pl.BlockSpec(memory_space=pl.ANY)],
            out_specs=pl.BlockSpec(memory_space=pl.ANY),
            aliases={0: 0},
            cost=0.0,
            name="pin_kernel",
        )


class Chain:
    def __init__(self, steps):
        self.steps = steps
        self.value = None

    def step(self):
        self.value = next(self.steps, self.value)
        return self.value

    def run(self, count):
        for _ in range(count):
            self.step()


def swap_dp(value, mask, size):
    return lax.ppermute(value, "dp", [(i, i ^ mask) for i in range(size)])


def swap_x(value):
    return lax.ppermute(value, "tensor", [(0, 1), (1, 0)])


def reverse_bits(position, bits):
    out = 0
    for k in range(bits):
        out |= ((position >> k) & 1) << (bits - 1 - k)
    return out


def place_kernel(starts, me_ref, *refs):
    out_ref = refs[-1]
    me = me_ref[0]
    at = 0
    for piece in refs[:-1]:
        height = piece.shape[2]
        for b in range(piece.shape[0]):
            start = pl.multiple_of(starts[at](me), 16)
            for c in range(piece.shape[1]):
                if out_ref.ndim == 3:
                    out_ref[c, pl.ds(start, height), :] = piece[b, c].astype(out_ref.dtype)
                else:
                    lanes = slice(c * piece.shape[3], (c + 1) * piece.shape[3])
                    out_ref[pl.ds(start, height), lanes] = piece[b, c].astype(out_ref.dtype)
            at += 1


def place(order, me, parts, shape):
    pieces, starts = [], []
    for held, begin in parts:
        pieces += held
        starts += begin
    kernel = functools.partial(place_kernel, tuple(starts))
    return order.call(kernel, shaped(shape, bfloat), *pieces, scalars=(me,), cost=2.4, name="place_kernel")


def pack_kernel(first_ref, second_ref, out_ref):
    out_ref[0] = first_ref[0]
    out_ref[1] = second_ref[0]


def swap_mixed(value, first, second, size):
    pairs = []
    for d in range(size):
        mask = second if d & 1 else first
        for t in range(2):
            to = (d, 1 - t) if mask is None else (d ^ mask, t)
            pairs.append((2 * d + t, 2 * to[0] + to[1]))
    return lax.ppermute(value, ("dp", "tensor"), pairs)


def fetch_spread(order, held, size, pack_cost):
    arrived = swap_mixed(held, 4, 2, size)
    yield
    both = order.call(pack_kernel, shaped((2,) + held.shape[1:], single), held, arrived, cost=pack_cost)
    arrived = swap_mixed(both, 2, 4, size)
    both_core = swap_dp(both, 1, size)
    yield
    both_core = order.pin(both_core)
    yield
    arrived = order.pin(arrived)
    arrived_core = swap_dp(arrived, 1, size)
    rows = held.shape[-2]

    def start(even, odd, flip):
        return lambda index: ((index & 7) ^ flip ^ jnp.where(index & 1 == flip, even, odd)) * rows

    offsets = list(zip((0, 4, 2, 6), (0, 2, 4, 6)))
    yield [both, arrived, both_core, arrived_core], [
        start(even, odd, flip) for flip in range(2) for even, odd in offsets
    ]


def fetch_direct(order, held, size, base):
    held = order.pin(held)
    rows = held.shape[-2]
    yield [held, swap_dp(held, 1, size)], [
        lambda index: base + (index & 1) * rows,
        lambda index: base + (1 - (index & 1)) * rows,
    ]


def unpack_kernel(all_ref, into_ref, down_ref):
    rows = into_ref.shape[2]
    for c in range(2):
        into_ref[0, c] = all_ref[c * rows : (c + 1) * rows, :]
    down_ref[0, 0] = all_ref[2 * rows :, :]


def product_kernel(groups, sides, cuts, places, extras, core_ref, *refs):
    lefts, rights = refs[: len(groups)], refs[len(groups) : (1 + sides) * len(groups)]
    rest = refs[(1 + sides) * len(groups) :]
    tile = pl.program_id(0)
    first = core_ref[0] == 0

    def spread(side, total, low_ref, high_ref, table, height):
        half = len(table[0])
        for block in range(half):
            at = table[side][block]
            out_ref, at = (low_ref, at) if at < half else (high_ref, at - half)
            out_ref[at * height : (at + 1) * height, :] = total[block * height : (block + 1) * height]

    def run(k, j):
        for side in range(sides):
            total = dot(lefts[k][...], rights[sides * k + side][...])
            rows = total.shape[0]
            cut = side * cuts + j * cuts // sum(groups)
            if places is None:
                rest[extras + cut][:rows, :] = total
                if extras:
                    rest[extras + cut][rows:, :] = rest[0][...]
                continue
            total = total + rest[cut][:rows, :]
            low_ref, high_ref = rest[sides * cuts + extras :][:2]
            even, odd, height = places
            pl.when(first)(lambda: spread(side, total, low_ref, high_ref, even, height))
            pl.when(jnp.logical_not(first))(lambda: spread(side, total, low_ref, high_ref, odd, height))
            if extras and side == 0:
                extra = rest[sides * cuts][...] + rest[cut][rows:, :]
                rest[-1][...] = extra
                high_ref[low_ref.shape[0] :, :] = extra

    j = 0
    for k, tiles in enumerate(groups):
        for _ in range(tiles):
            pl.when(tile == j)(functools.partial(run, k, j))
            j += 1


def product(order, core, half, terms, cuts, added=(), places=None, extras=()):
    rows = terms[0][0].shape[0] // 2
    tokens = terms[0][0].shape[1]
    sides = len(terms[0][1])
    tile = 768 if all(term[2] % 768 == 0 and term[3] % 768 == 0 for term in terms) else 384
    groups = tuple(term[3] // tile for term in terms)
    begins = [sum(groups[:k]) for k in range(len(groups))]
    tiles = sum(groups)

    def right_spec(k):
        first = terms[k][2] // tile
        return pl.BlockSpec((tokens, tile), lambda j: (0, first + jnp.clip(j - begins[k], 0, groups[k] - 1)))

    def tall(height):
        return shaped((height, tiles * tile), single), pl.BlockSpec((height, tile), lambda j: (0, j))

    each = tiles // cuts
    beyond = sum(part.shape[0] for part in extras)
    heights = [rows + (beyond if side == 0 else 0) for side in range(sides) for _ in range(cuts)]
    pieces = [
        pl.BlockSpec((height, tile), lambda j, k=k % cuts: (0, jnp.clip(j - k * each, 0, each - 1)))
        for k, height in enumerate(heights)
    ]
    if places is None:
        outs, out_specs = [shaped((height, each * tile), single) for height in heights], pieces
    else:
        height = len(places[0][0]) * places[2]
        heights = [height, height + beyond] + ([beyond] if extras else [])
        outs, out_specs = zip(*[tall(height) for height in heights])
    return order.call(
        functools.partial(product_kernel, groups, sides, cuts, places, len(extras)),
        list(outs),
        *[term[0] for term in terms],
        *[right for term in terms for right in term[1]],
        *added,
        *extras,
        scalars=(core,),
        grid=(tiles,),
        in_specs=[
            *[pl.BlockSpec((rows, tokens), lambda j: (half, 0)) for _ in terms],
            *[right_spec(k) for k in range(len(terms)) for _ in range(sides)],
            *(pieces if added else []),
            *[tall(part.shape[0])[1] for part in extras],
        ],
        out_specs=list(out_specs),
        cost=sides * tiles * tile / 384 * (0.4 if places is None else 0.6),
        name="send_kernel" if places is None else "keep_kernel",
    )


def sum_kernel(whole, low_ref, arrived_ref, *refs):
    rows = low_ref.shape[0]
    extra = refs[0][...] + arrived_ref[rows:, :] if arrived_ref.shape[0] > rows else None
    outs = refs if extra is None else refs[1:]
    if whole:
        outs[0][...] = low_ref[...] + arrived_ref[:rows, :]
    else:
        half = rows // 2
        outs[0][...] = low_ref[:half, :] + arrived_ref[:half, :]
        outs[1][:half, :] = low_ref[half:, :] + arrived_ref[half:rows, :]
    if extra is not None:
        outs[-1][...] = extra
        if not whole:
            outs[1][rows // 2 :, :] = extra


def add_arrived(order, low, arrived, extra, whole=False):
    rows, width = low.shape
    beyond = arrived.shape[0] - rows
    heights = [rows] if whole else [rows // 2, rows // 2 + beyond]
    heights += [beyond] if beyond else []
    outs = order.call(
        functools.partial(sum_kernel, whole),
        [shaped((height, width), single) for height in heights],
        low,
        arrived,
        *([extra] if beyond else []),
        cost=0.7,
        name="add_kernel",
    )
    return outs if beyond else [*outs, None]


def scatter(order, core, terms, cuts, orders, size, finish, extra=None, apart=False):
    masks = [1 << k for k in range(1, size.bit_length() - 1)]
    count = len(masks)

    def place_of(side, block, dims):
        at = 0
        for dim in dims:
            bit = side if dim is None else (block >> (count - 1 - masks.index(dim))) & 1
            at = 2 * at + bit
        return at

    tables = [
        [[place_of(side, block, dims) for block in range(1 << count)] for side in range(2)]
        for dims in orders
    ]
    def send(sides, extras):
        sent = product(order, core, 1, terms(sides), cuts, extras=extras)
        return [swap_dp(part, 1, size) for part in sent]

    if apart:
        arrived = send((1,), ())
        yield
        extras = () if extra is None else (extra(),)
        arrived = send((0,), extras) + arrived
    else:
        extras = ()
        arrived = send((0, 1), extras)
    terms = terms((0, 1))
    yield
    height = terms[0][0].shape[0] // size
    low, high, *extra = product(order, core, 0, terms, cuts, arrived, (*tables, height), extras)
    extra = extra[0] if extras else None
    for k in range(count + 1):
        arrived = swap_mixed(high, orders[0][k], orders[1][k], size)
        yield
        if k < count:
            low, high, extra = add_arrived(order, low, arrived, extra)
    yield finish(low, arrived, extra)


def last_kernel(side_ref, low_ref, arrived_ref, extra_ref, qkv_ref, out_ref, gains_ref, shifts_ref, *vectors):
    b_out_ref, b_in_ref, b_down_ref, b_qv_ref = vectors
    rows = low_ref.shape[0]
    local = qkv_ref.shape[2]
    width = gains_ref.shape[1]
    total = low_ref[...] + arrived_ref[:rows, :]
    out_ref[...] = total[:, :local]
    for k in range(3):
        qkv_ref[k] = total[:, (k + 1) * local : (k + 2) * local]
    sums = extra_ref[...] + arrived_ref[rows:, :]
    for k in range(2):
        half = slice(k * width, (k + 1) * width)
        gains_ref[k : k + 1, :] = sums[0:1, half]
        shifts_ref[k : k + 1, :] = sums[1:2, half]
    b_out_ref[...] = sums[2, :width]
    b_down_ref[...] = sums[2, width:]
    first = side_ref[0] == 0
    b_in_ref[...] = jnp.where(first, sums[3, :], sums[5, :])
    parts = jnp.where(first, sums[4:5, :], sums[6:7, :])
    b_qv_ref[0:1, :] = parts[:, :local]
    b_qv_ref[1:2, :] = parts[:, local : 2 * local]


def relative_kernel(size, side_ref, me_ref, value_ref, out_ref, turned_ref):
    value = value_ref[side_ref[0]] if len(value_ref.shape) == 3 else value_ref[...]
    depth = value.shape[1]
    share = depth // size
    bits = size.bit_length() - 1
    me = me_ref[0]
    if share % 16 == 0:
        turned_ref[...] = value.T
        for p in range(size):
            block = pl.multiple_of((reverse_bits(p, bits) ^ me) * share, 16)
            out_ref[p * share : (p + 1) * share, :] = turned_ref[pl.ds(block, share), :]
        return
    tile = 96
    lanes = lax.broadcasted_iota(jnp.int32, (tile, depth), 1)
    local = lax.broadcasted_iota(jnp.int32, (tile, depth), 0)
    for j in range(0, depth, tile):
        source = jnp.zeros_like(local)
        for p in range(j // share, (j + tile) // share):
            here = (local >= p * share - j) & (local < (p + 1) * share - j)
            source = jnp.where(here, (reverse_bits(p, bits) ^ me) * share + local + (j - p * share), source)
        picks = jnp.where(lanes == source, 1.0, 0.0).astype(bfloat)
        out_ref[j : j + tile, :] = dot_cols(picks, value).astype(bfloat)


def relative(order, side, me, size, value):
    shape = value.shape[-2:][::-1]
    return order.call(
        functools.partial(relative_kernel, size),
        shaped(shape, bfloat),
        value,
        scalars=(side, me),
        scratch=[pltpu.VMEM(shape, bfloat)],
        cost=0.8,
        name="relative_kernel",
    )


def attend_kernel(side_ref, lengths_ref, inputs_ref, qkv_ref, bias_ref, start_ref, *refs):
    *out_w, parts_ref, chance_ref, context_ref, hidden_ref, turned_ref = refs
    tokens = inputs_ref.shape[1]
    local = qkv_ref.shape[2]
    side = side_ref[0]
    rows = inputs_ref[side]
    flat = bias_ref.shape[0] == 1
    for part in range(3):
        projected = dot(rows, qkv_ref[part])
        if part != 1:
            k = part // 2
            projected = projected + (bias_ref[:, k * local : (k + 1) * local] if flat else bias_ref[k : k + 1, :])
        parts_ref[part] = projected.astype(bfloat)
    tile = tokens
    visible = lax.broadcasted_iota(jnp.int32, (tokens, tile), 0) < lengths_ref[side]

    def pair_step(pair):
        at = pair * PAIR
        keys = parts_ref[1, :, pl.ds(at, PAIR)]
        queries = parts_ref[0, :, pl.ds(at, PAIR)].T
        values = parts_ref[2, :, pl.ds(at, PAIR)].T
        owner = lax.broadcasted_iota(jnp.int32, (PAIR, tile), 0) // HEAD_DIM
        for h in range(2):
            value_rows = values[h * HEAD_DIM : (h + 1) * HEAD_DIM]
            for q in range(tokens // tile):
                picked = queries[:, q * tile : (q + 1) * tile] * HEAD_DIM**-0.5
                picked = jnp.where(owner == h, picked, jnp.zeros_like(picked))
                scores = jnp.where(visible, dot(keys, picked), -1e9)
                raised = jnp.exp(scores - jnp.max(scores, axis=0, keepdims=True))
                chances = raised * (1.0 / jnp.sum(raised, axis=0, keepdims=True))
                chances = chances.astype(bfloat)
                chance_ref[pair * 2 + h, :, q * tile : (q + 1) * tile] = chances
                turned_ref[pl.ds(at + h * HEAD_DIM, HEAD_DIM), q * tile : (q + 1) * tile] = dot(value_rows, chances).astype(bfloat)

    for pair in range(local // PAIR):
        pair_step(pair)
    context = turned_ref[...].T
    context_ref[...] = context
    if out_w:
        hidden_ref[...] = rows.astype(single) + start_ref[...] + dot(context, out_w[0][...])
    else:
        middle = hidden_ref.shape[1] // 2
        hidden_ref[:, :middle] = start_ref[:, :middle] + dot(context, qkv_ref[3, :local, :])
        hidden_ref[:, middle:] = start_ref[:, middle:] + dot(context, qkv_ref[3, local:, :])


def attend(order, side, lengths, inputs, qkv, bias, start, out=None):
    tokens, width = inputs.shape[1:]
    local = qkv.shape[2]
    return order.call(
        attend_kernel,
        [
            shaped((3, tokens, local), bfloat),
            shaped((local // HEAD_DIM, tokens, tokens), bfloat),
            shaped((tokens, local), bfloat),
            shaped((tokens, width), single),
        ],
        inputs,
        qkv,
        bias,
        start,
        *([] if out is None else [out]),
        scalars=(side, lengths),
        scratch=[pltpu.VMEM((local, tokens), bfloat)],
        cost=6.6,
    )


def unit_of(hidden):
    centred = hidden - jnp.mean(hidden, axis=-1, keepdims=True)
    scale = lax.rsqrt(jnp.mean(centred * centred, axis=-1, keepdims=True) + norm_eps)
    return centred * scale, scale


def norm_back(upstream, unit, scale, gain):
    scaled = upstream * gain
    return scale * (
        scaled
        - jnp.mean(scaled, axis=-1, keepdims=True)
        - unit * jnp.mean(scaled * unit, axis=-1, keepdims=True)
    )


STRIP = 256


def strips(tokens, body):
    def step(j, carry):
        body(pl.ds(pl.multiple_of(j * STRIP, STRIP), STRIP))
        return carry

    lax.fori_loop(0, tokens // STRIP, step, 0)


def norm_kernel(hidden_ref, gain_ref, shift_ref, down_ref, low_ref, next_ref):
    def body(at):
        unit, _ = unit_of(hidden_ref[at, :])
        normed = unit * gain_ref[0:1, :] + shift_ref[0:1, :]
        low_ref[at, :] = normed.astype(bfloat)
        next_ref[at, :] = normed + down_ref[...]

    strips(hidden_ref.shape[0], body)


def gelu_tiles(normed_ref, into_ref, bias_ref, act_ref, slope_ref):
    tokens, hidden_units = normed_ref.shape[0], into_ref.shape[1]
    tile, height = 512, 128
    before = bias_ref.shape[1] - hidden_units
    for j in range(0, hidden_units, tile):
        at = pl.ds(j, tile)
        for k in range(0, tokens, height):
            strip = pl.ds(k, height)
            pre = dot(normed_ref[strip, :], into_ref[:, at]) + bias_ref[:, pl.ds(before + j, tile)]
            bell = jnp.exp(-0.5 * pre * pre)
            reach = 1.0 / (1.0 + 0.23164189 * jnp.abs(pre))
            tail = reach * (
                0.127414796
                + reach * (-0.142248368 + reach * (0.7107068705 + reach * (-0.7265760135 + reach * 0.5307027145)))
            )
            tail = tail * bell
            chance = jnp.where(pre >= 0, 1.0 - tail, tail)
            act_ref[strip, at] = (pre * chance).astype(bfloat)
            slope_ref[strip, at] = (chance + pre * bell * 0.3989422804014327).astype(bfloat)


def feed_kernel(normed_ref, into_ref, bias_ref, down_ref, start_ref, act_ref, slope_ref, hidden_ref):
    gelu_tiles(normed_ref, into_ref, bias_ref, act_ref, slope_ref)
    hidden_ref[...] = start_ref[...] + dot(act_ref[...], down_ref[...])


def feed(order, normed, into, bias, down, start):
    tokens, width = normed.shape
    units = into.shape[1]
    return order.call(
        feed_kernel,
        [shaped((tokens, units), bfloat), shaped((tokens, units), bfloat), shaped((tokens, width), single)],
        normed,
        into,
        bias,
        down,
        start,
        cost=4.4,
    )


def feed_up(order, normed, into, bias):
    units = into.shape[1]
    return order.call(
        gelu_tiles,
        [shaped((normed.shape[0], units), bfloat)] * 2,
        normed,
        into,
        bias,
        cost=4.0,
        name="feed_up_kernel",
    )


def add_columns(ref, row, value):
    ref[row : row + 1, :] += jnp.sum(value, axis=0, keepdims=True)


def turn_kernel(side_ref, act_ref, down_ref, start_ref, gain_ref, upstream_ref, grad_ref, sums_ref, unit_ref, branch_ref):
    sums_ref[...] = jnp.zeros_like(sums_ref)

    def body(at):
        unit, scale = unit_of(start_ref[at, :] + dot(act_ref[at, :], down_ref[...]))
        gain = gain_ref[1:2, :]
        upstream = upstream_ref[side_ref[0], at, :].astype(single)
        unit_ref[at, :] = unit
        grad = norm_back(upstream, unit, scale, gain)
        grad_ref[at, :] = grad
        branch_ref[at, :] = grad.astype(bfloat)
        add_columns(sums_ref, 0, upstream * unit)
        add_columns(sums_ref, 1, upstream)
        add_columns(sums_ref, 2, grad)

    strips(start_ref.shape[0], body)


def feed_back_kernel(branch_ref, down_ref, slope_ref, into_ref, start_ref, grad_ref, sums_ref, normed_ref):
    tile = 512
    for j in range(0, into_ref.shape[1], tile):
        at = pl.ds(j, tile)
        pre = dot_cols(branch_ref[...], down_ref[at, :]) * slope_ref[:, at].astype(single)
        low = pre.astype(bfloat)
        grad_ref[:, at] = low
        sums_ref[:, at] = jnp.sum(low.astype(single), axis=0, keepdims=True)
    normed_ref[...] = start_ref[...] + dot_cols(grad_ref[...], into_ref[...])


def feed_back(order, branch, down, slope, into, start):
    tokens, width = branch.shape
    units = into.shape[1]
    return order.call(
        feed_back_kernel,
        [shaped((tokens, units), bfloat), shaped((1, units), single), shaped((tokens, width), single)],
        branch,
        down,
        slope,
        into,
        start,
        cost=3.0,
    )


def norm_back_kernel(hidden_ref, gain_ref, upstream_ref, grad_ref, sums_ref, low_ref):
    sums_ref[...] = jnp.zeros_like(sums_ref)

    def body(at):
        unit, scale = unit_of(hidden_ref[at, :])
        upstream = upstream_ref[at, :]
        grad = norm_back(upstream, unit, scale, gain_ref[0:1, :])
        grad_ref[at, :] = grad
        low_ref[at, :] = grad.astype(bfloat)
        add_columns(sums_ref, 0, upstream * unit)
        add_columns(sums_ref, 1, upstream)
        add_columns(sums_ref, 2, grad)

    strips(hidden_ref.shape[0], body)


def attend_back_kernel(upstream_ref, parts_ref, chance_ref, qkv_ref, start_ref, *refs):
    *out_w, grad_ref, sums_ref, rows_ref, turned_ref = refs
    tokens = upstream_ref.shape[0]
    local = qkv_ref.shape[2]
    middle = upstream_ref.shape[1] // 2
    tile = tokens
    factor = HEAD_DIM**-0.5

    def pair_step(pair):
        at = pair * PAIR
        lanes = pl.ds(at, PAIR)
        queries = parts_ref[0, :, lanes]
        keys_turned = parts_ref[1, :, lanes].T
        values = parts_ref[2, :, lanes]
        if out_w:
            grad_context = dot_cols(upstream_ref[...], out_w[0][lanes, :])
        else:
            grad_context = dot_cols(upstream_ref[:, :middle], qkv_ref[3, lanes, :])
            grad_context = grad_context + dot_cols(
                upstream_ref[:, middle:], qkv_ref[3, pl.ds(local + at, PAIR), :]
            )
        grad_context = grad_context.astype(bfloat)
        context_turned = grad_context.T
        owner = lax.broadcasted_iota(jnp.int32, (PAIR, tile), 0) // HEAD_DIM
        first_lane = lax.broadcasted_iota(jnp.int32, (tokens, PAIR), 1) < HEAD_DIM
        grads_k, grads_v = [], []
        for h in range(2):
            key_rows = keys_turned[h * HEAD_DIM : (h + 1) * HEAD_DIM]
            grad_k = jnp.zeros((tokens, PAIR), single)
            grad_v = jnp.zeros((tokens, PAIR), single)
            for q in range(tokens // tile):
                cut = slice(q * tile, (q + 1) * tile)
                picked = context_turned[:, cut]
                picked = jnp.where(owner == h, picked, jnp.zeros_like(picked))
                chances_low = chance_ref[pair * 2 + h, :, cut]
                chances = chances_low.astype(single)
                grad_chances = dot(values, picked)
                inner = jnp.sum(chances * grad_chances, axis=0, keepdims=True)
                grad_scores = (chances * (grad_chances - inner)).astype(bfloat)
                grad_v = grad_v + dot(chances_low, grad_context[cut, :])
                grad_k = grad_k + dot(grad_scores, queries[cut, :])
                turned_ref[pl.ds(at + h * HEAD_DIM, HEAD_DIM), cut] = (dot(key_rows, grad_scores) * factor).astype(bfloat)
            grads_k.append(grad_k)
            grads_v.append(grad_v)
        grad_k = (jnp.where(first_lane, grads_k[0], grads_k[1]) * factor).astype(bfloat)
        grad_v = jnp.where(first_lane, grads_v[0], grads_v[1]).astype(bfloat)
        grad_ref[:, pl.ds(local + at, PAIR)] = grad_k
        grad_ref[:, pl.ds(2 * local + at, PAIR)] = grad_v

    for pair in range(local // PAIR):
        pair_step(pair)
    grad_ref[:, 0:local] = turned_ref[...].T
    sums_ref[...] = jnp.sum(grad_ref[...].astype(single), axis=0, keepdims=True)
    total = start_ref[...]
    for part in range(3):
        total = total + dot_cols(grad_ref[:, part * local : (part + 1) * local], qkv_ref[part])
    rows_ref[...] = total


def attend_back(order, upstream, parts, chances, qkv, start, out=None):
    tokens, width = upstream.shape
    local = qkv.shape[2]
    return order.call(
        attend_back_kernel,
        [shaped((tokens, 3 * local), bfloat), shaped((1, 3 * local), single), shaped((tokens, width), single)],
        upstream,
        parts,
        chances,
        qkv,
        start,
        *([] if out is None else [out]),
        scratch=[pltpu.VMEM((local, tokens), bfloat)],
        cost=7.4,
    )


def vectors_kernel(side_ref, first_ref, second_ref, units_own, units_other, proj_own, proj_other, out_ref):
    width = first_ref.shape[1]
    local = proj_own.shape[1] // 3
    out_ref[...] = jnp.zeros_like(out_ref)
    out_ref[0:3, :width] = first_ref[...]
    out_ref[0:3, width:] = second_ref[...]
    swapped = side_ref[0] == 1
    for row, units, proj in (
        (3, (units_own, units_other), (proj_own, proj_other)),
        (5, (units_other, units_own), (proj_other, proj_own)),
    ):
        out_ref[row : row + 1, :] = jnp.where(swapped, units[1][...], units[0][...])
        parts = jnp.where(swapped, proj[1][...], proj[0][...])
        out_ref[row + 1 : row + 2, :local] = parts[:, :local]
        out_ref[row + 1 : row + 2, local : 2 * local] = parts[:, 2 * local :]


def both_result_kernel(side_ref, mine_ref, other_ref, gain_ref, shift_ref, out_ref):
    side = side_ref[0]

    def body(at):
        for place, ref in ((side, mine_ref), (1 - side, other_ref)):
            out_ref[place, at, :] = (ref[at, :] * gain_ref[1:2, :] + shift_ref[1:2, :]).astype(bfloat)

    strips(mine_ref.shape[0], body)


def both_kernel(side_ref, mine_ref, other_ref, out_ref):
    side = side_ref[0]
    out_ref[side] = mine_ref[...]
    out_ref[1 - side] = other_ref[...]


def heads_share_kernel(rank_ref, qkv_ref, out_ref, heads_ref):
    heads_ref[0, 0:3] = qkv_ref[...].astype(single)
    heads_ref[0, 3] = out_ref[...].astype(single)


def feed_share_kernel(rank_ref, left_ref, right_ref, down_ref, feed_ref):
    depth = left_ref.shape[0]
    feed_ref[0:depth, :] = left_ref[...].astype(single)
    feed_ref[depth : 2 * depth, :] = right_ref[...].astype(single)
    feed_ref[2 * depth :, :] = down_ref[...].astype(single)


def direct_share_kernel(rank_ref, last_ref, direct_ref):
    direct_ref[0, 0] = last_ref[...].astype(single)


def small_kernel(bias_ref, units_ref, small_ref):
    local = bias_ref.shape[1]
    small_ref[:, 0:local] = bias_ref[0:1, :]
    small_ref[:, local : 2 * local] = bias_ref[1:2, :]
    small_ref[:, 2 * local :] = units_ref[...]


def shares(rank, qkv, out, into, down):
    width, local, hidden = qkv.shape[1], qkv.shape[2], into.shape[1]
    depth = width // 8
    quarters = local // depth
    rows, last = hidden // 12, hidden // 6

    def cut(kernel, specs, shape, *args):
        return pl.pallas_call(
            kernel,
            grid_spec=pltpu.PrefetchScalarGridSpec(
                num_scalar_prefetch=1,
                grid=(1,),
                in_specs=specs,
                out_specs=pl.BlockSpec(shape, lambda j, r: (0,) * len(shape)),
            ),
            out_shape=shaped(shape, single),
            cost_estimate=pl.CostEstimate(flops=1000, bytes_accessed=1000, transcendentals=0),
            name=kernel.__name__,
        )(rank, *args)

    heads = cut(
        heads_share_kernel,
        [
            pl.BlockSpec((3, depth, local), lambda j, r: (0, r[0], 0)),
            pl.BlockSpec((depth, local), lambda j, r: (r[0] % quarters, r[0] // quarters)),
        ],
        (1, 4, depth, local),
        qkv,
        out,
    )
    feed_in = cut(
        feed_share_kernel,
        [
            pl.BlockSpec((depth, width), lambda j, r: (r[0], 0)),
            pl.BlockSpec((depth, width), lambda j, r: (r[0], 1)),
            pl.BlockSpec((rows, width), lambda j, r: (r[0], 0)),
        ],
        (2 * depth + rows, width),
        into,
        into,
        down,
    )
    direct = cut(
        direct_share_kernel,
        [pl.BlockSpec((last, width), lambda j, r: (4 + r[0] % 2, 0))],
        (1, 1, last, width),
        down,
    )
    return heads, feed_in, direct


SCHEDULE = ["ss", 8.0, "ao", 20.0, 20.0, "tH", 2.0, "H", "tF", "rr", "H", "H", "I", "sm", 2.0, 10.0, "pH", "D", 2.0, "at", "no", 2.0, "rn", "I", "I", 10.0, "tX", 10.0, "D", "fo", "pI", "D", 5.0, "ff", 20.0, "pD", "tu", "rb", "sd", "bf", "bo", "d", "si", "nb", "ba", "i", "ra", "d", 30.0, "so", 2.0, "bs", "sq", 20.0, "u", "d", "q", 10.0, "i", 20.0, "d", "q", "d", "i", "q", "br", 20.0, 20.0, 20.0, "bg", "i", "g", "q", "i", 5.0, "dr"]
KINDS = ["zwyx/xyzw", "zwyx/yzwx", "xyzw/yzwx"]
CUTS = [1, 2, 2]


def body(
    inputs,
    lengths,
    w_qkv,
    b_qv,
    w_out,
    b_out,
    ln_gains,
    ln_biases,
    w_in,
    b_in,
    w_down,
    b_down,
    cotangent,
):
    size = lax.axis_size("dp")
    me = lax.axis_index("dp")
    side = lax.axis_index("tensor")
    side_index = side.astype(jnp.int32).reshape(1)
    tokens, width = inputs.shape[1:]
    local = w_qkv.shape[2]
    units = w_in.shape[1]
    order = Order()

    rank, core = me & 7, me & 1
    core_index = core.astype(jnp.int32).reshape(1)
    me_index = me.astype(jnp.int32).reshape(1)
    qkv_own = jnp.transpose(w_qkv, (1, 0, 2))
    depth = width // 8
    heads_share, feed_share, direct_share = shares(rank.astype(jnp.int32).reshape(1), qkv_own, w_out, w_in, w_down)
    heads_share = swap_x(heads_share)
    feed_share = swap_x(feed_share)
    direct_share = swap_x(direct_share)

    dims = [1 << k for k in range(1, size.bit_length() - 1)]
    letters = {"x": [None], "y": dims[:1], "z": dims[1:2], "w": dims[2:]}

    def kind(k):
        return [[dim for letter in word for dim in letters[letter]] for word in KINDS[k].split("/")]

    chains = {}
    v = types.SimpleNamespace()

    def step(name):
        return lambda: chains[name].step()

    def attend_own():
        v.own = attend(order, side_index, lengths, inputs, qkv_own, b_qv, b_out.reshape(1, -1), w_out)

    def send_small():
        hidden = b_in.reshape(1, -1)
        v.small_own = order.call(small_kernel, shaped((1, 2 * local + units), single), b_qv, hidden, cost=0.3)
        v.small_sent = swap_x(v.small_own)

    def take_small():
        v.small = order.pin(v.small_sent)

    def take_heads():
        chains["H"] = Chain(fetch_spread(order, order.pin(heads_share), size, 2.0))
        chains["H"].step()

    def take_feed():
        into_share, down_share = order.call(
            unpack_kernel,
            [shaped((1, 2, depth, width), single), shaped((1, 1, units // 12, width), single)],
            feed_share,
            cost=10.0,
        )
        chains["I"] = Chain(fetch_spread(order, into_share, size, 8.0))
        chains["D"] = Chain(fetch_spread(order, down_share, size, 8.0))
        chains["I"].step()
        chains["D"].step()

    def take_direct():
        chains["X"] = Chain(fetch_direct(order, direct_share, size, units // 3 * 2))
        chains["X"].step()

    def place_heads():
        v.w_heads = place(order, me_index, [chains["H"].value], (4, width, local))

    def place_in():
        v.w_in = place(order, me_index, [chains["I"].value], w_in.shape)

    def place_down():
        v.w_down = place(order, me_index, [chains["D"].value, chains["X"].value], w_down.shape)

    def relative_rows():
        v.rows_rel = relative(order, side_index, me_index, size, inputs)

    def attend_other():
        v.other = attend(order, side_index, lengths, inputs, v.w_heads, v.small, v.own[3])

    def norm():
        v.normed, v.two_start = order.call(
            norm_kernel,
            [shaped((tokens, width), bfloat), shaped((tokens, width), single)],
            v.other[3],
            ln_gains,
            ln_biases,
            b_down.reshape(1, -1),
        )

    def feed_own():
        v.act_own, v.slope_own, v.two_own = feed(
            order, v.normed, w_in, b_in.reshape(1, -1), w_down, v.two_start
        )

    def feed_other():
        v.act, v.slope = feed_up(order, v.normed, v.w_in, v.small)

    def relative_normed():
        v.normed_rel = relative(order, side_index, me_index, size, v.normed)

    def turn():
        v.grad_two, v.sums_two, v.unit, v.branch = order.call(
            turn_kernel,
            [
                shaped((tokens, width), single),
                shaped((3, width), single),
                shaped((tokens, width), single),
                shaped((tokens, width), bfloat),
            ],
            v.act,
            v.w_down,
            v.two_own,
            ln_gains,
            cotangent,
            scalars=(side_index,),
            cost=2.6,
        )
        v.unit_other = swap_x(v.unit)

    def start(name, k, terms, finish, *more):
        chains[name] = Chain(scatter(order, core_index, terms, CUTS[k], kind(k), size, finish, *more))
        chains[name].step()

    share = width // size

    def finish(low, arrived, extra):
        return add_arrived(order, low, arrived, extra, True)[0]

    def finish_project(low, arrived, extra):
        shapes = [(3, share, local), (share, local), (2, width), (2, width)]
        shapes += [(width,), (units,), (width,), (2, local)]
        return order.call(
            last_kernel,
            [shaped(shape, single) for shape in shapes],
            low,
            arrived,
            extra,
            scalars=(side_index,),
            cost=1.0,
        )

    def relative_branch():
        v.branch_rel = relative(order, side_index, me_index, size, v.branch)

    def start_down():
        rights = (v.act_own, v.act)
        start("d", 0, lambda sides: [(v.branch_rel, [rights[k] for k in sides], 0, units)], finish)

    def feed_back_other():
        v.pre, v.units_sum, v.grad_other = feed_back(
            order, v.branch, v.w_down, v.slope, v.w_in, v.grad_two
        )

    def feed_back_own():
        v.pre_own, v.units_sum_own, v.grad = feed_back(
            order, v.branch, w_down, v.slope_own, w_in, v.grad_other
        )

    def start_into():
        rights = (v.pre_own, v.pre)
        start("i", 1, lambda sides: [(v.normed_rel, [rights[k] for k in sides], 0, units)], finish)

    def norm_two():
        v.grad_one, v.sums_one, v.attended = order.call(
            norm_back_kernel,
            [shaped((tokens, width), single), shaped((3, width), single), shaped((tokens, width), bfloat)],
            v.other[3],
            ln_gains,
            v.grad,
            cost=1.5,
        )

    def relative_attended():
        v.attended_rel = relative(order, side_index, me_index, size, v.attended)

    def attend_back_other():
        v.proj, v.proj_sum, v.rows_other = attend_back(
            order, v.attended, v.other[0], v.other[1], v.w_heads, v.grad_one
        )

    def attend_back_own():
        v.proj_own, v.proj_sum_own, v.grad_rows = attend_back(
            order, v.attended, v.own[0], v.own[1], qkv_own, v.rows_other, w_out
        )
        v.grad_other_rows = swap_x(v.grad_rows)

    def vectors():
        return order.call(
            vectors_kernel,
            shaped((8, 2 * width), single),
            v.sums_one,
            v.sums_two,
            v.units_sum_own,
            v.units_sum,
            v.proj_sum_own,
            v.proj_sum,
            scalars=(side_index,),
            cost=0.5,
        )

    def start_project():
        def terms(sides):
            contexts = [(v.own, v.other)[k][2] for k in sides]
            projs = [v.proj if k else v.proj_own for k in sides]
            return [(v.attended_rel, contexts, 0, local), (v.rows_rel, projs, 0, 3 * local)]

        start("q", 2, terms, finish_project, vectors, True)

    def take_unit():
        v.unit_other = order.pin(v.unit_other)

    def take_grad():
        v.grad_other_rows = order.pin(v.grad_other_rows)

    def both_results():
        v.results = order.call(
            both_result_kernel,
            shaped((2, tokens, width), bfloat),
            v.unit,
            v.unit_other,
            ln_gains,
            ln_biases,
            scalars=(side_index,),
            cost=1.5,
        )

    def both_grads():
        v.grads = order.call(
            both_kernel,
            shaped((2, tokens, width), single),
            v.grad_rows,
            v.grad_other_rows,
            scalars=(side_index,),
            cost=2.0,
        )

    def drain():
        last = [chains[name] for name in "diq"]
        while any(chain.value is None for chain in last):
            for chain in last:
                if chain.value is None:
                    chain.step()

    steps = {
        "ao": attend_own,
        "ss": send_small,
        "sm": take_small,
        "tH": take_heads,
        "tF": take_feed,
        "tX": take_direct,
        "H": step("H"),
        "I": step("I"),
        "D": step("D"),
        "pH": place_heads,
        "pI": place_in,
        "pD": place_down,
        "rr": relative_rows,
        "at": attend_other,
        "no": norm,
        "fo": feed_own,
        "ff": feed_other,
        "rn": relative_normed,
        "tu": turn,
        "rb": relative_branch,
        "sd": start_down,
        "bf": feed_back_other,
        "bo": feed_back_own,
        "si": start_into,
        "nb": norm_two,
        "ra": relative_attended,
        "ba": attend_back_other,
        "bs": attend_back_own,
        "so": start_project,
        "sq": step("q"),
        **{name: step(name) for name in "diq"},
        "u": take_unit,
        "g": take_grad,
        "br": both_results,
        "bg": both_grads,
        "dr": drain,
    }
    for name in SCHEDULE:
        if isinstance(name, str):
            steps[name]()
        else:
            order.pad(float(name))
    results, grads = v.results, v.grads
    g_qkv, g_out, gains, shifts, g_b_out, g_b_in, g_b_down, g_b_qv = chains["q"].value
    return (
        results,
        grads,
        jnp.transpose(g_qkv, (1, 0, 2)),
        g_b_qv,
        g_out.T,
        g_b_out,
        gains,
        shifts,
        chains["i"].value,
        g_b_in,
        chains["d"].value.T,
        g_b_down,
    )


def solution(mesh):
    placed = (
        P("dp", None, None),
        P("dp"),
        P(None, None, "tensor"),
        P(None, "tensor"),
        P("tensor", None),
        P(),
        P(),
        P(),
        P(None, "tensor"),
        P("tensor"),
        P("tensor", None),
        P(),
        P("dp", None, None),
    )
    return jax.shard_map(
        body,
        mesh=mesh,
        in_specs=placed,
        out_specs=(
            P("dp", None, None),
            P("dp", None, None),
            P("dp", None, "tensor"),
            P(None, "tensor"),
            P("tensor", "dp"),
            P(),
            P(),
            P(),
            P("dp", "tensor"),
            P("tensor"),
            P("tensor", "dp"),
            P(),
        ),
        check_vma=False,
    )
```

```python
import functools
import types

import jax
import jax.numpy as jnp
from jax import lax
from jax.experimental import pallas as pl
from jax.experimental.pallas import tpu as pltpu
from jax.sharding import PartitionSpec as P

HEAD_DIM = 64
PAIR = 2 * HEAD_DIM
norm_eps = 1e-12
bfloat = jnp.bfloat16
single = jnp.float32
MIB = 1 << 20
COST_UNIT = 1.0e9


def dot(left, right):
    return jnp.dot(left, right, preferred_element_type=single)


def dot_cols(left, right):
    return lax.dot_general(
        left, right, (((1,), (1,)), ((), ())), preferred_element_type=single
    )


def shaped(shape, dtype):
    return jax.ShapeDtypeStruct(shape, dtype)


def nothing_kernel(out_ref):
    out_ref[...] = jnp.zeros_like(out_ref)


class Order:
    def __init__(self):
        self.last = None

    def call(self, kernel, outs, *args, scalars=(), scratch=(), grid=(), in_specs=None, out_specs=None, limit=16, aliases=None, cost=1.0, name=None):
        many = isinstance(outs, (tuple, list))
        if in_specs is None:
            in_specs = [pl.BlockSpec(memory_space=pltpu.VMEM)] * len(args)
        if out_specs is None:
            out_specs = [pl.BlockSpec(memory_space=pltpu.VMEM)] * len(outs) if many else pl.BlockSpec(memory_space=pltpu.VMEM)
        in_specs = [pl.BlockSpec(memory_space=pltpu.SMEM)] * len(scalars) + list(in_specs)
        operands = list(scalars) + list(args)
        run = kernel
        if self.last is not None:
            before = len(operands)
            operands.append(self.last)
            in_specs.append(pl.BlockSpec(memory_space=pl.ANY))

            def run(*refs):
                kernel(*refs[:before], *refs[before + 1 :])

        made = pl.pallas_call(
            run,
            out_shape=outs,
            grid=grid,
            in_specs=in_specs,
            out_specs=out_specs,
            scratch_shapes=list(scratch),
            name=name or kernel.__name__,
            input_output_aliases=aliases or {},
            compiler_params=pltpu.CompilerParams(vmem_limit_bytes=limit * MIB),
            cost_estimate=pl.CostEstimate(flops=int(cost * COST_UNIT), bytes_accessed=1000, transcendentals=0),
        )(*operands)
        self.last = made[-1] if many else made
        return made

    def pad(self, cost):
        self.call(nothing_kernel, shaped((8, 128), single), cost=cost)

    def pin(self, value):
        return self.call(
            lambda *refs: None,
            shaped(value.shape, value.dtype),
            value,
            in_specs=[pl.BlockSpec(memory_space=pl.ANY)],
            out_specs=pl.BlockSpec(memory_space=pl.ANY),
            aliases={0: 0},
            cost=0.0,
            name="pin_kernel",
        )


class Chain:
    def __init__(self, steps):
        self.steps = steps
        self.value = None

    def step(self):
        self.value = next(self.steps, self.value)
        return self.value

    def run(self, count):
        for _ in range(count):
            self.step()


def swap_dp(value, mask, size):
    return lax.ppermute(value, "dp", [(i, i ^ mask) for i in range(size)])


def swap_x(value):
    return lax.ppermute(value, "tensor", [(0, 1), (1, 0)])


def reverse_bits(position, bits):
    out = 0
    for k in range(bits):
        out |= ((position >> k) & 1) << (bits - 1 - k)
    return out


def place_kernel(starts, me_ref, *refs):
    out_ref = refs[-1]
    me = me_ref[0]
    at = 0
    for piece in refs[:-1]:
        height = piece.shape[2]
        for b in range(piece.shape[0]):
            start = pl.multiple_of(starts[at](me), 16)
            for c in range(piece.shape[1]):
                if out_ref.ndim == 3:
                    out_ref[c, pl.ds(start, height), :] = piece[b, c].astype(out_ref.dtype)
                else:
                    lanes = slice(c * piece.shape[3], (c + 1) * piece.shape[3])
                    out_ref[pl.ds(start, height), lanes] = piece[b, c].astype(out_ref.dtype)
            at += 1


def place(order, me, parts, shape):
    pieces, starts = [], []
    for held, begin in parts:
        pieces += held
        starts += begin
    kernel = functools.partial(place_kernel, tuple(starts))
    return order.call(kernel, shaped(shape, bfloat), *pieces, scalars=(me,), cost=2.4, name="place_kernel")


def pack_kernel(first_ref, second_ref, out_ref):
    out_ref[0] = first_ref[0]
    out_ref[1] = second_ref[0]


def swap_mixed(value, first, second, size):
    pairs = []
    for d in range(size):
        mask = second if d & 1 else first
        for t in range(2):
            to = (d, 1 - t) if mask is None else (d ^ mask, t)
            pairs.append((2 * d + t, 2 * to[0] + to[1]))
    return lax.ppermute(value, ("dp", "tensor"), pairs)


def fetch_spread(order, held, size, pack_cost):
    arrived = swap_mixed(held, 4, 2, size)
    yield
    both = order.call(pack_kernel, shaped((2,) + held.shape[1:], single), held, arrived, cost=pack_cost)
    arrived = swap_mixed(both, 2, 4, size)
    both_core = swap_dp(both, 1, size)
    yield
    both_core = order.pin(both_core)
    yield
    arrived = order.pin(arrived)
    arrived_core = swap_dp(arrived, 1, size)
    rows = held.shape[-2]

    def start(even, odd, flip):
        return lambda index: ((index & 7) ^ flip ^ jnp.where(index & 1 == flip, even, odd)) * rows

    offsets = list(zip((0, 4, 2, 6), (0, 2, 4, 6)))
    yield [both, arrived, both_core, arrived_core], [
        start(even, odd, flip) for flip in range(2) for even, odd in offsets
    ]


def fetch_direct(order, held, size, base):
    held = order.pin(held)
    rows = held.shape[-2]
    yield [held, swap_dp(held, 1, size)], [
        lambda index: base + (index & 1) * rows,
        lambda index: base + (1 - (index & 1)) * rows,
    ]


def unpack_kernel(all_ref, into_ref, down_ref):
    rows = into_ref.shape[2]
    for c in range(2):
        into_ref[0, c] = all_ref[c * rows : (c + 1) * rows, :]
    down_ref[0, 0] = all_ref[2 * rows :, :]


def product_kernel(groups, sides, cuts, places, extras, core_ref, *refs):
    lefts, rights = refs[: len(groups)], refs[len(groups) : (1 + sides) * len(groups)]
    rest = refs[(1 + sides) * len(groups) :]
    tile = pl.program_id(0)
    first = core_ref[0] == 0

    def spread(side, total, low_ref, high_ref, table, height):
        half = len(table[0])
        for block in range(half):
            at = table[side][block]
            out_ref, at = (low_ref, at) if at < half else (high_ref, at - half)
            out_ref[at * height : (at + 1) * height, :] = total[block * height : (block + 1) * height]

    def run(k, j):
        for side in range(sides):
            total = dot(lefts[k][...], rights[sides * k + side][...])
            rows = total.shape[0]
            cut = sum(cuts[:side]) + j * cuts[side] // sum(groups)
            if places is None:
                rest[extras + cut][:rows, :] = total
                if extras:
                    rest[extras + cut][rows:, :] = rest[0][...]
                continue
            total = total + rest[cut][:rows, :]
            low_ref, high_ref = rest[sum(cuts) + extras :][:2]
            even, odd, height = places
            pl.when(first)(lambda: spread(side, total, low_ref, high_ref, even, height))
            pl.when(jnp.logical_not(first))(lambda: spread(side, total, low_ref, high_ref, odd, height))
            if extras and side == 0:
                extra = rest[sum(cuts)][...] + rest[cut][rows:, :]
                rest[-1][...] = extra
                high_ref[low_ref.shape[0] :, :] = extra

    j = 0
    for k, tiles in enumerate(groups):
        for _ in range(tiles):
            pl.when(tile == j)(functools.partial(run, k, j))
            j += 1


def product(order, core, half, terms, cuts, added=(), places=None, extras=()):
    rows = terms[0][0].shape[0] // 2
    tokens = terms[0][0].shape[1]
    sides = len(terms[0][1])
    tile = 768 if all(term[2] % 768 == 0 and term[3] % 768 == 0 for term in terms) else 384
    groups = tuple(term[3] // tile for term in terms)
    begins = [sum(groups[:k]) for k in range(len(groups))]
    tiles = sum(groups)

    def right_spec(k):
        first = terms[k][2] // tile
        return pl.BlockSpec((tokens, tile), lambda j: (0, first + jnp.clip(j - begins[k], 0, groups[k] - 1)))

    def tall(height):
        return shaped((height, tiles * tile), single), pl.BlockSpec((height, tile), lambda j: (0, j))

    beyond = sum(part.shape[0] for part in extras)
    cut_list = [(side, k, tiles // count) for side, count in enumerate(cuts) for k in range(count)]
    heights = [rows + (beyond if side == 0 else 0) for side, _, _ in cut_list]
    pieces = [
        pl.BlockSpec((height, tile), lambda j, k=k, each=each: (0, jnp.clip(j - k * each, 0, each - 1)))
        for height, (_, k, each) in zip(heights, cut_list)
    ]
    if places is None:
        outs = [shaped((height, cut[2] * tile), single) for height, cut in zip(heights, cut_list)]
        out_specs = pieces
    else:
        height = len(places[0][0]) * places[2]
        heights = [height, height + beyond] + ([beyond] if extras else [])
        outs, out_specs = zip(*[tall(height) for height in heights])
    return order.call(
        functools.partial(product_kernel, groups, sides, cuts, places, len(extras)),
        list(outs),
        *[term[0] for term in terms],
        *[right for term in terms for right in term[1]],
        *added,
        *extras,
        scalars=(core,),
        grid=(tiles,),
        in_specs=[
            *[pl.BlockSpec((rows, tokens), lambda j: (half, 0)) for _ in terms],
            *[right_spec(k) for k in range(len(terms)) for _ in range(sides)],
            *(pieces if added else []),
            *[tall(part.shape[0])[1] for part in extras],
        ],
        out_specs=list(out_specs),
        cost=sides * tiles * tile / 384 * (0.4 if places is None else 0.6),
        name="send_kernel" if places is None else "keep_kernel",
    )


def sum_kernel(whole, low_ref, arrived_ref, *refs):
    rows = low_ref.shape[0]
    extra = refs[0][...] + arrived_ref[rows:, :] if arrived_ref.shape[0] > rows else None
    outs = refs if extra is None else refs[1:]
    if whole:
        outs[0][...] = low_ref[...] + arrived_ref[:rows, :]
    else:
        half = rows // 2
        outs[0][...] = low_ref[:half, :] + arrived_ref[:half, :]
        outs[1][:half, :] = low_ref[half:, :] + arrived_ref[half:rows, :]
    if extra is not None:
        outs[-1][...] = extra
        if not whole:
            outs[1][rows // 2 :, :] = extra


def add_arrived(order, low, arrived, extra, whole=False):
    rows, width = low.shape
    beyond = arrived.shape[0] - rows
    heights = [rows] if whole else [rows // 2, rows // 2 + beyond]
    heights += [beyond] if beyond else []
    outs = order.call(
        functools.partial(sum_kernel, whole),
        [shaped((height, width), single) for height in heights],
        low,
        arrived,
        *([extra] if beyond else []),
        cost=0.7,
        name="add_kernel",
    )
    return outs if beyond else [*outs, None]


def scatter(order, core, terms, cuts, orders, size, finish, extra=None, apart=False):
    masks = [1 << k for k in range(1, size.bit_length() - 1)]
    count = len(masks)

    def place_of(side, block, dims):
        at = 0
        for dim in dims:
            bit = side if dim is None else (block >> (count - 1 - masks.index(dim))) & 1
            at = 2 * at + bit
        return at

    tables = [
        [[place_of(side, block, dims) for block in range(1 << count)] for side in range(2)]
        for dims in orders
    ]
    def send(sides, extras):
        sent = product(order, core, 1, terms(sides), [cuts[side] for side in sides], extras=extras)
        return [swap_dp(part, 1, size) for part in sent]

    if apart:
        arrived = send((1,), ())
        yield
        extras = () if extra is None else (extra(),)
        arrived = send((0,), extras) + arrived
    else:
        extras = ()
        arrived = send((0, 1), extras)
    terms = terms((0, 1))
    yield
    height = terms[0][0].shape[0] // size
    low, high, *extra = product(order, core, 0, terms, cuts, arrived, (*tables, height), extras)
    extra = extra[0] if extras else None
    for k in range(count + 1):
        arrived = swap_mixed(high, orders[0][k], orders[1][k], size)
        yield
        if k < count:
            low, high, extra = add_arrived(order, low, arrived, extra)
    yield finish(low, arrived, extra)


def last_kernel(side_ref, low_ref, arrived_ref, extra_ref, qkv_ref, out_ref, gains_ref, shifts_ref, *vectors):
    b_out_ref, b_in_ref, b_down_ref, b_qv_ref = vectors
    rows = low_ref.shape[0]
    local = qkv_ref.shape[2]
    width = gains_ref.shape[1]
    total = low_ref[...] + arrived_ref[:rows, :]
    out_ref[...] = total[:, :local]
    for k in range(3):
        qkv_ref[k] = total[:, (k + 1) * local : (k + 2) * local]
    sums = extra_ref[...] + arrived_ref[rows:, :]
    for k in range(2):
        half = slice(k * width, (k + 1) * width)
        gains_ref[k : k + 1, :] = sums[0:1, half]
        shifts_ref[k : k + 1, :] = sums[1:2, half]
    b_out_ref[...] = sums[2, :width]
    b_down_ref[...] = sums[2, width:]
    first = side_ref[0] == 0
    b_in_ref[...] = jnp.where(first, sums[3, :], sums[5, :])
    parts = jnp.where(first, sums[4:5, :], sums[6:7, :])
    b_qv_ref[0:1, :] = parts[:, :local]
    b_qv_ref[1:2, :] = parts[:, local : 2 * local]


def relative_kernel(size, side_ref, me_ref, value_ref, out_ref, turned_ref):
    value = value_ref[side_ref[0]] if len(value_ref.shape) == 3 else value_ref[...]
    depth = value.shape[1]
    share = depth // size
    bits = size.bit_length() - 1
    me = me_ref[0]
    if share % 16 == 0:
        turned_ref[...] = value.T
        for p in range(size):
            block = pl.multiple_of((reverse_bits(p, bits) ^ me) * share, 16)
            out_ref[p * share : (p + 1) * share, :] = turned_ref[pl.ds(block, share), :]
        return
    tile = 96
    lanes = lax.broadcasted_iota(jnp.int32, (tile, depth), 1)
    local = lax.broadcasted_iota(jnp.int32, (tile, depth), 0)
    for j in range(0, depth, tile):
        source = jnp.zeros_like(local)
        for p in range(j // share, (j + tile) // share):
            here = (local >= p * share - j) & (local < (p + 1) * share - j)
            source = jnp.where(here, (reverse_bits(p, bits) ^ me) * share + local + (j - p * share), source)
        picks = jnp.where(lanes == source, 1.0, 0.0).astype(bfloat)
        out_ref[j : j + tile, :] = dot_cols(picks, value).astype(bfloat)


def relative(order, side, me, size, value):
    shape = value.shape[-2:][::-1]
    return order.call(
        functools.partial(relative_kernel, size),
        shaped(shape, bfloat),
        value,
        scalars=(side, me),
        scratch=[pltpu.VMEM(shape, bfloat)],
        cost=0.8,
        name="relative_kernel",
    )


def attend_kernel(side_ref, lengths_ref, inputs_ref, qkv_ref, bias_ref, start_ref, *refs):
    *out_w, parts_ref, chance_ref, context_ref, hidden_ref, turned_ref = refs
    tokens = inputs_ref.shape[1]
    local = qkv_ref.shape[2]
    side = side_ref[0]
    rows = inputs_ref[side]
    flat = bias_ref.shape[0] == 1
    for part in range(3):
        projected = dot(rows, qkv_ref[part])
        if part != 1:
            k = part // 2
            projected = projected + (bias_ref[:, k * local : (k + 1) * local] if flat else bias_ref[k : k + 1, :])
        parts_ref[part] = projected.astype(bfloat)
    tile = tokens
    visible = lax.broadcasted_iota(jnp.int32, (tokens, tile), 0) < lengths_ref[side]

    def pair_step(pair):
        at = pair * PAIR
        keys = parts_ref[1, :, pl.ds(at, PAIR)]
        queries = parts_ref[0, :, pl.ds(at, PAIR)].T
        values = parts_ref[2, :, pl.ds(at, PAIR)].T
        owner = lax.broadcasted_iota(jnp.int32, (PAIR, tile), 0) // HEAD_DIM
        for h in range(2):
            value_rows = values[h * HEAD_DIM : (h + 1) * HEAD_DIM]
            for q in range(tokens // tile):
                picked = queries[:, q * tile : (q + 1) * tile] * HEAD_DIM**-0.5
                picked = jnp.where(owner == h, picked, jnp.zeros_like(picked))
                scores = jnp.where(visible, dot(keys, picked), -1e9)
                raised = jnp.exp(scores - jnp.max(scores, axis=0, keepdims=True))
                chances = raised * (1.0 / jnp.sum(raised, axis=0, keepdims=True))
                chances = chances.astype(bfloat)
                chance_ref[pair * 2 + h, :, q * tile : (q + 1) * tile] = chances
                turned_ref[pl.ds(at + h * HEAD_DIM, HEAD_DIM), q * tile : (q + 1) * tile] = dot(value_rows, chances).astype(bfloat)

    for pair in range(local // PAIR):
        pair_step(pair)
    context = turned_ref[...].T
    context_ref[...] = context
    if out_w:
        hidden_ref[...] = rows.astype(single) + start_ref[...] + dot(context, out_w[0][...])
    else:
        middle = hidden_ref.shape[1] // 2
        hidden_ref[:, :middle] = start_ref[:, :middle] + dot(context, qkv_ref[3, :local, :])
        hidden_ref[:, middle:] = start_ref[:, middle:] + dot(context, qkv_ref[3, local:, :])


def attend(order, side, lengths, inputs, qkv, bias, start, out=None):
    tokens, width = inputs.shape[1:]
    local = qkv.shape[2]
    return order.call(
        attend_kernel,
        [
            shaped((3, tokens, local), bfloat),
            shaped((local // HEAD_DIM, tokens, tokens), bfloat),
            shaped((tokens, local), bfloat),
            shaped((tokens, width), single),
        ],
        inputs,
        qkv,
        bias,
        start,
        *([] if out is None else [out]),
        scalars=(side, lengths),
        scratch=[pltpu.VMEM((local, tokens), bfloat)],
        cost=6.6,
    )


def unit_of(hidden):
    centred = hidden - jnp.mean(hidden, axis=-1, keepdims=True)
    scale = lax.rsqrt(jnp.mean(centred * centred, axis=-1, keepdims=True) + norm_eps)
    return centred * scale, scale


def norm_back(upstream, unit, scale, gain):
    scaled = upstream * gain
    return scale * (
        scaled
        - jnp.mean(scaled, axis=-1, keepdims=True)
        - unit * jnp.mean(scaled * unit, axis=-1, keepdims=True)
    )


STRIP = 256


def strips(tokens, body):
    def step(j, carry):
        body(pl.ds(pl.multiple_of(j * STRIP, STRIP), STRIP))
        return carry

    lax.fori_loop(0, tokens // STRIP, step, 0)


def norm_kernel(hidden_ref, gain_ref, shift_ref, down_ref, low_ref, next_ref):
    def body(at):
        unit, _ = unit_of(hidden_ref[at, :])
        normed = unit * gain_ref[0:1, :] + shift_ref[0:1, :]
        low_ref[at, :] = normed.astype(bfloat)
        next_ref[at, :] = normed + down_ref[...]

    strips(hidden_ref.shape[0], body)


def gelu_tiles(normed_ref, into_ref, bias_ref, act_ref, slope_ref):
    tokens, hidden_units = normed_ref.shape[0], into_ref.shape[1]
    tile, height = 512, 128
    before = bias_ref.shape[1] - hidden_units
    for j in range(0, hidden_units, tile):
        at = pl.ds(j, tile)
        for k in range(0, tokens, height):
            strip = pl.ds(k, height)
            pre = dot(normed_ref[strip, :], into_ref[:, at]) + bias_ref[:, pl.ds(before + j, tile)]
            bell = jnp.exp(-0.5 * pre * pre)
            reach = 1.0 / (1.0 + 0.23164189 * jnp.abs(pre))
            tail = reach * (
                0.127414796
                + reach * (-0.142248368 + reach * (0.7107068705 + reach * (-0.7265760135 + reach * 0.5307027145)))
            )
            tail = tail * bell
            chance = jnp.where(pre >= 0, 1.0 - tail, tail)
            act_ref[strip, at] = (pre * chance).astype(bfloat)
            slope_ref[strip, at] = (chance + pre * bell * 0.3989422804014327).astype(bfloat)


def feed_kernel(normed_ref, into_ref, bias_ref, down_ref, start_ref, act_ref, slope_ref, hidden_ref):
    gelu_tiles(normed_ref, into_ref, bias_ref, act_ref, slope_ref)
    hidden_ref[...] = start_ref[...] + dot(act_ref[...], down_ref[...])


def feed(order, normed, into, bias, down, start):
    tokens, width = normed.shape
    units = into.shape[1]
    return order.call(
        feed_kernel,
        [shaped((tokens, units), bfloat), shaped((tokens, units), bfloat), shaped((tokens, width), single)],
        normed,
        into,
        bias,
        down,
        start,
        cost=4.4,
    )


def feed_up(order, normed, into, bias):
    units = into.shape[1]
    return order.call(
        gelu_tiles,
        [shaped((normed.shape[0], units), bfloat)] * 2,
        normed,
        into,
        bias,
        cost=4.0,
        name="feed_up_kernel",
    )


def add_columns(ref, row, value):
    ref[row : row + 1, :] += jnp.sum(value, axis=0, keepdims=True)


def turn_kernel(side_ref, act_ref, down_ref, start_ref, gain_ref, upstream_ref, grad_ref, sums_ref, unit_ref, branch_ref):
    sums_ref[...] = jnp.zeros_like(sums_ref)

    def body(at):
        unit, scale = unit_of(start_ref[at, :] + dot(act_ref[at, :], down_ref[...]))
        gain = gain_ref[1:2, :]
        upstream = upstream_ref[side_ref[0], at, :].astype(single)
        unit_ref[at, :] = unit
        grad = norm_back(upstream, unit, scale, gain)
        grad_ref[at, :] = grad
        branch_ref[at, :] = grad.astype(bfloat)
        add_columns(sums_ref, 0, upstream * unit)
        add_columns(sums_ref, 1, upstream)
        add_columns(sums_ref, 2, grad)

    strips(start_ref.shape[0], body)


def feed_back_kernel(branch_ref, down_ref, slope_ref, into_ref, start_ref, grad_ref, sums_ref, normed_ref):
    tile = 512
    for j in range(0, into_ref.shape[1], tile):
        at = pl.ds(j, tile)
        pre = dot_cols(branch_ref[...], down_ref[at, :]) * slope_ref[:, at].astype(single)
        low = pre.astype(bfloat)
        grad_ref[:, at] = low
        sums_ref[:, at] = jnp.sum(low.astype(single), axis=0, keepdims=True)
    normed_ref[...] = start_ref[...] + dot_cols(grad_ref[...], into_ref[...])


def feed_back(order, branch, down, slope, into, start):
    tokens, width = branch.shape
    units = into.shape[1]
    return order.call(
        feed_back_kernel,
        [shaped((tokens, units), bfloat), shaped((1, units), single), shaped((tokens, width), single)],
        branch,
        down,
        slope,
        into,
        start,
        cost=3.0,
    )


def norm_back_kernel(hidden_ref, gain_ref, upstream_ref, grad_ref, sums_ref, low_ref):
    sums_ref[...] = jnp.zeros_like(sums_ref)

    def body(at):
        unit, scale = unit_of(hidden_ref[at, :])
        upstream = upstream_ref[at, :]
        grad = norm_back(upstream, unit, scale, gain_ref[0:1, :])
        grad_ref[at, :] = grad
        low_ref[at, :] = grad.astype(bfloat)
        add_columns(sums_ref, 0, upstream * unit)
        add_columns(sums_ref, 1, upstream)
        add_columns(sums_ref, 2, grad)

    strips(hidden_ref.shape[0], body)


def attend_back_kernel(upstream_ref, parts_ref, chance_ref, qkv_ref, start_ref, *refs):
    *out_w, grad_ref, sums_ref, rows_ref, turned_ref = refs
    tokens = upstream_ref.shape[0]
    local = qkv_ref.shape[2]
    middle = upstream_ref.shape[1] // 2
    tile = tokens
    factor = HEAD_DIM**-0.5

    def pair_step(pair):
        at = pair * PAIR
        lanes = pl.ds(at, PAIR)
        queries = parts_ref[0, :, lanes]
        keys_turned = parts_ref[1, :, lanes].T
        values = parts_ref[2, :, lanes]
        if out_w:
            grad_context = dot_cols(upstream_ref[...], out_w[0][lanes, :])
        else:
            grad_context = dot_cols(upstream_ref[:, :middle], qkv_ref[3, lanes, :])
            grad_context = grad_context + dot_cols(
                upstream_ref[:, middle:], qkv_ref[3, pl.ds(local + at, PAIR), :]
            )
        grad_context = grad_context.astype(bfloat)
        context_turned = grad_context.T
        owner = lax.broadcasted_iota(jnp.int32, (PAIR, tile), 0) // HEAD_DIM
        first_lane = lax.broadcasted_iota(jnp.int32, (tokens, PAIR), 1) < HEAD_DIM
        grads_k, grads_v = [], []
        for h in range(2):
            key_rows = keys_turned[h * HEAD_DIM : (h + 1) * HEAD_DIM]
            grad_k = jnp.zeros((tokens, PAIR), single)
            grad_v = jnp.zeros((tokens, PAIR), single)
            for q in range(tokens // tile):
                cut = slice(q * tile, (q + 1) * tile)
                picked = context_turned[:, cut]
                picked = jnp.where(owner == h, picked, jnp.zeros_like(picked))
                chances_low = chance_ref[pair * 2 + h, :, cut]
                chances = chances_low.astype(single)
                grad_chances = dot(values, picked)
                inner = jnp.sum(chances * grad_chances, axis=0, keepdims=True)
                grad_scores = (chances * (grad_chances - inner)).astype(bfloat)
                grad_v = grad_v + dot(chances_low, grad_context[cut, :])
                grad_k = grad_k + dot(grad_scores, queries[cut, :])
                turned_ref[pl.ds(at + h * HEAD_DIM, HEAD_DIM), cut] = (dot(key_rows, grad_scores) * factor).astype(bfloat)
            grads_k.append(grad_k)
            grads_v.append(grad_v)
        grad_k = (jnp.where(first_lane, grads_k[0], grads_k[1]) * factor).astype(bfloat)
        grad_v = jnp.where(first_lane, grads_v[0], grads_v[1]).astype(bfloat)
        grad_ref[:, pl.ds(local + at, PAIR)] = grad_k
        grad_ref[:, pl.ds(2 * local + at, PAIR)] = grad_v

    for pair in range(local // PAIR):
        pair_step(pair)
    grad_ref[:, 0:local] = turned_ref[...].T
    sums_ref[...] = jnp.sum(grad_ref[...].astype(single), axis=0, keepdims=True)
    total = start_ref[...]
    for part in range(3):
        total = total + dot_cols(grad_ref[:, part * local : (part + 1) * local], qkv_ref[part])
    rows_ref[...] = total


def attend_back(order, upstream, parts, chances, qkv, start, out=None):
    tokens, width = upstream.shape
    local = qkv.shape[2]
    return order.call(
        attend_back_kernel,
        [shaped((tokens, 3 * local), bfloat), shaped((1, 3 * local), single), shaped((tokens, width), single)],
        upstream,
        parts,
        chances,
        qkv,
        start,
        *([] if out is None else [out]),
        scratch=[pltpu.VMEM((local, tokens), bfloat)],
        cost=7.4,
    )


def vectors_kernel(side_ref, first_ref, second_ref, units_own, units_other, proj_own, proj_other, out_ref):
    width = first_ref.shape[1]
    local = proj_own.shape[1] // 3
    out_ref[...] = jnp.zeros_like(out_ref)
    out_ref[0:3, :width] = first_ref[...]
    out_ref[0:3, width:] = second_ref[...]
    swapped = side_ref[0] == 1
    for row, units, proj in (
        (3, (units_own, units_other), (proj_own, proj_other)),
        (5, (units_other, units_own), (proj_other, proj_own)),
    ):
        out_ref[row : row + 1, :] = jnp.where(swapped, units[1][...], units[0][...])
        parts = jnp.where(swapped, proj[1][...], proj[0][...])
        out_ref[row + 1 : row + 2, :local] = parts[:, :local]
        out_ref[row + 1 : row + 2, local : 2 * local] = parts[:, 2 * local :]


def both_result_kernel(side_ref, mine_ref, other_ref, gain_ref, shift_ref, out_ref):
    side = side_ref[0]

    def body(at):
        for place, ref in ((side, mine_ref), (1 - side, other_ref)):
            out_ref[place, at, :] = (ref[at, :] * gain_ref[1:2, :] + shift_ref[1:2, :]).astype(bfloat)

    strips(mine_ref.shape[0], body)


def both_kernel(side_ref, mine_ref, other_ref, out_ref):
    side = side_ref[0]
    out_ref[side] = mine_ref[...]
    out_ref[1 - side] = other_ref[...]


def heads_share_kernel(rank_ref, qkv_ref, out_ref, heads_ref):
    heads_ref[0, 0:3] = qkv_ref[...].astype(single)
    heads_ref[0, 3] = out_ref[...].astype(single)


def feed_share_kernel(rank_ref, left_ref, right_ref, down_ref, feed_ref):
    depth = left_ref.shape[0]
    feed_ref[0:depth, :] = left_ref[...].astype(single)
    feed_ref[depth : 2 * depth, :] = right_ref[...].astype(single)
    feed_ref[2 * depth :, :] = down_ref[...].astype(single)


def direct_share_kernel(rank_ref, last_ref, direct_ref):
    direct_ref[0, 0] = last_ref[...].astype(single)


def small_kernel(bias_ref, units_ref, small_ref):
    local = bias_ref.shape[1]
    small_ref[:, 0:local] = bias_ref[0:1, :]
    small_ref[:, local : 2 * local] = bias_ref[1:2, :]
    small_ref[:, 2 * local :] = units_ref[...]


def shares(rank, qkv, out, into, down):
    width, local, hidden = qkv.shape[1], qkv.shape[2], into.shape[1]
    depth = width // 8
    quarters = local // depth
    rows, last = hidden // 12, hidden // 6

    def cut(kernel, specs, shape, *args):
        return pl.pallas_call(
            kernel,
            grid_spec=pltpu.PrefetchScalarGridSpec(
                num_scalar_prefetch=1,
                grid=(1,),
                in_specs=specs,
                out_specs=pl.BlockSpec(shape, lambda j, r: (0,) * len(shape)),
            ),
            out_shape=shaped(shape, single),
            cost_estimate=pl.CostEstimate(flops=1000, bytes_accessed=1000, transcendentals=0),
            name=kernel.__name__,
        )(rank, *args)

    heads = cut(
        heads_share_kernel,
        [
            pl.BlockSpec((3, depth, local), lambda j, r: (0, r[0], 0)),
            pl.BlockSpec((depth, local), lambda j, r: (r[0] % quarters, r[0] // quarters)),
        ],
        (1, 4, depth, local),
        qkv,
        out,
    )
    feed_in = cut(
        feed_share_kernel,
        [
            pl.BlockSpec((depth, width), lambda j, r: (r[0], 0)),
            pl.BlockSpec((depth, width), lambda j, r: (r[0], 1)),
            pl.BlockSpec((rows, width), lambda j, r: (r[0], 0)),
        ],
        (2 * depth + rows, width),
        into,
        into,
        down,
    )
    direct = cut(
        direct_share_kernel,
        [pl.BlockSpec((last, width), lambda j, r: (4 + r[0] % 2, 0))],
        (1, 1, last, width),
        down,
    )
    return heads, feed_in, direct


SCHEDULE = ["ao", "ss", 8.0, 20.0, 20.0, "tH", 2.0, "H", "tF", "rr", "H", "H", "I", "sm", 2.0, 10.0, "pH", "D", 2.0, "at", "no", 2.0, "rn", "I", "I", 10.0, "tX", 10.0, "D", "fo", "pI", "D", 5.0, "ff", 20.0, "pD", "tu", "rb", "sd", "bf", "bo", "d", "si", "nb", "ba", "i", "ra", "d", 30.0, "so", 2.0, "bs", "sq", 20.0, "u", "d", "q", "i", 20.0, "d", 10.0, "q", "d", 2.0, "i", "q", 20.0, 20.0, 20.0, "br", "bg", "i", "g", "q", "i", 5.0, "dr"]
KINDS = ["zwxy/xyzw", "zwyx/yzwx", "xyzw/yzwx"]
CUTS = [[1, 1], [2, 2], [2, 1]]


def body(
    inputs,
    lengths,
    w_qkv,
    b_qv,
    w_out,
    b_out,
    ln_gains,
    ln_biases,
    w_in,
    b_in,
    w_down,
    b_down,
    cotangent,
):
    size = lax.axis_size("dp")
    me = lax.axis_index("dp")
    side = lax.axis_index("tensor")
    side_index = side.astype(jnp.int32).reshape(1)
    tokens, width = inputs.shape[1:]
    local = w_qkv.shape[2]
    units = w_in.shape[1]
    order = Order()

    rank, core = me & 7, me & 1
    core_index = core.astype(jnp.int32).reshape(1)
    me_index = me.astype(jnp.int32).reshape(1)
    qkv_own = jnp.transpose(w_qkv, (1, 0, 2))
    depth = width // 8
    heads_share, feed_share, direct_share = shares(rank.astype(jnp.int32).reshape(1), qkv_own, w_out, w_in, w_down)
    heads_share = swap_x(heads_share)
    feed_share = swap_x(feed_share)
    direct_share = swap_x(direct_share)

    dims = [1 << k for k in range(1, size.bit_length() - 1)]
    letters = {"x": [None], "y": dims[:1], "z": dims[1:2], "w": dims[2:]}

    def kind(k):
        return [[dim for letter in word for dim in letters[letter]] for word in KINDS[k].split("/")]

    chains = {}
    v = types.SimpleNamespace()

    def step(name):
        return lambda: chains[name].step()

    def attend_own():
        v.own = attend(order, side_index, lengths, inputs, qkv_own, b_qv, b_out.reshape(1, -1), w_out)

    def send_small():
        hidden = b_in.reshape(1, -1)
        v.small_own = order.call(small_kernel, shaped((1, 2 * local + units), single), b_qv, hidden, cost=0.3)
        v.small_sent = swap_x(v.small_own)

    def take_small():
        v.small = order.pin(v.small_sent)

    def take_heads():
        chains["H"] = Chain(fetch_spread(order, order.pin(heads_share), size, 2.0))
        chains["H"].step()

    def take_feed():
        into_share, down_share = order.call(
            unpack_kernel,
            [shaped((1, 2, depth, width), single), shaped((1, 1, units // 12, width), single)],
            feed_share,
            cost=10.0,
        )
        chains["I"] = Chain(fetch_spread(order, into_share, size, 8.0))
        chains["D"] = Chain(fetch_spread(order, down_share, size, 8.0))
        chains["I"].step()
        chains["D"].step()

    def take_direct():
        chains["X"] = Chain(fetch_direct(order, direct_share, size, units // 3 * 2))
        chains["X"].step()

    def place_heads():
        v.w_heads = place(order, me_index, [chains["H"].value], (4, width, local))

    def place_in():
        v.w_in = place(order, me_index, [chains["I"].value], w_in.shape)

    def place_down():
        v.w_down = place(order, me_index, [chains["D"].value, chains["X"].value], w_down.shape)

    def relative_rows():
        v.rows_rel = relative(order, side_index, me_index, size, inputs)

    def attend_other():
        v.other = attend(order, side_index, lengths, inputs, v.w_heads, v.small, v.own[3])

    def norm():
        v.normed, v.two_start = order.call(
            norm_kernel,
            [shaped((tokens, width), bfloat), shaped((tokens, width), single)],
            v.other[3],
            ln_gains,
            ln_biases,
            b_down.reshape(1, -1),
        )

    def feed_own():
        v.act_own, v.slope_own, v.two_own = feed(
            order, v.normed, w_in, b_in.reshape(1, -1), w_down, v.two_start
        )

    def feed_other():
        v.act, v.slope = feed_up(order, v.normed, v.w_in, v.small)

    def relative_normed():
        v.normed_rel = relative(order, side_index, me_index, size, v.normed)

    def turn():
        v.grad_two, v.sums_two, v.unit, v.branch = order.call(
            turn_kernel,
            [
                shaped((tokens, width), single),
                shaped((3, width), single),
                shaped((tokens, width), single),
                shaped((tokens, width), bfloat),
            ],
            v.act,
            v.w_down,
            v.two_own,
            ln_gains,
            cotangent,
            scalars=(side_index,),
            cost=2.6,
        )
        v.unit_other = swap_x(v.unit)

    def start(name, k, terms, finish, *more):
        chains[name] = Chain(scatter(order, core_index, terms, CUTS[k], kind(k), size, finish, *more))
        chains[name].step()

    share = width // size

    def finish(low, arrived, extra):
        return add_arrived(order, low, arrived, extra, True)[0]

    def finish_project(low, arrived, extra):
        shapes = [(3, share, local), (share, local), (2, width), (2, width)]
        shapes += [(width,), (units,), (width,), (2, local)]
        return order.call(
            last_kernel,
            [shaped(shape, single) for shape in shapes],
            low,
            arrived,
            extra,
            scalars=(side_index,),
            cost=1.0,
        )

    def relative_branch():
        v.branch_rel = relative(order, side_index, me_index, size, v.branch)

    def start_down():
        rights = (v.act_own, v.act)
        start("d", 0, lambda sides: [(v.branch_rel, [rights[k] for k in sides], 0, units)], finish)

    def feed_back_other():
        v.pre, v.units_sum, v.grad_other = feed_back(
            order, v.branch, v.w_down, v.slope, v.w_in, v.grad_two
        )

    def feed_back_own():
        v.pre_own, v.units_sum_own, v.grad = feed_back(
            order, v.branch, w_down, v.slope_own, w_in, v.grad_other
        )

    def start_into():
        rights = (v.pre_own, v.pre)
        start("i", 1, lambda sides: [(v.normed_rel, [rights[k] for k in sides], 0, units)], finish)

    def norm_two():
        v.grad_one, v.sums_one, v.attended = order.call(
            norm_back_kernel,
            [shaped((tokens, width), single), shaped((3, width), single), shaped((tokens, width), bfloat)],
            v.other[3],
            ln_gains,
            v.grad,
            cost=1.5,
        )

    def relative_attended():
        v.attended_rel = relative(order, side_index, me_index, size, v.attended)

    def attend_back_other():
        v.proj, v.proj_sum, v.rows_other = attend_back(
            order, v.attended, v.other[0], v.other[1], v.w_heads, v.grad_one
        )

    def attend_back_own():
        v.proj_own, v.proj_sum_own, v.grad_rows = attend_back(
            order, v.attended, v.own[0], v.own[1], qkv_own, v.rows_other, w_out
        )
        v.grad_other_rows = swap_x(v.grad_rows)

    def vectors():
        return order.call(
            vectors_kernel,
            shaped((8, 2 * width), single),
            v.sums_one,
            v.sums_two,
            v.units_sum_own,
            v.units_sum,
            v.proj_sum_own,
            v.proj_sum,
            scalars=(side_index,),
            cost=0.5,
        )

    def start_project():
        def terms(sides):
            contexts = [(v.own, v.other)[k][2] for k in sides]
            projs = [v.proj if k else v.proj_own for k in sides]
            return [(v.attended_rel, contexts, 0, local), (v.rows_rel, projs, 0, 3 * local)]

        start("q", 2, terms, finish_project, vectors, True)

    def take_unit():
        v.unit_other = order.pin(v.unit_other)

    def take_grad():
        v.grad_other_rows = order.pin(v.grad_other_rows)

    def both_results():
        v.results = order.call(
            both_result_kernel,
            shaped((2, tokens, width), bfloat),
            v.unit,
            v.unit_other,
            ln_gains,
            ln_biases,
            scalars=(side_index,),
            cost=1.5,
        )

    def both_grads():
        v.grads = order.call(
            both_kernel,
            shaped((2, tokens, width), single),
            v.grad_rows,
            v.grad_other_rows,
            scalars=(side_index,),
            cost=2.0,
        )

    def drain():
        last = [chains[name] for name in "diq"]
        while any(chain.value is None for chain in last):
            for chain in last:
                if chain.value is None:
                    chain.step()

    steps = {
        "ao": attend_own,
        "ss": send_small,
        "sm": take_small,
        "tH": take_heads,
        "tF": take_feed,
        "tX": take_direct,
        "H": step("H"),
        "I": step("I"),
        "D": step("D"),
        "pH": place_heads,
        "pI": place_in,
        "pD": place_down,
        "rr": relative_rows,
        "at": attend_other,
        "no": norm,
        "fo": feed_own,
        "ff": feed_other,
        "rn": relative_normed,
        "tu": turn,
        "rb": relative_branch,
        "sd": start_down,
        "bf": feed_back_other,
        "bo": feed_back_own,
        "si": start_into,
        "nb": norm_two,
        "ra": relative_attended,
        "ba": attend_back_other,
        "bs": attend_back_own,
        "so": start_project,
        "sq": step("q"),
        **{name: step(name) for name in "diq"},
        "u": take_unit,
        "g": take_grad,
        "br": both_results,
        "bg": both_grads,
        "dr": drain,
    }
    for name in SCHEDULE:
        if isinstance(name, str):
            steps[name]()
        else:
            order.pad(float(name))
    results, grads = v.results, v.grads
    g_qkv, g_out, gains, shifts, g_b_out, g_b_in, g_b_down, g_b_qv = chains["q"].value
    return (
        results,
        grads,
        jnp.transpose(g_qkv, (1, 0, 2)),
        g_b_qv,
        g_out.T,
        g_b_out,
        gains,
        shifts,
        chains["i"].value,
        g_b_in,
        chains["d"].value.T,
        g_b_down,
    )


def solution(mesh):
    placed = (
        P("dp", None, None),
        P("dp"),
        P(None, None, "tensor"),
        P(None, "tensor"),
        P("tensor", None),
        P(),
        P(),
        P(),
        P(None, "tensor"),
        P("tensor"),
        P("tensor", None),
        P(),
        P("dp", None, None),
    )
    return jax.shard_map(
        body,
        mesh=mesh,
        in_specs=placed,
        out_specs=(
            P("dp", None, None),
            P("dp", None, None),
            P("dp", None, "tensor"),
            P(None, "tensor"),
            P("tensor", "dp"),
            P(),
            P(),
            P(),
            P("dp", "tensor"),
            P("tensor"),
            P("tensor", "dp"),
            P(),
        ),
        check_vma=False,
    )
```

```python
import functools
import types

import jax
import jax.numpy as jnp
from jax import lax
from jax.experimental import pallas as pl
from jax.experimental.pallas import tpu as pltpu
from jax.sharding import PartitionSpec as P

HEAD_DIM = 64
PAIR = 2 * HEAD_DIM
norm_eps = 1e-12
bfloat = jnp.bfloat16
single = jnp.float32
MIB = 1 << 20
COST_UNIT = 1.0e9


def dot(left, right):
    return jnp.dot(left, right, preferred_element_type=single)


def dot_cols(left, right):
    return lax.dot_general(
        left, right, (((1,), (1,)), ((), ())), preferred_element_type=single
    )


def shaped(shape, dtype):
    return jax.ShapeDtypeStruct(shape, dtype)


def nothing_kernel(out_ref):
    out_ref[...] = jnp.zeros_like(out_ref)


class Order:
    def __init__(self):
        self.last = None

    def call(self, kernel, outs, *args, scalars=(), scratch=(), grid=(), in_specs=None, out_specs=None, limit=16, aliases=None, cost=1.0, name=None):
        many = isinstance(outs, (tuple, list))
        if in_specs is None:
            in_specs = [pl.BlockSpec(memory_space=pltpu.VMEM)] * len(args)
        if out_specs is None:
            out_specs = [pl.BlockSpec(memory_space=pltpu.VMEM)] * len(outs) if many else pl.BlockSpec(memory_space=pltpu.VMEM)
        in_specs = [pl.BlockSpec(memory_space=pltpu.SMEM)] * len(scalars) + list(in_specs)
        operands = list(scalars) + list(args)
        run = kernel
        if self.last is not None:
            before = len(operands)
            operands.append(self.last)
            in_specs.append(pl.BlockSpec(memory_space=pl.ANY))

            def run(*refs):
                kernel(*refs[:before], *refs[before + 1 :])

        made = pl.pallas_call(
            run,
            out_shape=outs,
            grid=grid,
            in_specs=in_specs,
            out_specs=out_specs,
            scratch_shapes=list(scratch),
            name=name or kernel.__name__,
            input_output_aliases=aliases or {},
            compiler_params=pltpu.CompilerParams(vmem_limit_bytes=limit * MIB),
            cost_estimate=pl.CostEstimate(flops=int(cost * COST_UNIT), bytes_accessed=1000, transcendentals=0),
        )(*operands)
        self.last = made[-1] if many else made
        return made

    def pad(self, cost):
        self.call(nothing_kernel, shaped((8, 128), single), cost=cost)

    def pin(self, value):
        return self.call(
            lambda *refs: None,
            shaped(value.shape, value.dtype),
            value,
            in_specs=[pl.BlockSpec(memory_space=pl.ANY)],
            out_specs=pl.BlockSpec(memory_space=pl.ANY),
            aliases={0: 0},
            cost=0.0,
            name="pin_kernel",
        )


class Chain:
    def __init__(self, steps):
        self.steps = steps
        self.value = None

    def step(self):
        self.value = next(self.steps, self.value)
        return self.value

    def run(self, count):
        for _ in range(count):
            self.step()


def swap_dp(value, mask, size):
    return lax.ppermute(value, "dp", [(i, i ^ mask) for i in range(size)])


def swap_x(value):
    return lax.ppermute(value, "tensor", [(0, 1), (1, 0)])


def reverse_bits(position, bits):
    out = 0
    for k in range(bits):
        out |= ((position >> k) & 1) << (bits - 1 - k)
    return out


def place_kernel(starts, me_ref, *refs):
    out_ref = refs[-1]
    me = me_ref[0]
    at = 0
    for piece in refs[:-1]:
        height = piece.shape[2]
        for b in range(piece.shape[0]):
            start = pl.multiple_of(starts[at](me), 16)
            for c in range(piece.shape[1]):
                if out_ref.ndim == 3:
                    out_ref[c, pl.ds(start, height), :] = piece[b, c].astype(out_ref.dtype)
                else:
                    lanes = slice(c * piece.shape[3], (c + 1) * piece.shape[3])
                    out_ref[pl.ds(start, height), lanes] = piece[b, c].astype(out_ref.dtype)
            at += 1


def place(order, me, parts, shape):
    pieces, starts = [], []
    for held, begin in parts:
        pieces += held
        starts += begin
    kernel = functools.partial(place_kernel, tuple(starts))
    return order.call(kernel, shaped(shape, bfloat), *pieces, scalars=(me,), cost=2.4, name="place_kernel")


def pack_kernel(first_ref, second_ref, out_ref):
    out_ref[0] = first_ref[0]
    out_ref[1] = second_ref[0]


def swap_mixed(value, first, second, size):
    pairs = []
    for d in range(size):
        mask = second if d & 1 else first
        for t in range(2):
            to = (d, 1 - t) if mask is None else (d ^ mask, t)
            pairs.append((2 * d + t, 2 * to[0] + to[1]))
    return lax.ppermute(value, ("dp", "tensor"), pairs)


def fetch_spread(order, held, size, pack_cost):
    arrived = swap_mixed(held, 4, 2, size)
    yield
    both = order.call(pack_kernel, shaped((2,) + held.shape[1:], single), held, arrived, cost=pack_cost)
    arrived = swap_mixed(both, 2, 4, size)
    both_core = swap_dp(both, 1, size)
    yield
    both_core = order.pin(both_core)
    yield
    arrived = order.pin(arrived)
    arrived_core = swap_dp(arrived, 1, size)
    rows = held.shape[-2]

    def start(even, odd, flip):
        return lambda index: ((index & 7) ^ flip ^ jnp.where(index & 1 == flip, even, odd)) * rows

    offsets = list(zip((0, 4, 2, 6), (0, 2, 4, 6)))
    yield [both, arrived, both_core, arrived_core], [
        start(even, odd, flip) for flip in range(2) for even, odd in offsets
    ]


def fetch_direct(order, held, size, base):
    held = order.pin(held)
    rows = held.shape[-2]
    yield [held, swap_dp(held, 1, size)], [
        lambda index: base + (index & 1) * rows,
        lambda index: base + (1 - (index & 1)) * rows,
    ]


def unpack_kernel(all_ref, into_ref, down_ref):
    rows = into_ref.shape[2]
    for c in range(2):
        into_ref[0, c] = all_ref[c * rows : (c + 1) * rows, :]
    down_ref[0, 0] = all_ref[2 * rows :, :]


def product_kernel(groups, sides, cuts, places, extras, core_ref, *refs):
    lefts, rights = refs[: len(groups)], refs[len(groups) : (1 + sides) * len(groups)]
    rest = refs[(1 + sides) * len(groups) :]
    tile = pl.program_id(0)
    first = core_ref[0] == 0

    def spread(side, total, low_ref, high_ref, table, height):
        half = len(table[0])
        for block in range(half):
            at = table[side][block]
            out_ref, at = (low_ref, at) if at < half else (high_ref, at - half)
            out_ref[at * height : (at + 1) * height, :] = total[block * height : (block + 1) * height]

    def run(k, j):
        for side in range(sides):
            total = dot(lefts[k][...], rights[sides * k + side][...])
            rows = total.shape[0]
            cut = sum(cuts[:side]) + j * cuts[side] // sum(groups)
            if places is None:
                rest[extras + cut][:rows, :] = total
                if extras:
                    rest[extras + cut][rows:, :] = rest[0][...]
                continue
            total = total + rest[cut][:rows, :]
            low_ref, high_ref = rest[sum(cuts) + extras :][:2]
            even, odd, height = places
            pl.when(first)(lambda: spread(side, total, low_ref, high_ref, even, height))
            pl.when(jnp.logical_not(first))(lambda: spread(side, total, low_ref, high_ref, odd, height))
            if extras and side == 0:
                extra = rest[sum(cuts)][...] + rest[cut][rows:, :]
                rest[-1][...] = extra
                high_ref[low_ref.shape[0] :, :] = extra

    j = 0
    for k, tiles in enumerate(groups):
        for _ in range(tiles):
            pl.when(tile == j)(functools.partial(run, k, j))
            j += 1


def product(order, core, half, terms, cuts, added=(), places=None, extras=()):
    rows = terms[0][0].shape[0] // 2
    tokens = terms[0][0].shape[1]
    sides = len(terms[0][1])
    tile = 768 if all(term[2] % 768 == 0 and term[3] % 768 == 0 for term in terms) else 384
    groups = tuple(term[3] // tile for term in terms)
    begins = [sum(groups[:k]) for k in range(len(groups))]
    tiles = sum(groups)

    def right_spec(k):
        first = terms[k][2] // tile
        return pl.BlockSpec((tokens, tile), lambda j: (0, first + jnp.clip(j - begins[k], 0, groups[k] - 1)))

    def tall(height):
        return shaped((height, tiles * tile), single), pl.BlockSpec((height, tile), lambda j: (0, j))

    beyond = sum(part.shape[0] for part in extras)
    cut_list = [(side, k, tiles // count) for side, count in enumerate(cuts) for k in range(count)]
    heights = [rows + (beyond if side == 0 else 0) for side, _, _ in cut_list]
    pieces = [
        pl.BlockSpec((height, tile), lambda j, k=k, each=each: (0, jnp.clip(j - k * each, 0, each - 1)))
        for height, (_, k, each) in zip(heights, cut_list)
    ]
    if places is None:
        outs = [shaped((height, cut[2] * tile), single) for height, cut in zip(heights, cut_list)]
        out_specs = pieces
    else:
        height = len(places[0][0]) * places[2]
        heights = [height, height + beyond] + ([beyond] if extras else [])
        outs, out_specs = zip(*[tall(height) for height in heights])
    return order.call(
        functools.partial(product_kernel, groups, sides, cuts, places, len(extras)),
        list(outs),
        *[term[0] for term in terms],
        *[right for term in terms for right in term[1]],
        *added,
        *extras,
        scalars=(core,),
        grid=(tiles,),
        in_specs=[
            *[pl.BlockSpec((rows, tokens), lambda j: (half, 0)) for _ in terms],
            *[right_spec(k) for k in range(len(terms)) for _ in range(sides)],
            *(pieces if added else []),
            *[tall(part.shape[0])[1] for part in extras],
        ],
        out_specs=list(out_specs),
        cost=sides * tiles * tile / 384 * (0.4 if places is None else 0.6),
        name="send_kernel" if places is None else "keep_kernel",
    )


def sum_kernel(whole, low_ref, arrived_ref, *refs):
    rows = low_ref.shape[0]
    extra = refs[0][...] + arrived_ref[rows:, :] if arrived_ref.shape[0] > rows else None
    outs = refs if extra is None else refs[1:]
    if whole:
        outs[0][...] = low_ref[...] + arrived_ref[:rows, :]
    else:
        half = rows // 2
        outs[0][...] = low_ref[:half, :] + arrived_ref[:half, :]
        outs[1][:half, :] = low_ref[half:, :] + arrived_ref[half:rows, :]
    if extra is not None:
        outs[-1][...] = extra
        if not whole:
            outs[1][rows // 2 :, :] = extra


def add_arrived(order, low, arrived, extra, whole=False):
    rows, width = low.shape
    beyond = arrived.shape[0] - rows
    heights = [rows] if whole else [rows // 2, rows // 2 + beyond]
    heights += [beyond] if beyond else []
    outs = order.call(
        functools.partial(sum_kernel, whole),
        [shaped((height, width), single) for height in heights],
        low,
        arrived,
        *([extra] if beyond else []),
        cost=0.7,
        name="add_kernel",
    )
    return outs if beyond else [*outs, None]


def scatter(order, core, terms, cuts, orders, size, finish, extra=None, apart=False):
    masks = [1 << k for k in range(1, size.bit_length() - 1)]
    count = len(masks)

    def place_of(side, block, dims):
        at = 0
        for dim in dims:
            bit = side if dim is None else (block >> (count - 1 - masks.index(dim))) & 1
            at = 2 * at + bit
        return at

    tables = [
        [[place_of(side, block, dims) for block in range(1 << count)] for side in range(2)]
        for dims in orders
    ]
    def send(sides, extras):
        sent = product(order, core, 1, terms(sides), [cuts[side] for side in sides], extras=extras)
        return [swap_dp(part, 1, size) for part in sent]

    if apart:
        arrived = send((1,), ())
        yield
        extras = () if extra is None else (extra(),)
        arrived = send((0,), extras) + arrived
    else:
        extras = ()
        arrived = send((0, 1), extras)
    terms = terms((0, 1))
    yield
    height = terms[0][0].shape[0] // size
    low, high, *extra = product(order, core, 0, terms, cuts, arrived, (*tables, height), extras)
    extra = extra[0] if extras else None
    for k in range(count + 1):
        arrived = swap_mixed(high, orders[0][k], orders[1][k], size)
        yield
        if k < count:
            low, high, extra = add_arrived(order, low, arrived, extra)
    yield finish(low, arrived, extra)


def last_kernel(side_ref, low_ref, arrived_ref, extra_ref, qkv_ref, out_ref, gains_ref, shifts_ref, *vectors):
    b_out_ref, b_in_ref, b_down_ref, b_qv_ref = vectors
    rows = low_ref.shape[0]
    local = qkv_ref.shape[2]
    width = gains_ref.shape[1]
    total = low_ref[...] + arrived_ref[:rows, :]
    out_ref[...] = total[:, :local]
    for k in range(3):
        qkv_ref[k] = total[:, (k + 1) * local : (k + 2) * local]
    sums = extra_ref[...] + arrived_ref[rows:, :]
    for k in range(2):
        half = slice(k * width, (k + 1) * width)
        gains_ref[k : k + 1, :] = sums[0:1, half]
        shifts_ref[k : k + 1, :] = sums[1:2, half]
    b_out_ref[...] = sums[2, :width]
    b_down_ref[...] = sums[2, width:]
    first = side_ref[0] == 0
    b_in_ref[...] = jnp.where(first, sums[3, :], sums[5, :])
    parts = jnp.where(first, sums[4:5, :], sums[6:7, :])
    b_qv_ref[0:1, :] = parts[:, :local]
    b_qv_ref[1:2, :] = parts[:, local : 2 * local]


def relative_kernel(size, side_ref, me_ref, value_ref, out_ref, turned_ref):
    value = value_ref[side_ref[0]] if len(value_ref.shape) == 3 else value_ref[...]
    depth = value.shape[1]
    share = depth // size
    bits = size.bit_length() - 1
    me = me_ref[0]
    if share % 16 == 0:
        turned_ref[...] = value.T
        for p in range(size):
            block = pl.multiple_of((reverse_bits(p, bits) ^ me) * share, 16)
            out_ref[p * share : (p + 1) * share, :] = turned_ref[pl.ds(block, share), :]
        return
    tile = 96
    lanes = lax.broadcasted_iota(jnp.int32, (tile, depth), 1)
    local = lax.broadcasted_iota(jnp.int32, (tile, depth), 0)
    for j in range(0, depth, tile):
        source = jnp.zeros_like(local)
        for p in range(j // share, (j + tile) // share):
            here = (local >= p * share - j) & (local < (p + 1) * share - j)
            source = jnp.where(here, (reverse_bits(p, bits) ^ me) * share + local + (j - p * share), source)
        picks = jnp.where(lanes == source, 1.0, 0.0).astype(bfloat)
        out_ref[j : j + tile, :] = dot_cols(picks, value).astype(bfloat)


def relative(order, side, me, size, value):
    shape = value.shape[-2:][::-1]
    return order.call(
        functools.partial(relative_kernel, size),
        shaped(shape, bfloat),
        value,
        scalars=(side, me),
        scratch=[pltpu.VMEM(shape, bfloat)],
        cost=0.8,
        name="relative_kernel",
    )


def attend_kernel(side_ref, lengths_ref, inputs_ref, qkv_ref, bias_ref, start_ref, *refs):
    *out_w, parts_ref, chance_ref, context_ref, hidden_ref, turned_ref = refs
    tokens = inputs_ref.shape[1]
    local = qkv_ref.shape[2]
    side = side_ref[0]
    rows = inputs_ref[side]
    flat = bias_ref.shape[0] == 1
    for part in range(3):
        projected = dot(rows, qkv_ref[part])
        if part != 1:
            k = part // 2
            projected = projected + (bias_ref[:, k * local : (k + 1) * local] if flat else bias_ref[k : k + 1, :])
        parts_ref[part] = projected.astype(bfloat)
    tile = tokens
    visible = lax.broadcasted_iota(jnp.int32, (tokens, tile), 0) < lengths_ref[side]

    def pair_step(pair):
        at = pair * PAIR
        keys = parts_ref[1, :, pl.ds(at, PAIR)]
        queries = parts_ref[0, :, pl.ds(at, PAIR)].T
        values = parts_ref[2, :, pl.ds(at, PAIR)].T
        owner = lax.broadcasted_iota(jnp.int32, (PAIR, tile), 0) // HEAD_DIM
        for h in range(2):
            value_rows = values[h * HEAD_DIM : (h + 1) * HEAD_DIM]
            for q in range(tokens // tile):
                picked = queries[:, q * tile : (q + 1) * tile] * HEAD_DIM**-0.5
                picked = jnp.where(owner == h, picked, jnp.zeros_like(picked))
                scores = jnp.where(visible, dot(keys, picked), -1e9)
                raised = jnp.exp(scores - jnp.max(scores, axis=0, keepdims=True))
                chances = raised * (1.0 / jnp.sum(raised, axis=0, keepdims=True))
                chances = chances.astype(bfloat)
                chance_ref[pair * 2 + h, :, q * tile : (q + 1) * tile] = chances
                turned_ref[pl.ds(at + h * HEAD_DIM, HEAD_DIM), q * tile : (q + 1) * tile] = dot(value_rows, chances).astype(bfloat)

    for pair in range(local // PAIR):
        pair_step(pair)
    context = turned_ref[...].T
    context_ref[...] = context
    if out_w:
        hidden_ref[...] = rows.astype(single) + start_ref[...] + dot(context, out_w[0][...])
    else:
        middle = hidden_ref.shape[1] // 2
        hidden_ref[:, :middle] = start_ref[:, :middle] + dot(context, qkv_ref[3, :local, :])
        hidden_ref[:, middle:] = start_ref[:, middle:] + dot(context, qkv_ref[3, local:, :])


def attend(order, side, lengths, inputs, qkv, bias, start, out=None):
    tokens, width = inputs.shape[1:]
    local = qkv.shape[2]
    return order.call(
        attend_kernel,
        [
            shaped((3, tokens, local), bfloat),
            shaped((local // HEAD_DIM, tokens, tokens), bfloat),
            shaped((tokens, local), bfloat),
            shaped((tokens, width), single),
        ],
        inputs,
        qkv,
        bias,
        start,
        *([] if out is None else [out]),
        scalars=(side, lengths),
        scratch=[pltpu.VMEM((local, tokens), bfloat)],
        cost=6.6,
    )


def unit_of(hidden):
    centred = hidden - jnp.mean(hidden, axis=-1, keepdims=True)
    scale = lax.rsqrt(jnp.mean(centred * centred, axis=-1, keepdims=True) + norm_eps)
    return centred * scale, scale


def norm_back(upstream, unit, scale, gain):
    scaled = upstream * gain
    return scale * (
        scaled
        - jnp.mean(scaled, axis=-1, keepdims=True)
        - unit * jnp.mean(scaled * unit, axis=-1, keepdims=True)
    )


STRIP = 512


def strips(tokens, body):
    def step(j, carry):
        body(pl.ds(pl.multiple_of(j * STRIP, STRIP), STRIP))
        return carry

    lax.fori_loop(0, tokens // STRIP, step, 0)


def norm_kernel(hidden_ref, gain_ref, shift_ref, down_ref, low_ref, next_ref):
    def body(at):
        unit, _ = unit_of(hidden_ref[at, :])
        normed = unit * gain_ref[0:1, :] + shift_ref[0:1, :]
        low_ref[at, :] = normed.astype(bfloat)
        next_ref[at, :] = normed + down_ref[...]

    strips(hidden_ref.shape[0], body)


def gelu_tiles(normed_ref, into_ref, bias_ref, act_ref, slope_ref):
    tokens, hidden_units = normed_ref.shape[0], into_ref.shape[1]
    tile, height = 512, 128
    before = bias_ref.shape[1] - hidden_units
    for j in range(0, hidden_units, tile):
        at = pl.ds(j, tile)
        for k in range(0, tokens, height):
            strip = pl.ds(k, height)
            pre = dot(normed_ref[strip, :], into_ref[:, at]) + bias_ref[:, pl.ds(before + j, tile)]
            bell = jnp.exp(-0.5 * pre * pre)
            reach = 1.0 / (1.0 + 0.23164189 * jnp.abs(pre))
            tail = reach * (
                0.127414796
                + reach * (-0.142248368 + reach * (0.7107068705 + reach * (-0.7265760135 + reach * 0.5307027145)))
            )
            tail = tail * bell
            chance = jnp.where(pre >= 0, 1.0 - tail, tail)
            act_ref[strip, at] = (pre * chance).astype(bfloat)
            slope_ref[strip, at] = (chance + pre * bell * 0.3989422804014327).astype(bfloat)


def feed_kernel(normed_ref, into_ref, bias_ref, down_ref, start_ref, act_ref, slope_ref, hidden_ref):
    gelu_tiles(normed_ref, into_ref, bias_ref, act_ref, slope_ref)
    hidden_ref[...] = start_ref[...] + dot(act_ref[...], down_ref[...])


def feed(order, normed, into, bias, down, start):
    tokens, width = normed.shape
    units = into.shape[1]
    return order.call(
        feed_kernel,
        [shaped((tokens, units), bfloat), shaped((tokens, units), bfloat), shaped((tokens, width), single)],
        normed,
        into,
        bias,
        down,
        start,
        cost=4.4,
    )


def feed_up(order, normed, into, bias):
    units = into.shape[1]
    return order.call(
        gelu_tiles,
        [shaped((normed.shape[0], units), bfloat)] * 2,
        normed,
        into,
        bias,
        cost=4.0,
        name="feed_up_kernel",
    )


def add_columns(ref, row, value):
    ref[row : row + 1, :] += jnp.sum(value, axis=0, keepdims=True)


def turn_kernel(side_ref, act_ref, down_ref, start_ref, gain_ref, upstream_ref, grad_ref, sums_ref, unit_ref, branch_ref):
    sums_ref[...] = jnp.zeros_like(sums_ref)

    def body(at):
        unit, scale = unit_of(start_ref[at, :] + dot(act_ref[at, :], down_ref[...]))
        gain = gain_ref[1:2, :]
        upstream = upstream_ref[side_ref[0], at, :].astype(single)
        unit_ref[at, :] = unit
        grad = norm_back(upstream, unit, scale, gain)
        grad_ref[at, :] = grad
        branch_ref[at, :] = grad.astype(bfloat)
        add_columns(sums_ref, 0, upstream * unit)
        add_columns(sums_ref, 1, upstream)
        add_columns(sums_ref, 2, grad)

    strips(start_ref.shape[0], body)


def feed_back_kernel(branch_ref, down_ref, slope_ref, into_ref, start_ref, grad_ref, sums_ref, normed_ref):
    tile = 512
    for j in range(0, into_ref.shape[1], tile):
        at = pl.ds(j, tile)
        pre = dot_cols(branch_ref[...], down_ref[at, :]) * slope_ref[:, at].astype(single)
        low = pre.astype(bfloat)
        grad_ref[:, at] = low
        sums_ref[:, at] = jnp.sum(low.astype(single), axis=0, keepdims=True)
    normed_ref[...] = start_ref[...] + dot_cols(grad_ref[...], into_ref[...])


def feed_back(order, branch, down, slope, into, start):
    tokens, width = branch.shape
    units = into.shape[1]
    return order.call(
        feed_back_kernel,
        [shaped((tokens, units), bfloat), shaped((1, units), single), shaped((tokens, width), single)],
        branch,
        down,
        slope,
        into,
        start,
        cost=3.0,
    )


def norm_back_kernel(hidden_ref, gain_ref, upstream_ref, grad_ref, sums_ref, low_ref):
    sums_ref[...] = jnp.zeros_like(sums_ref)

    def body(at):
        unit, scale = unit_of(hidden_ref[at, :])
        upstream = upstream_ref[at, :]
        grad = norm_back(upstream, unit, scale, gain_ref[0:1, :])
        grad_ref[at, :] = grad
        low_ref[at, :] = grad.astype(bfloat)
        add_columns(sums_ref, 0, upstream * unit)
        add_columns(sums_ref, 1, upstream)
        add_columns(sums_ref, 2, grad)

    strips(hidden_ref.shape[0], body)


def attend_back_kernel(upstream_ref, parts_ref, chance_ref, qkv_ref, start_ref, *refs):
    *out_w, grad_ref, sums_ref, rows_ref, turned_ref = refs
    tokens = upstream_ref.shape[0]
    local = qkv_ref.shape[2]
    middle = upstream_ref.shape[1] // 2
    factor = HEAD_DIM**-0.5

    def pair_step(pair):
        at = pair * PAIR
        lanes = pl.ds(at, PAIR)
        queries = parts_ref[0, :, lanes]
        keys_turned = parts_ref[1, :, lanes].T
        values = parts_ref[2, :, lanes]
        if out_w:
            grad_context = dot_cols(upstream_ref[...], out_w[0][lanes, :])
        else:
            grad_context = dot_cols(upstream_ref[:, :middle], qkv_ref[3, lanes, :])
            grad_context = grad_context + dot_cols(
                upstream_ref[:, middle:], qkv_ref[3, pl.ds(local + at, PAIR), :]
            )
        grad_context = grad_context.astype(bfloat)
        context_turned = grad_context.T
        owner = lax.broadcasted_iota(jnp.int32, (PAIR, tokens), 0) // HEAD_DIM
        first_lane = lax.broadcasted_iota(jnp.int32, (tokens, PAIR), 1) < HEAD_DIM
        grads_k, grads_v = [], []
        for h in range(2):
            key_rows = keys_turned[h * HEAD_DIM : (h + 1) * HEAD_DIM]
            picked = jnp.where(owner == h, context_turned, jnp.zeros_like(context_turned))
            chances_low = chance_ref[pair * 2 + h]
            chances = chances_low.astype(single)
            grads_v.append(dot(chances_low, grad_context))
            grad_chances = dot(values, picked)
            inner = jnp.sum(chances * grad_chances, axis=0, keepdims=True)
            grad_scores = (chances * (grad_chances - inner)).astype(bfloat)
            grads_k.append(dot(grad_scores, queries))
            turned_ref[pl.ds(at + h * HEAD_DIM, HEAD_DIM), :] = (dot(key_rows, grad_scores) * factor).astype(bfloat)
        grad_k = (jnp.where(first_lane, grads_k[0], grads_k[1]) * factor).astype(bfloat)
        grad_v = jnp.where(first_lane, grads_v[0], grads_v[1]).astype(bfloat)
        grad_ref[:, pl.ds(local + at, PAIR)] = grad_k
        grad_ref[:, pl.ds(2 * local + at, PAIR)] = grad_v

    for pair in range(local // PAIR):
        pair_step(pair)
    grad_ref[:, 0:local] = turned_ref[...].T
    sums_ref[...] = jnp.sum(grad_ref[...].astype(single), axis=0, keepdims=True)
    total = start_ref[...]
    for part in range(3):
        total = total + dot_cols(grad_ref[:, part * local : (part + 1) * local], qkv_ref[part])
    rows_ref[...] = total


def attend_back(order, upstream, parts, chances, qkv, start, out=None):
    tokens, width = upstream.shape
    local = qkv.shape[2]
    return order.call(
        attend_back_kernel,
        [shaped((tokens, 3 * local), bfloat), shaped((1, 3 * local), single), shaped((tokens, width), single)],
        upstream,
        parts,
        chances,
        qkv,
        start,
        *([] if out is None else [out]),
        scratch=[pltpu.VMEM((local, tokens), bfloat)],
        cost=7.4,
    )


def vectors_kernel(side_ref, first_ref, second_ref, units_own, units_other, proj_own, proj_other, out_ref):
    width = first_ref.shape[1]
    local = proj_own.shape[1] // 3
    out_ref[...] = jnp.zeros_like(out_ref)
    out_ref[0:3, :width] = first_ref[...]
    out_ref[0:3, width:] = second_ref[...]
    swapped = side_ref[0] == 1
    for row, units, proj in (
        (3, (units_own, units_other), (proj_own, proj_other)),
        (5, (units_other, units_own), (proj_other, proj_own)),
    ):
        out_ref[row : row + 1, :] = jnp.where(swapped, units[1][...], units[0][...])
        parts = jnp.where(swapped, proj[1][...], proj[0][...])
        out_ref[row + 1 : row + 2, :local] = parts[:, :local]
        out_ref[row + 1 : row + 2, local : 2 * local] = parts[:, 2 * local :]


def both_result_kernel(side_ref, mine_ref, other_ref, gain_ref, shift_ref, out_ref):
    side = side_ref[0]

    def body(at):
        for place, ref in ((side, mine_ref), (1 - side, other_ref)):
            out_ref[place, at, :] = (ref[at, :] * gain_ref[1:2, :] + shift_ref[1:2, :]).astype(bfloat)

    strips(mine_ref.shape[0], body)


def both_kernel(side_ref, mine_ref, other_ref, out_ref):
    side = side_ref[0]
    out_ref[side] = mine_ref[...]
    out_ref[1 - side] = other_ref[...]


def heads_share_kernel(rank_ref, qkv_ref, out_ref, heads_ref):
    heads_ref[0, 0:3] = qkv_ref[...].astype(single)
    heads_ref[0, 3] = out_ref[...].astype(single)


def feed_share_kernel(rank_ref, left_ref, right_ref, down_ref, feed_ref):
    depth = left_ref.shape[0]
    feed_ref[0:depth, :] = left_ref[...].astype(single)
    feed_ref[depth : 2 * depth, :] = right_ref[...].astype(single)
    feed_ref[2 * depth :, :] = down_ref[...].astype(single)


def direct_share_kernel(rank_ref, last_ref, direct_ref):
    direct_ref[0, 0] = last_ref[...].astype(single)


def small_kernel(bias_ref, units_ref, small_ref):
    local = bias_ref.shape[1]
    small_ref[:, 0:local] = bias_ref[0:1, :]
    small_ref[:, local : 2 * local] = bias_ref[1:2, :]
    small_ref[:, 2 * local :] = units_ref[...]


def shares(rank, qkv, out, into, down):
    width, local, hidden = qkv.shape[1], qkv.shape[2], into.shape[1]
    depth = width // 8
    quarters = local // depth
    rows, last = hidden // 12, hidden // 6

    def cut(kernel, specs, shape, *args):
        return pl.pallas_call(
            kernel,
            grid_spec=pltpu.PrefetchScalarGridSpec(
                num_scalar_prefetch=1,
                grid=(1,),
                in_specs=specs,
                out_specs=pl.BlockSpec(shape, lambda j, r: (0,) * len(shape)),
            ),
            out_shape=shaped(shape, single),
            cost_estimate=pl.CostEstimate(flops=1000, bytes_accessed=1000, transcendentals=0),
            name=kernel.__name__,
        )(rank, *args)

    heads = cut(
        heads_share_kernel,
        [
            pl.BlockSpec((3, depth, local), lambda j, r: (0, r[0], 0)),
            pl.BlockSpec((depth, local), lambda j, r: (r[0] % quarters, r[0] // quarters)),
        ],
        (1, 4, depth, local),
        qkv,
        out,
    )
    feed_in = cut(
        feed_share_kernel,
        [
            pl.BlockSpec((depth, width), lambda j, r: (r[0], 0)),
            pl.BlockSpec((depth, width), lambda j, r: (r[0], 1)),
            pl.BlockSpec((rows, width), lambda j, r: (r[0], 0)),
        ],
        (2 * depth + rows, width),
        into,
        into,
        down,
    )
    direct = cut(
        direct_share_kernel,
        [pl.BlockSpec((last, width), lambda j, r: (4 + r[0] % 2, 0))],
        (1, 1, last, width),
        down,
    )
    return heads, feed_in, direct


SCHEDULE = ["ao", "ss", 8.0, 20.0, 20.0, "tH", 2.0, "H", "tF", "rr", "H", "H", "I", "sm", 2.0, 10.0, "pH", "D", 2.0, "at", "no", 2.0, "rn", "I", "I", 10.0, "tX", 10.0, "D", "fo", "pI", "D", 5.0, "ff", 20.0, "pD", "tu", "rb", "sd", "bf", "bo", "d", "si", "nb", "ba", "i", "ra", "d", 30.0, "so", 2.0, "bs", "sq", 20.0, "u", "d", "q", "i", 20.0, "d", 10.0, "q", "d", 2.0, "i", "q", 20.0, 20.0, 20.0, "br", "bg", "i", "g", "q", "i", 5.0, "dr"]
KINDS = ["xyzw/zwxy", "zwyx/yzwx", "xyzw/yzwx"]
CUTS = [[1, 1], [2, 2], [2, 1]]


def body(
    inputs,
    lengths,
    w_qkv,
    b_qv,
    w_out,
    b_out,
    ln_gains,
    ln_biases,
    w_in,
    b_in,
    w_down,
    b_down,
    cotangent,
):
    size = lax.axis_size("dp")
    me = lax.axis_index("dp")
    side = lax.axis_index("tensor")
    side_index = side.astype(jnp.int32).reshape(1)
    tokens, width = inputs.shape[1:]
    local = w_qkv.shape[2]
    units = w_in.shape[1]
    order = Order()

    rank, core = me & 7, me & 1
    core_index = core.astype(jnp.int32).reshape(1)
    me_index = me.astype(jnp.int32).reshape(1)
    qkv_own = jnp.transpose(w_qkv, (1, 0, 2))
    depth = width // 8
    heads_share, feed_share, direct_share = shares(rank.astype(jnp.int32).reshape(1), qkv_own, w_out, w_in, w_down)
    heads_share = swap_x(heads_share)
    feed_share = swap_x(feed_share)
    direct_share = swap_x(direct_share)

    dims = [1 << k for k in range(1, size.bit_length() - 1)]
    letters = {"x": [None], "y": dims[:1], "z": dims[1:2], "w": dims[2:]}

    def kind(k):
        return [[dim for letter in word for dim in letters[letter]] for word in KINDS[k].split("/")]

    chains = {}
    v = types.SimpleNamespace()

    def step(name):
        return lambda: chains[name].step()

    def attend_own():
        v.own = attend(order, side_index, lengths, inputs, qkv_own, b_qv, b_out.reshape(1, -1), w_out)

    def send_small():
        hidden = b_in.reshape(1, -1)
        v.small_own = order.call(small_kernel, shaped((1, 2 * local + units), single), b_qv, hidden, cost=0.3)
        v.small_sent = swap_x(v.small_own)

    def take_small():
        v.small = order.pin(v.small_sent)

    def take_heads():
        chains["H"] = Chain(fetch_spread(order, order.pin(heads_share), size, 2.0))
        chains["H"].step()

    def take_feed():
        into_share, down_share = order.call(
            unpack_kernel,
            [shaped((1, 2, depth, width), single), shaped((1, 1, units // 12, width), single)],
            feed_share,
            cost=10.0,
        )
        chains["I"] = Chain(fetch_spread(order, into_share, size, 8.0))
        chains["D"] = Chain(fetch_spread(order, down_share, size, 8.0))
        chains["I"].step()
        chains["D"].step()

    def take_direct():
        chains["X"] = Chain(fetch_direct(order, direct_share, size, units // 3 * 2))
        chains["X"].step()

    def place_heads():
        v.w_heads = place(order, me_index, [chains["H"].value], (4, width, local))

    def place_in():
        v.w_in = place(order, me_index, [chains["I"].value], w_in.shape)

    def place_down():
        v.w_down = place(order, me_index, [chains["D"].value, chains["X"].value], w_down.shape)

    def relative_rows():
        v.rows_rel = relative(order, side_index, me_index, size, inputs)

    def attend_other():
        v.other = attend(order, side_index, lengths, inputs, v.w_heads, v.small, v.own[3])

    def norm():
        v.normed, v.two_start = order.call(
            norm_kernel,
            [shaped((tokens, width), bfloat), shaped((tokens, width), single)],
            v.other[3],
            ln_gains,
            ln_biases,
            b_down.reshape(1, -1),
        )

    def feed_own():
        v.act_own, v.slope_own, v.two_own = feed(
            order, v.normed, w_in, b_in.reshape(1, -1), w_down, v.two_start
        )

    def feed_other():
        v.act, v.slope = feed_up(order, v.normed, v.w_in, v.small)

    def relative_normed():
        v.normed_rel = relative(order, side_index, me_index, size, v.normed)

    def turn():
        v.grad_two, v.sums_two, v.unit, v.branch = order.call(
            turn_kernel,
            [
                shaped((tokens, width), single),
                shaped((3, width), single),
                shaped((tokens, width), single),
                shaped((tokens, width), bfloat),
            ],
            v.act,
            v.w_down,
            v.two_own,
            ln_gains,
            cotangent,
            scalars=(side_index,),
            cost=2.6,
        )
        v.unit_other = swap_x(v.unit)

    def start(name, k, terms, finish, *more):
        chains[name] = Chain(scatter(order, core_index, terms, CUTS[k], kind(k), size, finish, *more))
        chains[name].step()

    share = width // size

    def finish(low, arrived, extra):
        return add_arrived(order, low, arrived, extra, True)[0]

    def finish_project(low, arrived, extra):
        shapes = [(3, share, local), (share, local), (2, width), (2, width)]
        shapes += [(width,), (units,), (width,), (2, local)]
        return order.call(
            last_kernel,
            [shaped(shape, single) for shape in shapes],
            low,
            arrived,
            extra,
            scalars=(side_index,),
            cost=1.0,
        )

    def relative_branch():
        v.branch_rel = relative(order, side_index, me_index, size, v.branch)

    def start_down():
        rights = (v.act_own, v.act)
        start("d", 0, lambda sides: [(v.branch_rel, [rights[k] for k in sides], 0, units)], finish)

    def feed_back_other():
        v.pre, v.units_sum, v.grad_other = feed_back(
            order, v.branch, v.w_down, v.slope, v.w_in, v.grad_two
        )

    def feed_back_own():
        v.pre_own, v.units_sum_own, v.grad = feed_back(
            order, v.branch, w_down, v.slope_own, w_in, v.grad_other
        )

    def start_into():
        rights = (v.pre_own, v.pre)
        start("i", 1, lambda sides: [(v.normed_rel, [rights[k] for k in sides], 0, units)], finish)

    def norm_two():
        v.grad_one, v.sums_one, v.attended = order.call(
            norm_back_kernel,
            [shaped((tokens, width), single), shaped((3, width), single), shaped((tokens, width), bfloat)],
            v.other[3],
            ln_gains,
            v.grad,
            cost=1.5,
        )

    def relative_attended():
        v.attended_rel = relative(order, side_index, me_index, size, v.attended)

    def attend_back_other():
        v.proj, v.proj_sum, v.rows_other = attend_back(
            order, v.attended, v.other[0], v.other[1], v.w_heads, v.grad_one
        )

    def attend_back_own():
        v.proj_own, v.proj_sum_own, v.grad_rows = attend_back(
            order, v.attended, v.own[0], v.own[1], qkv_own, v.rows_other, w_out
        )
        v.grad_other_rows = swap_x(v.grad_rows)

    def vectors():
        return order.call(
            vectors_kernel,
            shaped((8, 2 * width), single),
            v.sums_one,
            v.sums_two,
            v.units_sum_own,
            v.units_sum,
            v.proj_sum_own,
            v.proj_sum,
            scalars=(side_index,),
            cost=0.5,
        )

    def start_project():
        def terms(sides):
            contexts = [(v.own, v.other)[k][2] for k in sides]
            projs = [v.proj if k else v.proj_own for k in sides]
            return [(v.attended_rel, contexts, 0, local), (v.rows_rel, projs, 0, 3 * local)]

        start("q", 2, terms, finish_project, vectors, True)

    def take_unit():
        v.unit_other = order.pin(v.unit_other)

    def take_grad():
        v.grad_other_rows = order.pin(v.grad_other_rows)

    def both_results():
        v.results = order.call(
            both_result_kernel,
            shaped((2, tokens, width), bfloat),
            v.unit,
            v.unit_other,
            ln_gains,
            ln_biases,
            scalars=(side_index,),
            cost=1.5,
        )

    def both_grads():
        v.grads = order.call(
            both_kernel,
            shaped((2, tokens, width), single),
            v.grad_rows,
            v.grad_other_rows,
            scalars=(side_index,),
            cost=2.0,
        )

    def drain():
        last = [chains[name] for name in "diq"]
        while any(chain.value is None for chain in last):
            for chain in last:
                if chain.value is None:
                    chain.step()

    steps = {
        "ao": attend_own,
        "ss": send_small,
        "sm": take_small,
        "tH": take_heads,
        "tF": take_feed,
        "tX": take_direct,
        "H": step("H"),
        "I": step("I"),
        "D": step("D"),
        "pH": place_heads,
        "pI": place_in,
        "pD": place_down,
        "rr": relative_rows,
        "at": attend_other,
        "no": norm,
        "fo": feed_own,
        "ff": feed_other,
        "rn": relative_normed,
        "tu": turn,
        "rb": relative_branch,
        "sd": start_down,
        "bf": feed_back_other,
        "bo": feed_back_own,
        "si": start_into,
        "nb": norm_two,
        "ra": relative_attended,
        "ba": attend_back_other,
        "bs": attend_back_own,
        "so": start_project,
        "sq": step("q"),
        **{name: step(name) for name in "diq"},
        "u": take_unit,
        "g": take_grad,
        "br": both_results,
        "bg": both_grads,
        "dr": drain,
    }
    for name in SCHEDULE:
        if isinstance(name, str):
            steps[name]()
        else:
            order.pad(float(name))
    results, grads = v.results, v.grads
    g_qkv, g_out, gains, shifts, g_b_out, g_b_in, g_b_down, g_b_qv = chains["q"].value
    return (
        results,
        grads,
        jnp.transpose(g_qkv, (1, 0, 2)),
        g_b_qv,
        g_out.T,
        g_b_out,
        gains,
        shifts,
        chains["i"].value,
        g_b_in,
        chains["d"].value.T,
        g_b_down,
    )


def solution(mesh):
    placed = (
        P("dp", None, None),
        P("dp"),
        P(None, None, "tensor"),
        P(None, "tensor"),
        P("tensor", None),
        P(),
        P(),
        P(),
        P(None, "tensor"),
        P("tensor"),
        P("tensor", None),
        P(),
        P("dp", None, None),
    )
    return jax.shard_map(
        body,
        mesh=mesh,
        in_specs=placed,
        out_specs=(
            P("dp", None, None),
            P("dp", None, None),
            P("dp", None, "tensor"),
            P(None, "tensor"),
            P("tensor", "dp"),
            P(),
            P(),
            P(),
            P("dp", "tensor"),
            P("tensor"),
            P("tensor", "dp"),
            P(),
        ),
        check_vma=False,
    )
```
